32 devices in a mesh: parts: 2 (over y), src: 4 (over z), tile: 2 (over x), row: 2 (over core).
Axes of the slice: x: 2, y: 2, z: 4, core: 2. Of those that a mesh axis runs over, the one named last changes fastest.
Arguments:
- mask_windows: float32 [4, 256, 256], P(('parts', 'tile'), ('src', 'row')), parts along dimension 0, may hold values from -4 to 4
- target_windows: float32 [4, 256, 256], P(('parts', 'tile'), ('src', 'row')), parts along dimension 0, may hold values from 0 to 1
- pupil_bands: int32 [24, 128, 2], P(('parts', 'src')), parts along dimension 0, may hold values from 0 to 128, as said below
- pupil_phase: float32 [24, 128, 128], P(('parts', 'src')), parts along dimension 0, may hold values from -3.140625 to 3.140625
- source_weight: float32 [24], P(('parts', 'src')), parts along dimension 0, may hold values from 0.2 to 1
Outputs:
- mask_grad: float32 [4, 256, 256], P(('parts', 'tile'), ('src', 'row')), parts along dimension 0
- source_grad: float32 [24], P(('parts', 'src')), parts along dimension 0
The draws below stay inside these ranges and needn't reach their ends.
There are 2 independent parts, one for each index of `parts`. The reference program is written for one: setup_inputs(seed, part) draws one part's arguments, and reference() takes and returns one part's arrays. A program takes and returns all parts, laid end to end along the dimension named above; each array names one. Nothing has to cross between parts.
Inputs may be any that keep to these rules, and one draw needn't show every extreme that they name: For every source point and frequency row, pupil_bands[s, kx, 0] <= pupil_bands[s, kx, 1]; a row that passes nothing holds (0, 0).
All inputs are finite; a program needn't handle non-finite values.
Results may differ from the reference program's by a relative error of at most 0.00019.
Values sent between devices are 32-bit elements; how exact they have to be, the bound alone decides.
No kernel may reach another device: no remote copies, remote signals or barrier semaphores. Data moves between devices by JAX's collectives and lax.ppermute only.
A program may use at most 64 MiB of HBM per device.

```python
import math
import jax
import jax.numpy as jnp
from jax import lax

M = 256
K = 128
OV = 32
S = 12
W = 2


def draw_pupil_bands(key, part):
    reach_max = 3 * K // 16
    radius = 5 * K // 16
    centre = K // 2
    key_rows, key_cols = jax.random.split(jax.random.fold_in(key, 11))
    shift_rows = jax.random.randint(key_rows, (S,), -reach_max, reach_max + 1)
    shift_cols = jax.random.randint(key_cols, (S,), -reach_max, reach_max + 1)
    shift_cols = shift_cols.at[0].set(reach_max)
    freq_index = jnp.arange(K, dtype=jnp.int32)
    dist_rows = freq_index[None, :] - centre - shift_rows[:, None]
    dist_cols = freq_index[None, :] - centre - shift_cols[:, None]
    inside = dist_rows[:, :, None] * dist_rows[:, :, None] + dist_cols[:, None, :] * dist_cols[:, None, :] <= radius * radius
    inside = inside.astype(jnp.int32)
    band_hi = jnp.max(inside * (freq_index[None, None, :] + 1), axis=2)
    band_lo = jnp.where(band_hi > 0, K - jnp.max(inside * (K - freq_index[None, None, :]), axis=2), 0)
    return jnp.stack([band_lo, band_hi], axis=2).astype(jnp.int32)


def levels(rng, shape, shards, low, high):
    def one(dim, shards_of):
        heights = jax.random.uniform(jax.random.fold_in(jax.random.fold_in(rng, 6), dim), (shards_of,), jnp.float32, low / len(shards), high / len(shards))
        return jnp.repeat(jnp.exp(heights), shape[dim] // shards_of).reshape((-1,) + (1,) * (len(shape) - dim - 1))

    factor_of = one(*shards[0])
    for cut in shards[1:]:
        factor_of = factor_of * one(*cut)
    return factor_of


def scatter_about(own_key, extent, deviation, most, cuts=(), kind=jnp.bfloat16):
    drawn = jax.random.normal(own_key, extent, jnp.float32) * deviation
    if len(cuts) > 0:
        drawn = levels(own_key, extent, cuts, -0.22, 0.18) * drawn
    return jnp.clip(drawn, min=-most, max=most).astype(kind)


def setup_inputs(seed: int = 0, part: int = 0) -> dict:
    keys = jax.random.split(jax.random.key(seed), 6)
    part_keys = jax.random.split(jax.random.fold_in(keys[5], part), 6)
    return {
        "mask_windows": scatter_about(part_keys[0], (W, M, M), 1.0, 4.0, ((0, 2), (1, 8)), jnp.float32),
        "target_windows": jnp.clip(1.0 * jax.random.uniform(part_keys[1], (W, M, M), jnp.float32) ** levels(part_keys[1], (W, M, M), ((0, 2), (1, 8)), -0.2, 0.2), 0.0, 1.0),
        "pupil_bands": draw_pupil_bands(jax.random.fold_in(jax.random.fold_in(keys[5], part), 71), part),
        "pupil_phase": jnp.clip(jax.random.uniform(part_keys[3], (S, K, K), jnp.float32, -3.140625, 3.140625), -3.140625, 3.140625),
        "source_weight": jnp.clip(jnp.exp(math.log(1.0) - 1.609438 * jax.random.uniform(part_keys[4], (S,), jnp.float32) ** levels(part_keys[4], (S,), ((0, 4),), -0.2, 0.2)), 0.2, 1.0),
    }


STEEPNESS = 20.0
THRESHOLD = 0.15
LOSS_SCALE = 32.0


def matmul(left_op, right_op):
    return jnp.dot(left_op, right_op, precision=lax.Precision.HIGHEST, preferred_element_type=jnp.float32)


def wave_tables(positions):
    freq_index = jnp.arange(K, dtype=jnp.int32) - K // 2
    phase_index = (freq_index[:, None] * positions[None, :]) % M
    angles = (2.0 * math.pi / M) * phase_index.astype(jnp.float32)
    return jnp.cos(angles), jnp.sin(angles)


def pupil_gate(pupil_bands, pupil_phase):
    freq_cols = jnp.arange(K, dtype=jnp.int32)
    inside = (freq_cols[None, None, :] >= pupil_bands[:, :, 0:1]) & (freq_cols[None, None, :] < pupil_bands[:, :, 1:2])
    passing = inside.astype(jnp.float32)
    return passing * jnp.cos(pupil_phase), passing * jnp.sin(pupil_phase)


def reference(mask_windows, target_windows, pupil_bands, pupil_phase, source_weight):
    cos_tab, sin_tab = wave_tables(jnp.arange(M, dtype=jnp.int32))
    field_scale = 1.0 / (M * K)
    pupil_real, pupil_imag = pupil_gate(pupil_bands, pupil_phase)
    weights = source_weight / S

    def fields(spec_real, spec_imag, pass_real, pass_imag):
        amp_real = pass_real * spec_real - pass_imag * spec_imag
        amp_imag = pass_imag * spec_real + pass_real * spec_imag
        half_real = matmul(amp_real, cos_tab) - matmul(amp_imag, sin_tab)
        half_imag = matmul(amp_real, sin_tab) + matmul(amp_imag, cos_tab)
        field_real = field_scale * (matmul(cos_tab.T, half_real) - matmul(sin_tab.T, half_imag))
        field_imag = field_scale * (matmul(cos_tab.T, half_imag) + matmul(sin_tab.T, half_real))
        return field_real, field_imag

    def one_window(inputs):
        window, goal_window = inputs
        part_real = matmul(window, cos_tab.T)
        part_imag = -matmul(window, sin_tab.T)
        spec_real = matmul(cos_tab, part_real) + matmul(sin_tab, part_imag)
        spec_imag = matmul(cos_tab, part_imag) - matmul(sin_tab, part_real)

        def add_light(totals, source_in):
            pass_real, pass_imag, weight = source_in
            field_real, field_imag = fields(spec_real, spec_imag, pass_real, pass_imag)
            return totals + weight * (field_real * field_real + field_imag * field_imag), None

        intensity = lax.scan(add_light, jnp.zeros((M, M), jnp.float32), (pupil_real, pupil_imag, weights))[0]
        resist = jax.nn.sigmoid(STEEPNESS * (intensity - THRESHOLD))
        cotangent = LOSS_SCALE * (resist - goal_window) * STEEPNESS * resist * (1.0 - resist)

        def add_back(totals, source_in):
            grad_real, grad_imag = totals
            pass_real, pass_imag, weight = source_in
            field_real, field_imag = fields(spec_real, spec_imag, pass_real, pass_imag)
            back_scale = (2.0 * weight) * cotangent
            back_real = back_scale * field_real
            back_imag = back_scale * field_imag
            adj_real = matmul(cos_tab, back_real) + matmul(sin_tab, back_imag)
            adj_imag = matmul(cos_tab, back_imag) - matmul(sin_tab, back_real)
            amp_grad_real = field_scale * (matmul(adj_real, cos_tab.T) + matmul(adj_imag, sin_tab.T))
            amp_grad_imag = field_scale * (matmul(adj_imag, cos_tab.T) - matmul(adj_real, sin_tab.T))
            grad_real = grad_real + pass_real * amp_grad_real + pass_imag * amp_grad_imag
            grad_imag = grad_imag + pass_real * amp_grad_imag - pass_imag * amp_grad_real
            term_value = jnp.sum(cotangent * (field_real * field_real + field_imag * field_imag))
            return (grad_real, grad_imag), term_value

        zero_spec = jnp.zeros((K, K), jnp.float32)
        grads_pair, source_terms = lax.scan(add_back, (zero_spec, zero_spec), (pupil_real, pupil_imag, weights))
        grad_real, grad_imag = grads_pair
        q_one = matmul(grad_real, cos_tab) - matmul(grad_imag, sin_tab)
        q_two = matmul(grad_real, sin_tab) + matmul(grad_imag, cos_tab)
        grad_window = matmul(cos_tab.T, q_one) - matmul(sin_tab.T, q_two)
        return grad_window, source_terms

    grads, source_terms = lax.map(one_window, (mask_windows, target_windows))
    zero_strip = jnp.zeros((1, M, OV), jnp.float32)
    from_below = jnp.concatenate([zero_strip, grads[:-1, :, M - OV:]], axis=0)
    from_above = jnp.concatenate([grads[1:, :, :OV], zero_strip], axis=0)
    middle = jnp.zeros((W, M, M - 2 * OV), jnp.float32)
    mask_grad = grads + jnp.concatenate([from_below, middle, from_above], axis=2)
    source_grad = jnp.sum(source_terms, axis=0) / (S * M * W)
    return mask_grad, source_grad
```

```python
import functools
import math

import jax
import jax.numpy as jnp
import ml_dtypes
import numpy as np
from jax import lax
from jax.experimental import pallas as pl
from jax.experimental.pallas import tpu as pltpu
from jax.sharding import PartitionSpec as P

OV = 32
STEEPNESS = 20.0
THRESHOLD = 0.15
LOSS_SCALE = 32.0
PAD = 8
F32 = jnp.float32
BF16 = jnp.bfloat16
VMEM_BUDGET = 24 * 1024 * 1024


def wave_blocks(pixels, freqs):
    freq = np.arange(freqs) - freqs // 2
    angle = 2.0 * np.pi / pixels * ((freq[:, None] * np.arange(pixels)[None, :]) % pixels)
    c, s = np.cos(angle), np.sin(angle)
    fwd = np.block([[c, s], [-s, c]]).astype(np.float32)

    def pair(a):
        high = a.astype(ml_dtypes.bfloat16)
        low = (a - high.astype(np.float32)).astype(ml_dtypes.bfloat16)
        return high, low

    return pair(fwd), pair(np.ascontiguousarray(fwd.T))


def split(a):
    high = a.astype(BF16)
    return high, (a - high.astype(F32)).astype(BF16)


def dot(a, b):
    return jnp.dot(a, b, preferred_element_type=F32)


def dot_nt(a, b):
    return lax.dot_general(a, b, (((1,), (1,)), ((), ())), preferred_element_type=F32)


def mm3(left, right, op=dot):
    (lh, ll), (rh, rl) = left, right
    return op(lh, rh) + (op(lh, rl) + op(ll, rh))


def sincos(phase):
    h = 0.5 * phase
    u = h * h
    s = 1.0 / 6227020800.0
    for coef in (-1.0 / 39916800.0, 1.0 / 362880.0, -1.0 / 5040.0, 1.0 / 120.0, -1.0 / 6.0, 1.0):
        s = s * u + coef
    s = s * h
    c = 1.0 / 479001600.0
    for coef in (-1.0 / 3628800.0, 1.0 / 40320.0, -1.0 / 720.0, 1.0 / 24.0, -0.5, 1.0):
        c = c * u + coef
    two_s = s + s
    return two_s * c, 1.0 - two_s * s


def offset_of(index, offset, count):
    return index ^ offset if count & (count - 1) == 0 else lax.rem(index + offset, count)


def pick(values):
    row = lax.axis_index("row")
    out = values[0]
    for r in range(1, len(values)):
        out = jnp.where(row == r, values[r], out)
    return out


def spectrum_kernel(src_count, row_count, *refs):
    blocks = refs[:src_count]
    fwd_h, fwd_l, adj_h, adj_l, spec, goal, meta, part = refs[src_count:]
    rows, pixels = goal.shape[1], goal.shape[2]
    freqs = spec.shape[1]
    src, row = lax.axis_index("src"), lax.axis_index("row")
    slots = meta.shape[0]
    own = jnp.concatenate([b[:rows] for b in blocks], axis=0)
    waves = mm3(split(own), (adj_h[:pixels], adj_l[:pixels]))
    part[...] = jnp.zeros_like(part)
    for d in range(src_count):
        block = offset_of(src, d, src_count)
        start = pl.multiple_of((block * row_count + row) * rows, rows)
        mine = waves[d * rows : (d + 1) * rows]
        part[pl.ds(start, rows), :] = mine[:, :freqs]
        part[pl.ds(pl.multiple_of(pixels + start, rows), rows), :] = mine[:, freqs:]
        goal[block] = blocks[d][rows : 2 * rows]
    for j in range(slots):
        meta[j] = pick([blocks[r * slots + j][2 * rows :] for r in range(row_count)])
    spec[...] = mm3((fwd_h[...], fwd_l[...]), split(part[...]))


def fields_kernel(per_device, sources, slots, *refs):
    phases = refs[:slots]
    spec_a, spec_b, meta, fwd_h, fwd_l, adj_h, adj_l = refs[slots : slots + 7]
    field, pupil, intensity, amp_h, amp_l = refs[slots + 7 :]
    pixels = intensity.shape[1]
    freqs = spec_a.shape[1]
    spec = (spec_a[...] + spec_b[...]) * (1.0 / (pixels * freqs))
    spec_r, spec_i = spec[:freqs], spec[freqs:]
    column = lax.broadcasted_iota(jnp.int32, (freqs, freqs), 1).astype(F32)
    weight = []
    for j in range(slots):
        info = meta[j]
        bounds = info.T
        for i in range(per_device):
            s = j * per_device + i
            weight.append(info[per_device : per_device + 1, i : i + 1] * (1.0 / sources))
            inside = (column >= bounds[:freqs, i : i + 1]) & (
                column < bounds[freqs : 2 * freqs, i : i + 1]
            )
            sin_p, cos_p = sincos(phases[j][i])
            pass_r = jnp.where(inside, cos_p, 0.0)
            pass_i = jnp.where(inside, sin_p, 0.0)
            pupil[s, :freqs] = pass_r
            pupil[s, freqs:] = pass_i
            lanes = slice(s * freqs, (s + 1) * freqs)
            for half, value in enumerate(
                (pass_r * spec_r - pass_i * spec_i, pass_i * spec_r + pass_r * spec_i)
            ):
                high, low = split(value)
                amp_h[half * freqs : (half + 1) * freqs, lanes] = high
                amp_l[half * freqs : (half + 1) * freqs, lanes] = low
    total = jnp.zeros_like(intensity)
    group = 2
    for first in range(0, slots * per_device, group):
        members = range(first, min(first + group, slots * per_device))
        lanes = slice(first * freqs, (members[-1] + 1) * freqs)
        half = mm3((adj_h[...], adj_l[...]), (amp_h[:, lanes], amp_l[:, lanes]))
        for n, s in enumerate(members):
            lanes = slice(n * freqs, (n + 1) * freqs)
            pair = jnp.concatenate([half[:pixels, lanes], half[pixels:, lanes]], axis=1)
            out = mm3(split(pair), (fwd_h[...], fwd_l[...]))
            field[s] = out
            out_r, out_i = out[:, :pixels], out[:, pixels:]
            total = total + weight[s] * (out_r * out_r + out_i * out_i)
    intensity[...] = total


def adjoint_kernel(per_device, sources, *refs):
    (field, pupil, inten_a, inten_b, goal_a, goal_b, meta, fwd_h, fwd_l, adj_h, adj_l) = refs[:11]
    grad, strip, cot_ref, back_h, back_l = refs[11:]
    src_count, rows = goal_a.shape[0], goal_a.shape[1]
    pixels = inten_a.shape[1]
    freqs = grad.shape[1]
    row = lax.axis_index("row")
    tile = lax.axis_index("tile")
    for z in range(src_count):
        for r in range(2):
            here = slice((2 * z + r) * rows, (2 * z + r + 1) * rows)
            goal = jnp.where(row == r, goal_a[z], goal_b[z])
            intensity = inten_a[here] + inten_b[here]
            resist = 1.0 / (1.0 + jnp.exp(-STEEPNESS * (intensity - THRESHOLD)))
            cot_ref[here] = (LOSS_SCALE * STEEPNESS) * (resist - goal) * resist * (1.0 - resist)
    cot = cot_ref[...]
    count = field.shape[0]
    lane = lax.broadcasted_iota(jnp.int32, (PAD, freqs), 1)
    terms = jnp.zeros((PAD, freqs), F32)
    for s in range(count):
        value = field[s]
        back_r, back_i = cot * value[:, :pixels], cot * value[:, pixels:]
        power = back_r * value[:, :pixels] + back_i * value[:, pixels:]
        power = jnp.sum(jnp.sum(power, axis=0, keepdims=True), axis=1, keepdims=True)
        terms = terms + jnp.where(lane == s, power, 0.0)
        back = jnp.concatenate([back_r, back_i], axis=1)
        half = mm3(split(back), (adj_h[...], adj_l[...]))
        lanes = slice(s * freqs, (s + 1) * freqs)
        for n in range(2):
            high, low = split(half[:, n * freqs : (n + 1) * freqs])
            back_h[n * pixels : (n + 1) * pixels, lanes] = high
            back_l[n * pixels : (n + 1) * pixels, lanes] = low
    grad_r = jnp.zeros((freqs, freqs), F32)
    grad_i = jnp.zeros((freqs, freqs), F32)
    group = 2
    for first in range(0, count, group):
        members = range(first, min(first + group, count))
        lanes = slice(first * freqs, (members[-1] + 1) * freqs)
        out = mm3((fwd_h[...], fwd_l[...]), (back_h[:, lanes], back_l[:, lanes]))
        for n, s in enumerate(members):
            lanes = slice(n * freqs, (n + 1) * freqs)
            j, i = divmod(s, per_device)
            weight = meta[j][per_device : per_device + 1, i : i + 1] * (
                2.0 / (sources * pixels * freqs)
            )
            pass_r, pass_i = weight * pupil[s, :freqs], weight * pupil[s, freqs:]
            out_r, out_i = out[:freqs, lanes], out[freqs:, lanes]
            grad_r = grad_r + (pass_r * out_r + pass_i * out_i)
            grad_i = grad_i + (pass_r * out_i - pass_i * out_r)
    grad[:freqs] = grad_r
    grad[freqs : 2 * freqs] = grad_i
    grad[2 * freqs :] = terms
    flat = split(jnp.concatenate([grad_r, grad_i], axis=1))

    def edge(start):
        def part(table):
            return jnp.concatenate(
                [table[start : start + OV], table[pixels + start : pixels + start + OV]], axis=0
            )

        return part(adj_h), part(adj_l)

    high_h, high_l = edge(pixels - OV)
    low_h, low_l = edge(0)
    table = (jnp.where(tile == 0, high_h, low_h), jnp.where(tile == 0, high_l, low_l))
    strip[: 2 * OV] = mm3(table, flat, dot_nt)
    strip[2 * OV :] = terms


def window_kernel(per_device, term_scale, *refs):
    grad_a, grad_b, strip_a, strip_b, fwd_h, fwd_l, adj_h, adj_l, out, source = refs
    rows, pixels = out.shape
    freqs = grad_a.shape[1]
    src, row, tile = lax.axis_index("src"), lax.axis_index("row"), lax.axis_index("tile")
    total = grad_a[: 2 * freqs] + grad_b[: 2 * freqs]
    flat = split(jnp.concatenate([total[:freqs], total[freqs:]], axis=1))
    waves = mm3(flat, (fwd_h[...], fwd_l[...]))
    waves = jnp.concatenate([waves[:, :pixels], waves[:, pixels:]], axis=0)
    start = pl.multiple_of((src * 2 + row) * rows, rows)
    table = (adj_h[pl.ds(start, rows), :], adj_l[pl.ds(start, rows), :])
    window = mm3(table, split(waves))
    edge = strip_a[: 2 * OV] + strip_b[: 2 * OV]
    edge = mm3(table, split(jnp.concatenate([edge[:OV], edge[OV:]], axis=1)), dot_nt)
    zero = jnp.zeros_like(edge)
    middle = jnp.zeros((rows, pixels - 2 * OV), F32)
    low, high = jnp.where(tile == 1, edge, zero), jnp.where(tile == 0, edge, zero)
    out[...] = window + jnp.concatenate([low, middle, high], axis=1)
    first = jnp.where(row == 0, grad_a[2 * freqs :], grad_b[2 * freqs :])
    second = jnp.where(row == 0, strip_a[2 * OV :], strip_b[2 * OV :])
    source[...] = (first + second) * term_scale


def call(kernel, outs, scratch=()):
    return pl.pallas_call(
        kernel,
        out_shape=[jax.ShapeDtypeStruct(shape, F32) for shape in outs],
        out_specs=[pl.BlockSpec(memory_space=pltpu.VMEM) for _ in outs],
        scratch_shapes=[pltpu.VMEM(shape, kind) for shape, kind in scratch],
        compiler_params=pltpu.CompilerParams(vmem_limit_bytes=VMEM_BUDGET),
    )


def swap(x, axis, count, offset):
    return lax.ppermute(x, axis, [(i, i ^ offset) for i in range(count)])


def shards_full(mask_windows, target_windows, pupil_bands, pupil_phase, source_weight):
    src_count, tile_count, row_count = (lax.axis_size(a) for a in ("src", "tile", "row"))
    rows, pixels = mask_windows.shape[1:]
    per_device, freqs = pupil_phase.shape[:2]
    sources = per_device * src_count
    slots = src_count // row_count
    count = slots * per_device
    (fwd_h, fwd_l), (adj_h, adj_l) = wave_blocks(pixels, freqs)
    tables = [jnp.asarray(t) for t in (fwd_h, fwd_l, adj_h, adj_l)]

    bands = pupil_bands.astype(F32).transpose(0, 2, 1).reshape(per_device, 2 * freqs)
    weights = jnp.pad(source_weight[None, :], ((0, 0), (0, pixels - per_device)))
    meta = jnp.concatenate([bands, weights, jnp.zeros((PAD - per_device - 1, pixels), F32)])
    message = jnp.concatenate([mask_windows[0], target_windows[0], meta], axis=0)

    blocks = [message] + [swap(message, "src", src_count, d) for d in range(1, src_count)]
    phases = []
    for j in range(slots):
        pairs = []
        for z in range(src_count):
            for r in range(row_count):
                pairs.append(((z ^ (r * slots + j)) * row_count + r, z * row_count + r))
        phases.append(lax.ppermute(pupil_phase, ("src", "row"), pairs))

    spec, goal, meta = call(
        functools.partial(spectrum_kernel, src_count, row_count),
        [(2 * freqs, freqs), (src_count, rows, pixels), (slots, PAD, pixels)],
        [((2 * pixels, freqs), F32)],
    )(*blocks, *tables)
    spec_other = swap(spec, "row", row_count, 1)
    goal_other = swap(goal, "row", row_count, 1)

    field, pupil, inten = call(
        functools.partial(fields_kernel, per_device, sources, slots),
        [(count, pixels, 2 * pixels), (count, 2 * freqs, freqs), (pixels, pixels)],
        [((2 * freqs, count * freqs), BF16)] * 2,
    )(*phases, spec, spec_other, meta, *tables)
    inten_other = swap(inten, "row", row_count, 1)

    grad, strip = call(
        functools.partial(adjoint_kernel, per_device, sources),
        [(2 * freqs + PAD, freqs), (2 * OV + PAD, freqs)],
        [((pixels, pixels), F32)] + [((2 * pixels, count * freqs), BF16)] * 2,
    )(field, pupil, inten, inten_other, goal, goal_other, meta, *tables)
    grad_other = swap(grad, "row", row_count, 1)
    strip_a = swap(strip, "tile", tile_count, 1)
    strip_b = swap(strip, ("tile", "row"), tile_count * row_count, 3)

    out, source = call(
        functools.partial(window_kernel, per_device, 1.0 / (sources * pixels * tile_count)),
        [(rows, pixels), (PAD, freqs)],
    )(grad, grad_other, strip_a, strip_b, *tables)
    return out[None], source[0, :per_device]


M = 256
K = 128


def with_halo(block, sides, width):
    for axis, dim in sides:
        count = lax.axis_size(axis)
        forward = [(i, i + 1) for i in range(count - 1)]
        backward = [(target, source) for source, target in forward]
        low = lax.ppermute(
            lax.slice_in_dim(block, block.shape[dim] - width, None, axis=dim), axis, forward
        )
        high = lax.ppermute(lax.slice_in_dim(block, 0, width, axis=dim), axis, backward)
        block = jnp.concatenate([low, block, high], axis=dim)
    return block


def matmul(left_op, right_op):
    return lax.dot_general(
        left_op,
        right_op,
        (((1,), (0,)), ((), ())),
        precision=lax.Precision.HIGHEST,
        preferred_element_type=jnp.float32,
    )


def matmul_tn(left_op, right_op):
    return lax.dot_general(
        left_op,
        right_op,
        (((0,), (0,)), ((), ())),
        precision=lax.Precision.HIGHEST,
        preferred_element_type=jnp.float32,
    )


def matmul_nt(left_op, right_op):
    return lax.dot_general(
        left_op,
        right_op,
        (((1,), (1,)), ((), ())),
        precision=lax.Precision.HIGHEST,
        preferred_element_type=jnp.float32,
    )


def wave_tables(positions):
    freq_index = jnp.arange(K, dtype=jnp.int32) - K // 2
    phase_index = freq_index[:, None] * positions[None, :] % M
    angles = 2.0 * math.pi / M * phase_index.astype(jnp.float32)
    return (jnp.cos(angles), jnp.sin(angles))


def shards(mask_windows, target_windows, pupil_bands, pupil_phase, source_weight):
    src_count = lax.axis_size("src")
    tile_count = lax.axis_size("tile")
    row_count = lax.axis_size("row")
    local_x = mask_windows.shape[1]
    per_device = pupil_phase.shape[0]
    sources = per_device * src_count
    field_scale = 1.0 / (M * K)
    src_id = lax.axis_index("src")
    row_id = lax.axis_index("row")
    x_start = (src_id * row_count + row_id) * local_x
    block_starts = (jnp.arange(src_count, dtype=jnp.int32) * row_count + row_id) * local_x
    row_set = (block_starts[:, None] + jnp.arange(local_x, dtype=jnp.int32)[None, :]).reshape(
        src_count * local_x
    )
    cos_all, sin_all = wave_tables(jnp.arange(M, dtype=jnp.int32))
    cos_set, sin_set = wave_tables(row_set)
    cos_own, sin_own = wave_tables(x_start + jnp.arange(local_x, dtype=jnp.int32))
    window = mask_windows[0]
    goal_block = target_windows[0]
    zero_spec = jnp.zeros((K, K), jnp.float32)
    shard_rows = lax.all_gather(window, ("src", "row"), axis=0, tiled=True)
    part_real = matmul_nt(shard_rows, cos_all)
    part_imag = -matmul_nt(shard_rows, sin_all)
    spec_real = matmul(cos_all, part_real) + matmul(sin_all, part_imag)
    spec_imag = matmul(cos_all, part_imag) - matmul(sin_all, part_real)
    freq_cols = jnp.arange(K, dtype=jnp.int32)
    inside = (freq_cols[None, None, :] >= pupil_bands[:, :, 0:1]) & (
        freq_cols[None, None, :] < pupil_bands[:, :, 1:2]
    )
    passing = inside.astype(jnp.float32)
    pupil_real = passing * jnp.cos(pupil_phase)
    pupil_imag = passing * jnp.sin(pupil_phase)
    amp_real = (pupil_real * spec_real - pupil_imag * spec_imag).reshape(per_device * K, K)
    amp_imag = (pupil_imag * spec_real + pupil_real * spec_imag).reshape(per_device * K, K)
    half_real = (matmul(amp_real, cos_all) - matmul(amp_imag, sin_all)).reshape(per_device, K, M)
    half_imag = (matmul(amp_real, sin_all) + matmul(amp_imag, cos_all)).reshape(per_device, K, M)
    weights = source_weight / sources

    def fields(pair_in):
        one_real, one_imag = pair_in
        field_real = field_scale * (matmul_tn(cos_set, one_real) - matmul_tn(sin_set, one_imag))
        field_imag = field_scale * (matmul_tn(cos_set, one_imag) + matmul_tn(sin_set, one_real))
        return (field_real, field_imag)

    stack_real, stack_imag = lax.map(fields, (half_real, half_imag))
    part_real = stack_real
    part_imag = stack_imag
    intensity = lax.psum_scatter(
        jnp.sum(weights[:, None, None] * (part_real * part_real + part_imag * part_imag), axis=0),
        "src",
        scatter_dimension=0,
        tiled=True,
    )
    resist = jax.nn.sigmoid(STEEPNESS * (intensity - THRESHOLD))
    cotangent = LOSS_SCALE * (resist - goal_block) * STEEPNESS * resist * (1.0 - resist)
    cotangent_all = lax.all_gather(cotangent, "src", axis=0, tiled=True)
    source_ids = jnp.arange(per_device, dtype=jnp.int32)

    def add_back(source_id, totals):
        grad_real, grad_imag, source_terms = totals
        field_real = stack_real[source_id]
        field_imag = stack_imag[source_id]
        back_scale = 2.0 * weights[source_id] * cotangent_all
        back_real = back_scale * field_real
        back_imag = back_scale * field_imag
        adj_real = matmul(cos_set, back_real) + matmul(sin_set, back_imag)
        adj_imag = matmul(cos_set, back_imag) - matmul(sin_set, back_real)
        amp_grad_real = field_scale * (matmul_nt(adj_real, cos_all) + matmul_nt(adj_imag, sin_all))
        amp_grad_imag = field_scale * (matmul_nt(adj_imag, cos_all) - matmul_nt(adj_real, sin_all))
        pass_real = pupil_real[source_id]
        pass_imag = pupil_imag[source_id]
        grad_real = grad_real + pass_real * amp_grad_real + pass_imag * amp_grad_imag
        grad_imag = grad_imag + pass_real * amp_grad_imag - pass_imag * amp_grad_real
        term_value = jnp.sum(cotangent_all * (field_real * field_real + field_imag * field_imag))
        source_terms = source_terms + jnp.where(source_ids == source_id, term_value, 0.0)
        return (grad_real, grad_imag, source_terms)

    grad_real, grad_imag, source_terms = lax.fori_loop(
        0, per_device, add_back, (zero_spec, zero_spec, jnp.zeros((per_device,), jnp.float32))
    )
    grad_real, grad_imag = lax.psum((grad_real, grad_imag), ("src", "row"))
    source_sum = lax.psum(source_terms, ("tile", "row"))
    source_grad = source_sum / (sources * M * tile_count)
    q_one = matmul(grad_real, cos_all) - matmul(grad_imag, sin_all)
    q_two = matmul(grad_real, sin_all) + matmul(grad_imag, cos_all)
    grad_block = matmul_tn(cos_own, q_one) - matmul_tn(sin_own, q_two)
    padded = with_halo(grad_block, (("tile", 1),), OV)
    from_below = padded[:, :OV]
    from_above = padded[:, M + OV :]
    middle = jnp.zeros((local_x, M - 2 * OV), jnp.float32)
    grad_block = grad_block + jnp.concatenate([from_below, middle, from_above], axis=1)
    return (grad_block[None], source_grad)


def solution(mesh):
    small = mesh.shape["src"] == 4 and mesh.shape["tile"] == 2 and mesh.shape["row"] == 2
    return jax.shard_map(
        shards_full if small else shards,
        mesh=mesh,
        in_specs=(
            P(("parts", "tile"), ("src", "row"), None),
            P(("parts", "tile"), ("src", "row"), None),
            P(("parts", "src"), None, None),
            P(("parts", "src"), None, None),
            P(("parts", "src")),
        ),
        out_specs=(P(("parts", "tile"), ("src", "row"), None), P(("parts", "src"))),
        check_vma=False,
    )
```

```python
import functools
import math

import jax
import jax.numpy as jnp
from jax import lax
from jax.experimental import pallas as pl
from jax.experimental.pallas import tpu as pltpu
from jax.sharding import PartitionSpec as P

OV = 32
STEEPNESS = 20.0
THRESHOLD = 0.15
LOSS_SCALE = 32.0
PAD = 8
F32 = jnp.float32
BF16 = jnp.bfloat16
VMEM_BUDGET = 24 * 1024 * 1024


def split(a):
    high = a.astype(BF16)
    return high, (a - high.astype(F32)).astype(BF16)


def dot(a, b):
    return jnp.dot(a, b, preferred_element_type=F32)


def dot_nt(a, b):
    return lax.dot_general(a, b, (((1,), (1,)), ((), ())), preferred_element_type=F32)


def mm3(left, right, op=dot):
    (lh, ll), (rh, rl) = left, right
    return op(lh, rh) + (op(lh, rl) + op(ll, rh))


def sincos(phase):
    h = 0.5 * phase
    u = h * h
    s = 1.0 / 6227020800.0
    for coef in (-1.0 / 39916800.0, 1.0 / 362880.0, -1.0 / 5040.0, 1.0 / 120.0, -1.0 / 6.0, 1.0):
        s = s * u + coef
    s = s * h
    c = 1.0 / 479001600.0
    for coef in (-1.0 / 3628800.0, 1.0 / 40320.0, -1.0 / 720.0, 1.0 / 24.0, -0.5, 1.0):
        c = c * u + coef
    two_s = s + s
    return two_s * c, 1.0 - two_s * s


def block_of(src, side, steps, half):
    same = half - 1 - steps
    other = half + steps
    low = src < half
    return jnp.where(low, same if side == 0 else other, other if side == 0 else same)


def message_kernel(mask, goal, bands, weight, message):
    rows = mask.shape[1]
    per_device, _, freqs = bands.shape
    message[:rows] = mask[0]
    message[rows : 2 * rows] = goal[0]
    message[2 * rows :] = jnp.zeros_like(message[2 * rows :])
    for i in range(per_device):
        for n in range(2):
            message[2 * rows + i : 2 * rows + i + 1, n * freqs : (n + 1) * freqs] = bands[
                i, n : n + 1, :
            ].astype(F32)
    message[2 * rows + per_device : 2 * rows + per_device + 1, :per_device] = weight[...]


def tables_kernel(fwd_h, fwd_l, adj_h, adj_l):
    freqs, pixels = fwd_h.shape[0] // 2, fwd_h.shape[1] // 2

    def waves(shape, freq_dim):
        freq = lax.broadcasted_iota(jnp.int32, shape, freq_dim) - freqs // 2
        turn = freq * lax.broadcasted_iota(jnp.int32, shape, 1 - freq_dim)
        turn = ((turn + pixels // 2) & (pixels - 1)) - pixels // 2
        sin, cos = sincos((2.0 * math.pi / pixels) * turn.astype(F32))
        return split(cos), split(sin)

    (cos_h, cos_l), (sin_h, sin_l) = waves((freqs, pixels), 0)
    for table, cos, sin in ((fwd_h, cos_h, sin_h), (fwd_l, cos_l, sin_l)):
        table[:freqs, :pixels] = cos
        table[:freqs, pixels:] = sin
        table[freqs:, :pixels] = -sin
        table[freqs:, pixels:] = cos
    (cos_h, cos_l), (sin_h, sin_l) = waves((pixels, freqs), 1)
    for table, cos, sin in ((adj_h, cos_h, sin_h), (adj_l, cos_l, sin_l)):
        table[:pixels, :freqs] = cos
        table[:pixels, freqs:] = -sin
        table[pixels:, :freqs] = sin
        table[pixels:, freqs:] = cos


def spectrum_kernel(half, *refs):
    blocks = refs[: 2 * half]
    fwd_h, fwd_l, adj_h, adj_l, spec, goal, meta, part = refs[2 * half :]
    rows, pixels = goal.shape[1], goal.shape[2]
    freqs = spec.shape[1]
    src, row = lax.axis_index("src"), lax.axis_index("row")
    own = jnp.concatenate([b[:rows] for b in blocks], axis=0)
    waves = mm3(split(own), (adj_h[:pixels], adj_l[:pixels]))
    part[...] = jnp.zeros_like(part)
    for d in range(2 * half):
        block = block_of(src, d // half, d % half, half)
        start = pl.multiple_of((block * 2 + row) * rows, rows)
        mine = waves[d * rows : (d + 1) * rows]
        part[pl.ds(start, rows), :] = mine[:, :freqs]
        part[pl.ds(pl.multiple_of(pixels + start, rows), rows), :] = mine[:, freqs:]
        goal[block] = blocks[d][rows : 2 * rows]
    for j in range(half):
        meta[j] = jnp.where(row == 0, blocks[j][2 * rows :], blocks[half + j][2 * rows :])
    spec[...] = mm3((fwd_h[...], fwd_l[...]), split(part[...]))


def fields_kernel(per_device, sources, slots, *refs):
    phase_own, *phases = refs[: slots + 1]
    spec_a, spec_b, meta, fwd_h, fwd_l, adj_h, adj_l = refs[slots + 1 : slots + 8]
    field, pupil, intensity, amp_h, amp_l = refs[slots + 8 :]
    row = lax.axis_index("row")
    pixels = intensity.shape[1]
    freqs = spec_a.shape[1]
    spec = (spec_a[...] + spec_b[...]) * (1.0 / (pixels * freqs))
    spec_r, spec_i = spec[:freqs], spec[freqs:]
    column = lax.broadcasted_iota(jnp.int32, (freqs, freqs), 1).astype(F32)
    weight = []
    for j in range(slots):
        info = meta[j]
        bounds = info.T
        for i in range(per_device):
            s = j * per_device + i
            weight.append(info[per_device : per_device + 1, i : i + 1] * (1.0 / sources))
            inside = (column >= bounds[:freqs, i : i + 1]) & (
                column < bounds[freqs : 2 * freqs, i : i + 1]
            )
            phase = phases[j][i]
            if j == 0:
                phase = jnp.where(row == 0, phase_own[i], phase)
            sin_p, cos_p = sincos(phase)
            pass_r = jnp.where(inside, cos_p, 0.0)
            pass_i = jnp.where(inside, sin_p, 0.0)
            pupil[s, :freqs] = pass_r
            pupil[s, freqs:] = pass_i
            lanes = slice(s * freqs, (s + 1) * freqs)
            for half, value in enumerate(
                (pass_r * spec_r - pass_i * spec_i, pass_i * spec_r + pass_r * spec_i)
            ):
                high, low = split(value)
                amp_h[half * freqs : (half + 1) * freqs, lanes] = high
                amp_l[half * freqs : (half + 1) * freqs, lanes] = low
    total = jnp.zeros_like(intensity)
    group = 2
    for first in range(0, slots * per_device, group):
        members = range(first, min(first + group, slots * per_device))
        lanes = slice(first * freqs, (members[-1] + 1) * freqs)
        half = mm3((adj_h[...], adj_l[...]), (amp_h[:, lanes], amp_l[:, lanes]))
        for n, s in enumerate(members):
            lanes = slice(n * freqs, (n + 1) * freqs)
            pair = jnp.concatenate([half[:pixels, lanes], half[pixels:, lanes]], axis=1)
            out = mm3(split(pair), (fwd_h[...], fwd_l[...]))
            field[s] = out
            out_r, out_i = out[:, :pixels], out[:, pixels:]
            total = total + weight[s] * (out_r * out_r + out_i * out_i)
    intensity[...] = total


def adjoint_kernel(per_device, sources, *refs):
    (field, pupil, inten_a, inten_b, goal_a, goal_b, meta, fwd_h, fwd_l, adj_h, adj_l) = refs[:11]
    grad, cot_ref, back_h, back_l = refs[11:]
    src_count, rows = goal_a.shape[0], goal_a.shape[1]
    pixels = inten_a.shape[1]
    freqs = grad.shape[1]
    row = lax.axis_index("row")
    for z in range(src_count):
        for r in range(2):
            here = slice((2 * z + r) * rows, (2 * z + r + 1) * rows)
            goal = jnp.where(row == r, goal_a[z], goal_b[z])
            intensity = inten_a[here] + inten_b[here]
            resist = 1.0 / (1.0 + jnp.exp(-STEEPNESS * (intensity - THRESHOLD)))
            cot_ref[here] = (LOSS_SCALE * STEEPNESS) * (resist - goal) * resist * (1.0 - resist)
    cot = cot_ref[...]
    count = field.shape[0]
    line = lax.broadcasted_iota(jnp.int32, (PAD, freqs), 0)
    lane = lax.broadcasted_iota(jnp.int32, (PAD, freqs), 1)
    terms = jnp.zeros((PAD, freqs), F32)
    for s in range(count):
        value = field[s]
        back_r, back_i = cot * value[:, :pixels], cot * value[:, pixels:]
        power = back_r * value[:, :pixels] + back_i * value[:, pixels:]
        power = jnp.sum(jnp.sum(power, axis=0, keepdims=True), axis=1, keepdims=True)
        j, i = divmod(s, per_device)
        terms = terms + jnp.where((lane == i) & (line == j), power, 0.0)
        back = jnp.concatenate([back_r, back_i], axis=1)
        half = mm3(split(back), (adj_h[...], adj_l[...]))
        lanes = slice(s * freqs, (s + 1) * freqs)
        for n in range(2):
            high, low = split(half[:, n * freqs : (n + 1) * freqs])
            back_h[n * pixels : (n + 1) * pixels, lanes] = high
            back_l[n * pixels : (n + 1) * pixels, lanes] = low
    grad_r = jnp.zeros((freqs, freqs), F32)
    grad_i = jnp.zeros((freqs, freqs), F32)
    group = 2
    for first in range(0, count, group):
        members = range(first, min(first + group, count))
        lanes = slice(first * freqs, (members[-1] + 1) * freqs)
        out = mm3((fwd_h[...], fwd_l[...]), (back_h[:, lanes], back_l[:, lanes]))
        for n, s in enumerate(members):
            lanes = slice(n * freqs, (n + 1) * freqs)
            j, i = divmod(s, per_device)
            weight = meta[j][per_device : per_device + 1, i : i + 1] * (
                2.0 / (sources * pixels * freqs)
            )
            pass_r, pass_i = weight * pupil[s, :freqs], weight * pupil[s, freqs:]
            out_r, out_i = out[:freqs, lanes], out[freqs:, lanes]
            grad_r = grad_r + (pass_r * out_r + pass_i * out_i)
            grad_i = grad_i + (pass_r * out_i - pass_i * out_r)
    grad[:freqs] = grad_r
    grad[freqs : 2 * freqs] = grad_i
    grad[2 * freqs :] = terms


def window_kernel(half, grad_a, grad_b, fwd_h, fwd_l, adj_h, adj_l, *outs):
    bodies, edges = outs[:half], outs[half:]
    rows, pixels = bodies[0].shape[0] - PAD, bodies[0].shape[1]
    freqs = grad_a.shape[1]
    src, row, tile = lax.axis_index("src"), lax.axis_index("row"), lax.axis_index("tile")
    total = grad_a[: 2 * freqs] + grad_b[: 2 * freqs]
    flat = split(jnp.concatenate([total[:freqs], total[freqs:]], axis=1))
    waves = mm3(flat, (fwd_h[...], fwd_l[...]))
    waves = jnp.concatenate([waves[:, :pixels], waves[:, pixels:]], axis=0)
    tables = []
    for table in (adj_h, adj_l):
        parts = []
        for steps in range(half):
            start = (block_of(src, 0, steps, half) * 2 + row) * rows
            parts.append(table[pl.ds(pl.multiple_of(start, rows), rows), :])
        tables.append(jnp.concatenate(parts, axis=0))
    window = mm3(tables, split(waves))
    terms = jnp.where(row == 0, grad_a[2 * freqs :], grad_b[2 * freqs :])
    for steps in range(half):
        block = window[steps * rows : (steps + 1) * rows]
        term = terms[steps : steps + 1]
        bodies[steps][:rows] = block
        bodies[steps][rows : rows + 1, :freqs] = term
        edge = jnp.where(tile == 0, block[:, pixels - OV :], block[:, :OV])
        edges[steps][:rows, :OV] = edge
        edges[steps][rows : rows + 1, :] = term


def place_kernel(half, term_scale, *refs):
    bodies, edges = refs[:half], refs[half : 2 * half]
    out, source = refs[2 * half :]
    rows, pixels = out.shape[1:]
    per_device = source.shape[1]
    src, tile = lax.axis_index("src"), lax.axis_index("tile")
    steps = jnp.where(src < half, half - 1 - src, src - half)

    def mine(refs, *index):
        value = refs[0][index]
        for n in range(1, half):
            value = jnp.where(steps == n, refs[n][index], value)
        return value

    body = mine(bodies, slice(0, rows), slice(None))
    edge = mine(edges, slice(0, rows), slice(0, OV))
    zero = jnp.zeros_like(edge)
    middle = jnp.zeros((rows, pixels - 2 * OV), F32)
    low, high = jnp.where(tile == 1, edge, zero), jnp.where(tile == 0, edge, zero)
    out[0] = body + jnp.concatenate([low, middle, high], axis=1)
    term = slice(rows, rows + 1), slice(0, per_device)
    source[...] = (mine(bodies, *term) + mine(edges, *term)) * term_scale


def call(kernel, outs, scratch=(), kind=F32):
    return pl.pallas_call(
        kernel,
        out_shape=[jax.ShapeDtypeStruct(shape, kind) for shape in outs],
        out_specs=[pl.BlockSpec(memory_space=pltpu.VMEM) for _ in outs],
        scratch_shapes=[pltpu.VMEM(shape, scratch_kind) for shape, scratch_kind in scratch],
        compiler_params=pltpu.CompilerParams(vmem_limit_bytes=VMEM_BUDGET),
    )


def swap_rows(x):
    return lax.ppermute(x, "row", [(0, 1), (1, 0)])


def hub_shards(mask_windows, target_windows, pupil_bands, pupil_phase, source_weight):
    src_count, tile_count = lax.axis_size("src"), lax.axis_size("tile")
    rows, pixels = mask_windows.shape[1:]
    per_device, freqs = pupil_phase.shape[:2]
    sources = per_device * src_count
    half = src_count // 2
    count = half * per_device

    def chip(low, steps):
        return half - 1 - steps if low else half + steps

    def to_hub(x, side, steps, cores=(0, 1)):
        sides = dict.fromkeys(cores, side) if side is not None else {0: 0, 1: 1}
        pairs = []
        for low in (True, False):
            for core, across in sides.items():
                source, hub = chip(low, steps), chip(low != (across == 1), 0)
                if source != hub:
                    pairs.append((source * 2 + core, hub * 2 + core))
        return lax.ppermute(x, ("src", "row"), pairs)

    (message,) = call(message_kernel, [(2 * rows + PAD, pixels)])(
        mask_windows,
        target_windows,
        pupil_bands.transpose(0, 2, 1),
        source_weight.reshape(1, per_device),
    )
    blocks = [message] + [to_hub(message, 0, n) for n in range(1, half)]
    blocks += [to_hub(message, 1, n) for n in range(half)]
    phases = [to_hub(pupil_phase, None, n) for n in range(half)]
    tables = call(
        tables_kernel, [(2 * freqs, 2 * pixels)] * 2 + [(2 * pixels, 2 * freqs)] * 2, kind=BF16
    )()

    spec, goal, meta = call(
        functools.partial(spectrum_kernel, half),
        [(2 * freqs, freqs), (src_count, rows, pixels), (half, PAD, pixels)],
        [((2 * pixels, freqs), F32)],
    )(*blocks, *tables)
    spec_other = swap_rows(spec)
    goal_other = swap_rows(goal)

    field, pupil, inten = call(
        functools.partial(fields_kernel, per_device, sources, half),
        [(count, pixels, 2 * pixels), (count, 2 * freqs, freqs), (pixels, pixels)],
        [((2 * freqs, count * freqs), BF16)] * 2,
    )(pupil_phase, *phases, spec, spec_other, meta, *tables)
    inten_other = swap_rows(inten)

    (grad,) = call(
        functools.partial(adjoint_kernel, per_device, sources),
        [(2 * freqs + PAD, freqs)],
        [((pixels, pixels), F32)] + [((2 * pixels, count * freqs), BF16)] * 2,
    )(field, pupil, inten, inten_other, goal, goal_other, meta, *tables)
    grad_other = swap_rows(grad)

    outs = call(
        functools.partial(window_kernel, half),
        [(rows + PAD, pixels)] * half + [(rows + PAD, freqs)] * half,
    )(grad, grad_other, *tables)
    bodies, edges = outs[:half], outs[half:]

    def from_hub(x, steps, flip):
        pairs = []
        for low in (True, False):
            for tile in range(2):
                target = tile ^ 1 if flip else tile
                pairs.append((chip(low, 0) * 2 + tile, chip(low, steps) * 2 + target))
        return lax.ppermute(x, ("src", "tile"), pairs)

    bodies = [bodies[0]] + [from_hub(bodies[n], n, False) for n in range(1, half)]
    edges = [from_hub(edges[n], n, True) for n in range(half)]
    out, source = call(
        functools.partial(place_kernel, half, 1.0 / (sources * pixels * tile_count)),
        [(1, rows, pixels), (1, per_device)],
    )(*bodies, *edges)
    return out, source[0]


M = 256
K = 128


def with_halo(block, sides, width):
    for axis, dim in sides:
        count = lax.axis_size(axis)
        forward = [(i, i + 1) for i in range(count - 1)]
        backward = [(target, source) for source, target in forward]
        low = lax.ppermute(
            lax.slice_in_dim(block, block.shape[dim] - width, None, axis=dim), axis, forward
        )
        high = lax.ppermute(lax.slice_in_dim(block, 0, width, axis=dim), axis, backward)
        block = jnp.concatenate([low, block, high], axis=dim)
    return block


def matmul(left_op, right_op):
    return lax.dot_general(
        left_op,
        right_op,
        (((1,), (0,)), ((), ())),
        precision=lax.Precision.HIGHEST,
        preferred_element_type=jnp.float32,
    )


def matmul_tn(left_op, right_op):
    return lax.dot_general(
        left_op,
        right_op,
        (((0,), (0,)), ((), ())),
        precision=lax.Precision.HIGHEST,
        preferred_element_type=jnp.float32,
    )


def matmul_nt(left_op, right_op):
    return lax.dot_general(
        left_op,
        right_op,
        (((1,), (1,)), ((), ())),
        precision=lax.Precision.HIGHEST,
        preferred_element_type=jnp.float32,
    )


def wave_tables(positions):
    freq_index = jnp.arange(K, dtype=jnp.int32) - K // 2
    phase_index = freq_index[:, None] * positions[None, :] % M
    angles = 2.0 * math.pi / M * phase_index.astype(jnp.float32)
    return (jnp.cos(angles), jnp.sin(angles))


def shards(mask_windows, target_windows, pupil_bands, pupil_phase, source_weight):
    src_count = lax.axis_size("src")
    tile_count = lax.axis_size("tile")
    row_count = lax.axis_size("row")
    local_x = mask_windows.shape[1]
    per_device = pupil_phase.shape[0]
    sources = per_device * src_count
    field_scale = 1.0 / (M * K)
    src_id = lax.axis_index("src")
    row_id = lax.axis_index("row")
    x_start = (src_id * row_count + row_id) * local_x
    block_starts = (jnp.arange(src_count, dtype=jnp.int32) * row_count + row_id) * local_x
    row_set = (block_starts[:, None] + jnp.arange(local_x, dtype=jnp.int32)[None, :]).reshape(
        src_count * local_x
    )
    cos_all, sin_all = wave_tables(jnp.arange(M, dtype=jnp.int32))
    cos_set, sin_set = wave_tables(row_set)
    cos_own, sin_own = wave_tables(x_start + jnp.arange(local_x, dtype=jnp.int32))
    window = mask_windows[0]
    goal_block = target_windows[0]
    zero_spec = jnp.zeros((K, K), jnp.float32)
    shard_rows = lax.all_gather(window, ("src", "row"), axis=0, tiled=True)
    part_real = matmul_nt(shard_rows, cos_all)
    part_imag = -matmul_nt(shard_rows, sin_all)
    spec_real = matmul(cos_all, part_real) + matmul(sin_all, part_imag)
    spec_imag = matmul(cos_all, part_imag) - matmul(sin_all, part_real)
    freq_cols = jnp.arange(K, dtype=jnp.int32)
    inside = (freq_cols[None, None, :] >= pupil_bands[:, :, 0:1]) & (
        freq_cols[None, None, :] < pupil_bands[:, :, 1:2]
    )
    passing = inside.astype(jnp.float32)
    pupil_real = passing * jnp.cos(pupil_phase)
    pupil_imag = passing * jnp.sin(pupil_phase)
    amp_real = (pupil_real * spec_real - pupil_imag * spec_imag).reshape(per_device * K, K)
    amp_imag = (pupil_imag * spec_real + pupil_real * spec_imag).reshape(per_device * K, K)
    half_real = (matmul(amp_real, cos_all) - matmul(amp_imag, sin_all)).reshape(per_device, K, M)
    half_imag = (matmul(amp_real, sin_all) + matmul(amp_imag, cos_all)).reshape(per_device, K, M)
    weights = source_weight / sources

    def fields(pair_in):
        one_real, one_imag = pair_in
        field_real = field_scale * (matmul_tn(cos_set, one_real) - matmul_tn(sin_set, one_imag))
        field_imag = field_scale * (matmul_tn(cos_set, one_imag) + matmul_tn(sin_set, one_real))
        return (field_real, field_imag)

    stack_real, stack_imag = lax.map(fields, (half_real, half_imag))
    part_real = stack_real
    part_imag = stack_imag
    intensity = lax.psum_scatter(
        jnp.sum(weights[:, None, None] * (part_real * part_real + part_imag * part_imag), axis=0),
        "src",
        scatter_dimension=0,
        tiled=True,
    )
    resist = jax.nn.sigmoid(STEEPNESS * (intensity - THRESHOLD))
    cotangent = LOSS_SCALE * (resist - goal_block) * STEEPNESS * resist * (1.0 - resist)
    cotangent_all = lax.all_gather(cotangent, "src", axis=0, tiled=True)
    source_ids = jnp.arange(per_device, dtype=jnp.int32)

    def add_back(source_id, totals):
        grad_real, grad_imag, source_terms = totals
        field_real = stack_real[source_id]
        field_imag = stack_imag[source_id]
        back_scale = 2.0 * weights[source_id] * cotangent_all
        back_real = back_scale * field_real
        back_imag = back_scale * field_imag
        adj_real = matmul(cos_set, back_real) + matmul(sin_set, back_imag)
        adj_imag = matmul(cos_set, back_imag) - matmul(sin_set, back_real)
        amp_grad_real = field_scale * (matmul_nt(adj_real, cos_all) + matmul_nt(adj_imag, sin_all))
        amp_grad_imag = field_scale * (matmul_nt(adj_imag, cos_all) - matmul_nt(adj_real, sin_all))
        pass_real = pupil_real[source_id]
        pass_imag = pupil_imag[source_id]
        grad_real = grad_real + pass_real * amp_grad_real + pass_imag * amp_grad_imag
        grad_imag = grad_imag + pass_real * amp_grad_imag - pass_imag * amp_grad_real
        term_value = jnp.sum(cotangent_all * (field_real * field_real + field_imag * field_imag))
        source_terms = source_terms + jnp.where(source_ids == source_id, term_value, 0.0)
        return (grad_real, grad_imag, source_terms)

    grad_real, grad_imag, source_terms = lax.fori_loop(
        0, per_device, add_back, (zero_spec, zero_spec, jnp.zeros((per_device,), jnp.float32))
    )
    grad_real, grad_imag = lax.psum((grad_real, grad_imag), ("src", "row"))
    source_sum = lax.psum(source_terms, ("tile", "row"))
    source_grad = source_sum / (sources * M * tile_count)
    q_one = matmul(grad_real, cos_all) - matmul(grad_imag, sin_all)
    q_two = matmul(grad_real, sin_all) + matmul(grad_imag, cos_all)
    grad_block = matmul_tn(cos_own, q_one) - matmul_tn(sin_own, q_two)
    padded = with_halo(grad_block, (("tile", 1),), OV)
    from_below = padded[:, :OV]
    from_above = padded[:, M + OV :]
    middle = jnp.zeros((local_x, M - 2 * OV), jnp.float32)
    grad_block = grad_block + jnp.concatenate([from_below, middle, from_above], axis=1)
    return (grad_block[None], source_grad)


def hubs_serve(mesh, mask_windows, pupil_phase):
    src_count = mesh.shape["src"]
    pixels = mask_windows.shape[2]
    sources, freqs = pupil_phase.shape[0] // mesh.shape["parts"], pupil_phase.shape[1]
    per_device = sources // src_count
    held = sources // 2 * (2 * pixels * pixels + 4 * freqs * freqs) * 4
    return (
        mesh.shape["row"] == 2
        and mesh.shape["tile"] == 2
        and src_count % 2 == 0
        and src_count // 2 <= PAD
        and per_device < PAD
        and mask_windows.shape[1] // (2 * src_count) % 16 == 0
        and pixels & (pixels - 1) == 0
        and pixels >= 2 * freqs
        and held <= VMEM_BUDGET // 2
    )


def solution(mesh):
    def run(mask_windows, target_windows, pupil_bands, pupil_phase, source_weight):
        hubs = hubs_serve(mesh, mask_windows, pupil_phase)
        return jax.shard_map(
            hub_shards if hubs else shards,
            mesh=mesh,
            in_specs=(
                P(("parts", "tile"), ("src", "row"), None),
                P(("parts", "tile"), ("src", "row"), None),
                P(("parts", "src"), None, None),
                P(("parts", "src"), None, None),
                P(("parts", "src")),
            ),
            out_specs=(P(("parts", "tile"), ("src", "row"), None), P(("parts", "src"))),
            check_vma=False,
        )(mask_windows, target_windows, pupil_bands, pupil_phase, source_weight)

    return run
```

```python
import functools
import itertools
import math

import jax
import jax.numpy as jnp
from jax import lax
from jax.experimental import pallas as pl
from jax.experimental.pallas import tpu as pltpu
from jax.sharding import PartitionSpec as P

OV = 32
STEEPNESS = 20.0
THRESHOLD = 0.15
LOSS_SCALE = 32.0
PAD = 8
F32 = jnp.float32
BF16 = jnp.bfloat16
VMEM_BUDGET = 24 * 1024 * 1024


def split(a):
    high = a.astype(BF16)
    return high, (a - high.astype(F32)).astype(BF16)


def dot(a, b):
    return jnp.dot(a, b, preferred_element_type=F32)


def dot_nt(a, b):
    return lax.dot_general(a, b, (((1,), (1,)), ((), ())), preferred_element_type=F32)


def mm3(left, right, op=dot):
    (lh, ll), (rh, rl) = left, right
    return op(lh, rh) + (op(lh, rl) + op(ll, rh))


def sincos(phase):
    h = 0.5 * phase
    u = h * h
    s = 1.0 / 6227020800.0
    for coef in (-1.0 / 39916800.0, 1.0 / 362880.0, -1.0 / 5040.0, 1.0 / 120.0, -1.0 / 6.0, 1.0):
        s = s * u + coef
    s = s * h
    c = 1.0 / 479001600.0
    for coef in (-1.0 / 3628800.0, 1.0 / 40320.0, -1.0 / 720.0, 1.0 / 24.0, -0.5, 1.0):
        c = c * u + coef
    two_s = s + s
    return two_s * c, 1.0 - two_s * s


def block_of(src, side, steps, half):
    same = half - 1 - steps
    other = half + steps
    low = src < half
    return jnp.where(low, same if side == 0 else other, other if side == 0 else same)


def fetch_kernel(mask, goal, bands, weight, phase, message, held, bands_in, weight_in, sems):
    rows = mask.shape[1]
    per_device, _, freqs = bands.shape
    message[2 * rows :] = jnp.zeros_like(message[2 * rows :])
    copies = [
        pltpu.make_async_copy(source, target, sems.at[n])
        for n, (source, target) in enumerate(
            (
                (mask.at[0], message.at[pl.ds(0, rows)]),
                (goal.at[0], message.at[pl.ds(rows, rows)]),
                (bands, bands_in),
                (weight, weight_in),
                (phase, held),
            )
        )
    ]
    for copy in copies:
        copy.start()
    for copy in copies:
        copy.wait()
    for i in range(per_device):
        for n in range(2):
            message[2 * rows + i : 2 * rows + i + 1, n * freqs : (n + 1) * freqs] = bands_in[
                i, n : n + 1, :
            ].astype(F32)
    line = 2 * rows + per_device
    message[line : line + 1, :per_device] = weight_in[...]


def tables_kernel(fwd_h, fwd_l, adj_h, adj_l):
    freqs, pixels = fwd_h.shape[0] // 2, fwd_h.shape[1] // 2

    def waves(shape, freq_dim):
        freq = lax.broadcasted_iota(jnp.int32, shape, freq_dim) - freqs // 2
        turn = freq * lax.broadcasted_iota(jnp.int32, shape, 1 - freq_dim)
        turn = ((turn + pixels // 2) & (pixels - 1)) - pixels // 2
        sin, cos = sincos((2.0 * math.pi / pixels) * turn.astype(F32))
        return split(cos), split(sin)

    (cos_h, cos_l), (sin_h, sin_l) = waves((freqs, pixels), 0)
    for table, cos, sin in ((fwd_h, cos_h, sin_h), (fwd_l, cos_l, sin_l)):
        table[:freqs, :pixels] = cos
        table[:freqs, pixels:] = sin
        table[freqs:, :pixels] = -sin
        table[freqs:, pixels:] = cos
    (cos_h, cos_l), (sin_h, sin_l) = waves((pixels, freqs), 1)
    for table, cos, sin in ((adj_h, cos_h, sin_h), (adj_l, cos_l, sin_l)):
        table[:pixels, :freqs] = cos
        table[:pixels, freqs:] = -sin
        table[pixels:, :freqs] = sin
        table[pixels:, freqs:] = cos


def spectrum_kernel(half, *refs):
    blocks = refs[: 2 * half]
    fwd_h, fwd_l, adj_h, adj_l, spec, goal, meta, part = refs[2 * half :]
    rows, pixels = goal.shape[1], goal.shape[2]
    freqs = spec.shape[1]
    src, row = lax.axis_index("src"), lax.axis_index("row")
    own = jnp.concatenate([b[:rows] for b in blocks], axis=0)
    waves = mm3(split(own), (adj_h[:pixels], adj_l[:pixels]))
    part[...] = jnp.zeros_like(part)
    for d in range(2 * half):
        block = block_of(src, d // half, d % half, half)
        start = pl.multiple_of((block * 2 + row) * rows, rows)
        mine = waves[d * rows : (d + 1) * rows]
        part[pl.ds(start, rows), :] = mine[:, :freqs]
        part[pl.ds(pl.multiple_of(pixels + start, rows), rows), :] = mine[:, freqs:]
        goal[block] = blocks[d][rows : 2 * rows]
    for j in range(half):
        meta[j] = jnp.where(row == 0, blocks[j][2 * rows :], blocks[half + j][2 * rows :])
    spec[...] = mm3((fwd_h[...], fwd_l[...]), split(part[...]))


def fields_kernel(per_device, sources, slots, *refs):
    phase_own, *phases = refs[: slots + 1]
    spec_a, spec_b, meta, fwd_h, fwd_l, adj_h, adj_l = refs[slots + 1 : slots + 8]
    field, pupil, intensity, amp_h, amp_l = refs[slots + 8 :]
    row = lax.axis_index("row")
    pixels = intensity.shape[1]
    freqs = spec_a.shape[1]
    spec = (spec_a[...] + spec_b[...]) * (1.0 / (pixels * freqs))
    spec_r, spec_i = spec[:freqs], spec[freqs:]
    column = lax.broadcasted_iota(jnp.int32, (freqs, freqs), 1).astype(F32)
    weight = []
    for j in range(slots):
        info = meta[j]
        bounds = info.T
        for i in range(per_device):
            s = j * per_device + i
            weight.append(info[per_device : per_device + 1, i : i + 1] * (1.0 / sources))
            inside = (column >= bounds[:freqs, i : i + 1]) & (
                column < bounds[freqs : 2 * freqs, i : i + 1]
            )
            phase = phases[j][i]
            if j == 0:
                phase = jnp.where(row == 0, phase_own[i], phase)
            sin_p, cos_p = sincos(phase)
            pass_r = jnp.where(inside, cos_p, 0.0)
            pass_i = jnp.where(inside, sin_p, 0.0)
            pupil[s, :freqs] = pass_r
            pupil[s, freqs:] = pass_i
            lanes = slice(s * freqs, (s + 1) * freqs)
            for half, value in enumerate(
                (pass_r * spec_r - pass_i * spec_i, pass_i * spec_r + pass_r * spec_i)
            ):
                high, low = split(value)
                amp_h[half * freqs : (half + 1) * freqs, lanes] = high
                amp_l[half * freqs : (half + 1) * freqs, lanes] = low
    total = jnp.zeros_like(intensity)
    group = 2
    for first in range(0, slots * per_device, group):
        members = range(first, min(first + group, slots * per_device))
        lanes = slice(first * freqs, (members[-1] + 1) * freqs)
        half = mm3((adj_h[...], adj_l[...]), (amp_h[:, lanes], amp_l[:, lanes]))
        for n, s in enumerate(members):
            lanes = slice(n * freqs, (n + 1) * freqs)
            pair = jnp.concatenate([half[:pixels, lanes], half[pixels:, lanes]], axis=1)
            out = mm3(split(pair), (fwd_h[...], fwd_l[...]))
            field[s] = out
            out_r, out_i = out[:, :pixels], out[:, pixels:]
            total = total + weight[s] * (out_r * out_r + out_i * out_i)
    intensity[...] = total


def adjoint_kernel(per_device, sources, *refs):
    (field, pupil, inten_a, inten_b, goal_a, goal_b, meta, fwd_h, fwd_l, adj_h, adj_l) = refs[:11]
    grad, cot_ref, back_h, back_l = refs[11:]
    src_count, rows = goal_a.shape[0], goal_a.shape[1]
    pixels = inten_a.shape[1]
    freqs = grad.shape[1]
    row = lax.axis_index("row")
    for z in range(src_count):
        for r in range(2):
            here = slice((2 * z + r) * rows, (2 * z + r + 1) * rows)
            goal = jnp.where(row == r, goal_a[z], goal_b[z])
            intensity = inten_a[here] + inten_b[here]
            resist = 1.0 / (1.0 + jnp.exp(-STEEPNESS * (intensity - THRESHOLD)))
            cot_ref[here] = (LOSS_SCALE * STEEPNESS) * (resist - goal) * resist * (1.0 - resist)
    cot = cot_ref[...]
    count = field.shape[0]
    line = lax.broadcasted_iota(jnp.int32, (PAD, freqs), 0)
    lane = lax.broadcasted_iota(jnp.int32, (PAD, freqs), 1)
    terms = jnp.zeros((PAD, freqs), F32)
    for s in range(count):
        value = field[s]
        back_r, back_i = cot * value[:, :pixels], cot * value[:, pixels:]
        power = back_r * value[:, :pixels] + back_i * value[:, pixels:]
        power = jnp.sum(jnp.sum(power, axis=0, keepdims=True), axis=1, keepdims=True)
        j, i = divmod(s, per_device)
        terms = terms + jnp.where((lane == i) & (line == j), power, 0.0)
        back = jnp.concatenate([back_r, back_i], axis=1)
        half = mm3(split(back), (adj_h[...], adj_l[...]))
        lanes = slice(s * freqs, (s + 1) * freqs)
        for n in range(2):
            high, low = split(half[:, n * freqs : (n + 1) * freqs])
            back_h[n * pixels : (n + 1) * pixels, lanes] = high
            back_l[n * pixels : (n + 1) * pixels, lanes] = low
    grad_r = jnp.zeros((freqs, freqs), F32)
    grad_i = jnp.zeros((freqs, freqs), F32)
    group = 2
    for first in range(0, count, group):
        members = range(first, min(first + group, count))
        lanes = slice(first * freqs, (members[-1] + 1) * freqs)
        out = mm3((fwd_h[...], fwd_l[...]), (back_h[:, lanes], back_l[:, lanes]))
        for n, s in enumerate(members):
            lanes = slice(n * freqs, (n + 1) * freqs)
            j, i = divmod(s, per_device)
            weight = meta[j][per_device : per_device + 1, i : i + 1] * (
                2.0 / (sources * pixels * freqs)
            )
            pass_r, pass_i = weight * pupil[s, :freqs], weight * pupil[s, freqs:]
            out_r, out_i = out[:freqs, lanes], out[freqs:, lanes]
            grad_r = grad_r + (pass_r * out_r + pass_i * out_i)
            grad_i = grad_i + (pass_r * out_i - pass_i * out_r)
    grad[:freqs] = grad_r
    grad[freqs : 2 * freqs] = grad_i
    grad[2 * freqs :] = terms


def window_kernel(half, grad_a, grad_b, fwd_h, fwd_l, adj_h, adj_l, *outs):
    bodies, edges = outs[:half], outs[half:]
    rows, pixels = bodies[0].shape[0] - PAD, bodies[0].shape[1]
    freqs = grad_a.shape[1]
    src, row, tile = lax.axis_index("src"), lax.axis_index("row"), lax.axis_index("tile")
    total = grad_a[: 2 * freqs] + grad_b[: 2 * freqs]
    flat = split(jnp.concatenate([total[:freqs], total[freqs:]], axis=1))
    waves = mm3(flat, (fwd_h[...], fwd_l[...]))
    waves = jnp.concatenate([waves[:, :pixels], waves[:, pixels:]], axis=0)
    tables = []
    for table in (adj_h, adj_l):
        parts = []
        for steps in range(half):
            start = (block_of(src, 0, steps, half) * 2 + row) * rows
            parts.append(table[pl.ds(pl.multiple_of(start, rows), rows), :])
        tables.append(jnp.concatenate(parts, axis=0))
    window = mm3(tables, split(waves))
    terms = jnp.where(row == 0, grad_a[2 * freqs :], grad_b[2 * freqs :])
    for steps in range(half):
        block = window[steps * rows : (steps + 1) * rows]
        term = terms[steps : steps + 1]
        bodies[steps][:rows] = block
        bodies[steps][rows : rows + 1, :freqs] = term
        edge = jnp.where(tile == 0, block[:, pixels - OV :], block[:, :OV])
        edges[steps][:rows, :OV] = edge
        edges[steps][rows : rows + 1, :] = term


def place_kernel(half, term_scale, *refs):
    bodies, edges = refs[:half], refs[half : 2 * half]
    out, source = refs[2 * half :]
    rows, pixels = out.shape[1:]
    per_device = source.shape[1]
    src, tile = lax.axis_index("src"), lax.axis_index("tile")
    steps = jnp.where(src < half, half - 1 - src, src - half)

    def mine(refs, *index):
        value = refs[0][index]
        for n in range(1, half):
            value = jnp.where(steps == n, refs[n][index], value)
        return value

    body = mine(bodies, slice(0, rows), slice(None))
    edge = mine(edges, slice(0, rows), slice(0, OV))
    zero = jnp.zeros_like(edge)
    middle = jnp.zeros((rows, pixels - 2 * OV), F32)
    low, high = jnp.where(tile == 1, edge, zero), jnp.where(tile == 0, edge, zero)
    out[0] = body + jnp.concatenate([low, middle, high], axis=1)
    term = slice(rows, rows + 1), slice(0, per_device)
    source[...] = (mine(bodies, *term) + mine(edges, *term)) * term_scale


def call(kernel, outs, scratch=(), kind=F32, hbm=False):
    held = {"in_specs": [pl.BlockSpec(memory_space=pltpu.HBM)] * 5} if hbm else {}
    return pl.pallas_call(
        kernel,
        out_shape=[jax.ShapeDtypeStruct(shape, kind) for shape in outs],
        out_specs=[pl.BlockSpec(memory_space=pltpu.VMEM) for _ in outs],
        scratch_shapes=list(scratch),
        compiler_params=pltpu.CompilerParams(vmem_limit_bytes=VMEM_BUDGET),
        **held,
    )


def permute(x, wanted):
    shape = tuple(lax.axis_size(a) for a in ("src", "tile", "row"))
    devices = list(itertools.product(*(range(n) for n in shape)))
    pairs = dict(wanted)
    sources = [d for d in devices if d not in pairs]
    targets = [d for d in devices if d not in pairs.values()]

    def cost(pair):
        source, target = pair
        hops = abs(source[0] - target[0]) + abs(source[1] - target[1])
        return (source == target, hops, source, target)

    for source, target in sorted(itertools.product(sources, targets), key=cost):
        if source not in pairs and target not in pairs.values():
            pairs[source] = target
    flat = {d: n for n, d in enumerate(devices)}
    return lax.ppermute(x, ("src", "tile", "row"), [(flat[a], flat[b]) for a, b in pairs.items()])


def swap_rows(x):
    return lax.ppermute(x, "row", [(0, 1), (1, 0)])


def hub_shards(mask_windows, target_windows, pupil_bands, pupil_phase, source_weight):
    src_count, tile_count = lax.axis_size("src"), lax.axis_size("tile")
    rows, pixels = mask_windows.shape[1:]
    per_device, freqs = pupil_phase.shape[:2]
    sources = per_device * src_count
    half = src_count // 2
    count = half * per_device

    def chip(low, steps):
        return half - 1 - steps if low else half + steps

    cores = list(itertools.product(range(tile_count), range(2)))
    halves = (True, False)

    def to_hub(x, side, steps):
        return permute(
            x,
            {
                (chip(low, steps), t, c): (chip(low != (side == 1), 0), t, c)
                for low in halves
                for t, c in cores
            },
        )

    def phases_to_hub(x, steps):
        pairs = {}
        for low, tile in itertools.product(halves, range(tile_count)):
            if steps:
                pairs[chip(low, steps), tile, 0] = chip(low, 0), tile, 0
            pairs[chip(low, steps), tile, 1 if steps else 0] = chip(not low, 0), tile, 1
        return permute(x, pairs)

    pin = functools.partial(pltpu.with_memory_space_constraint, memory_space=pltpu.HBM)
    message, phase = call(
        fetch_kernel,
        [(2 * rows + PAD, pixels), pupil_phase.shape],
        [
            pltpu.VMEM((per_device, 2, freqs), jnp.int32),
            pltpu.VMEM((1, per_device), F32),
            pltpu.SemaphoreType.DMA((5,)),
        ],
        hbm=True,
    )(
        pin(mask_windows),
        pin(target_windows),
        pin(pupil_bands.transpose(0, 2, 1)),
        pin(source_weight.reshape(1, per_device)),
        pin(pupil_phase),
    )
    blocks = [message] + [to_hub(message, 0, n) for n in range(1, half)]
    blocks += [to_hub(message, 1, n) for n in reversed(range(half))][::-1]
    phases = [phases_to_hub(phase, n) for n in reversed(range(half))][::-1]
    tables = call(
        tables_kernel, [(2 * freqs, 2 * pixels)] * 2 + [(2 * pixels, 2 * freqs)] * 2, kind=BF16
    )()

    spec, goal, meta = call(
        functools.partial(spectrum_kernel, half),
        [(2 * freqs, freqs), (src_count, rows, pixels), (half, PAD, pixels)],
        [pltpu.VMEM((2 * pixels, freqs), F32)],
    )(*blocks, *tables)
    spec_other = swap_rows(spec)
    goal_other = swap_rows(goal)

    field, pupil, inten = call(
        functools.partial(fields_kernel, per_device, sources, half),
        [(count, pixels, 2 * pixels), (count, 2 * freqs, freqs), (pixels, pixels)],
        [pltpu.VMEM((2 * freqs, count * freqs), BF16)] * 2,
    )(phase, *phases, spec, spec_other, meta, *tables)
    inten_other = swap_rows(inten)

    (grad,) = call(
        functools.partial(adjoint_kernel, per_device, sources),
        [(2 * freqs + PAD, freqs)],
        [pltpu.VMEM((pixels, pixels), F32)]
        + [pltpu.VMEM((2 * pixels, count * freqs), BF16)] * 2,
    )(field, pupil, inten, inten_other, goal, goal_other, meta, *tables)
    grad_other = swap_rows(grad)

    outs = call(
        functools.partial(window_kernel, half),
        [(rows + PAD, pixels)] * half + [(rows + PAD, freqs)] * half,
    )(grad, grad_other, *tables)
    bodies, edges = outs[:half], outs[half:]

    def from_hub(x, steps, flip):
        return permute(
            x,
            {
                (chip(low, 0), t, c): (chip(low, steps), 1 - t if flip else t, c)
                for low in halves
                for t, c in cores
            },
        )

    bodies = [bodies[0]] + [from_hub(bodies[n], n, False) for n in range(1, half)]
    edges = [from_hub(edges[n], n, True) for n in range(half)]
    out, source = call(
        functools.partial(place_kernel, half, 1.0 / (sources * pixels * tile_count)),
        [(1, rows, pixels), (1, per_device)],
    )(*bodies, *edges)
    return out, source[0]


M = 256
K = 128


def with_halo(block, sides, width):
    for axis, dim in sides:
        count = lax.axis_size(axis)
        forward = [(i, i + 1) for i in range(count - 1)]
        backward = [(target, source) for source, target in forward]
        low = lax.ppermute(
            lax.slice_in_dim(block, block.shape[dim] - width, None, axis=dim), axis, forward
        )
        high = lax.ppermute(lax.slice_in_dim(block, 0, width, axis=dim), axis, backward)
        block = jnp.concatenate([low, block, high], axis=dim)
    return block


def matmul(left_op, right_op):
    return lax.dot_general(
        left_op,
        right_op,
        (((1,), (0,)), ((), ())),
        precision=lax.Precision.HIGHEST,
        preferred_element_type=jnp.float32,
    )


def matmul_tn(left_op, right_op):
    return lax.dot_general(
        left_op,
        right_op,
        (((0,), (0,)), ((), ())),
        precision=lax.Precision.HIGHEST,
        preferred_element_type=jnp.float32,
    )


def matmul_nt(left_op, right_op):
    return lax.dot_general(
        left_op,
        right_op,
        (((1,), (1,)), ((), ())),
        precision=lax.Precision.HIGHEST,
        preferred_element_type=jnp.float32,
    )


def wave_tables(positions):
    freq_index = jnp.arange(K, dtype=jnp.int32) - K // 2
    phase_index = freq_index[:, None] * positions[None, :] % M
    angles = 2.0 * math.pi / M * phase_index.astype(jnp.float32)
    return (jnp.cos(angles), jnp.sin(angles))


def shards(mask_windows, target_windows, pupil_bands, pupil_phase, source_weight):
    src_count = lax.axis_size("src")
    tile_count = lax.axis_size("tile")
    row_count = lax.axis_size("row")
    local_x = mask_windows.shape[1]
    per_device = pupil_phase.shape[0]
    sources = per_device * src_count
    field_scale = 1.0 / (M * K)
    src_id = lax.axis_index("src")
    row_id = lax.axis_index("row")
    x_start = (src_id * row_count + row_id) * local_x
    block_starts = (jnp.arange(src_count, dtype=jnp.int32) * row_count + row_id) * local_x
    row_set = (block_starts[:, None] + jnp.arange(local_x, dtype=jnp.int32)[None, :]).reshape(
        src_count * local_x
    )
    cos_all, sin_all = wave_tables(jnp.arange(M, dtype=jnp.int32))
    cos_set, sin_set = wave_tables(row_set)
    cos_own, sin_own = wave_tables(x_start + jnp.arange(local_x, dtype=jnp.int32))
    window = mask_windows[0]
    goal_block = target_windows[0]
    zero_spec = jnp.zeros((K, K), jnp.float32)
    shard_rows = lax.all_gather(window, ("src", "row"), axis=0, tiled=True)
    part_real = matmul_nt(shard_rows, cos_all)
    part_imag = -matmul_nt(shard_rows, sin_all)
    spec_real = matmul(cos_all, part_real) + matmul(sin_all, part_imag)
    spec_imag = matmul(cos_all, part_imag) - matmul(sin_all, part_real)
    freq_cols = jnp.arange(K, dtype=jnp.int32)
    inside = (freq_cols[None, None, :] >= pupil_bands[:, :, 0:1]) & (
        freq_cols[None, None, :] < pupil_bands[:, :, 1:2]
    )
    passing = inside.astype(jnp.float32)
    pupil_real = passing * jnp.cos(pupil_phase)
    pupil_imag = passing * jnp.sin(pupil_phase)
    amp_real = (pupil_real * spec_real - pupil_imag * spec_imag).reshape(per_device * K, K)
    amp_imag = (pupil_imag * spec_real + pupil_real * spec_imag).reshape(per_device * K, K)
    half_real = (matmul(amp_real, cos_all) - matmul(amp_imag, sin_all)).reshape(per_device, K, M)
    half_imag = (matmul(amp_real, sin_all) + matmul(amp_imag, cos_all)).reshape(per_device, K, M)
    weights = source_weight / sources

    def fields(pair_in):
        one_real, one_imag = pair_in
        field_real = field_scale * (matmul_tn(cos_set, one_real) - matmul_tn(sin_set, one_imag))
        field_imag = field_scale * (matmul_tn(cos_set, one_imag) + matmul_tn(sin_set, one_real))
        return (field_real, field_imag)

    stack_real, stack_imag = lax.map(fields, (half_real, half_imag))
    part_real = stack_real
    part_imag = stack_imag
    intensity = lax.psum_scatter(
        jnp.sum(weights[:, None, None] * (part_real * part_real + part_imag * part_imag), axis=0),
        "src",
        scatter_dimension=0,
        tiled=True,
    )
    resist = jax.nn.sigmoid(STEEPNESS * (intensity - THRESHOLD))
    cotangent = LOSS_SCALE * (resist - goal_block) * STEEPNESS * resist * (1.0 - resist)
    cotangent_all = lax.all_gather(cotangent, "src", axis=0, tiled=True)
    source_ids = jnp.arange(per_device, dtype=jnp.int32)

    def add_back(source_id, totals):
        grad_real, grad_imag, source_terms = totals
        field_real = stack_real[source_id]
        field_imag = stack_imag[source_id]
        back_scale = 2.0 * weights[source_id] * cotangent_all
        back_real = back_scale * field_real
        back_imag = back_scale * field_imag
        adj_real = matmul(cos_set, back_real) + matmul(sin_set, back_imag)
        adj_imag = matmul(cos_set, back_imag) - matmul(sin_set, back_real)
        amp_grad_real = field_scale * (matmul_nt(adj_real, cos_all) + matmul_nt(adj_imag, sin_all))
        amp_grad_imag = field_scale * (matmul_nt(adj_imag, cos_all) - matmul_nt(adj_real, sin_all))
        pass_real = pupil_real[source_id]
        pass_imag = pupil_imag[source_id]
        grad_real = grad_real + pass_real * amp_grad_real + pass_imag * amp_grad_imag
        grad_imag = grad_imag + pass_real * amp_grad_imag - pass_imag * amp_grad_real
        term_value = jnp.sum(cotangent_all * (field_real * field_real + field_imag * field_imag))
        source_terms = source_terms + jnp.where(source_ids == source_id, term_value, 0.0)
        return (grad_real, grad_imag, source_terms)

    grad_real, grad_imag, source_terms = lax.fori_loop(
        0, per_device, add_back, (zero_spec, zero_spec, jnp.zeros((per_device,), jnp.float32))
    )
    grad_real, grad_imag = lax.psum((grad_real, grad_imag), ("src", "row"))
    source_sum = lax.psum(source_terms, ("tile", "row"))
    source_grad = source_sum / (sources * M * tile_count)
    q_one = matmul(grad_real, cos_all) - matmul(grad_imag, sin_all)
    q_two = matmul(grad_real, sin_all) + matmul(grad_imag, cos_all)
    grad_block = matmul_tn(cos_own, q_one) - matmul_tn(sin_own, q_two)
    padded = with_halo(grad_block, (("tile", 1),), OV)
    from_below = padded[:, :OV]
    from_above = padded[:, M + OV :]
    middle = jnp.zeros((local_x, M - 2 * OV), jnp.float32)
    grad_block = grad_block + jnp.concatenate([from_below, middle, from_above], axis=1)
    return (grad_block[None], source_grad)


def hubs_serve(mesh, mask_windows, pupil_phase):
    src_count = mesh.shape["src"]
    pixels = mask_windows.shape[2]
    sources, freqs = pupil_phase.shape[0] // mesh.shape["parts"], pupil_phase.shape[1]
    per_device = sources // src_count
    held = sources // 2 * (2 * pixels * pixels + 4 * freqs * freqs) * 4
    return (
        mesh.shape["row"] == 2
        and mesh.shape["tile"] == 2
        and src_count % 2 == 0
        and src_count // 2 <= PAD
        and per_device < PAD
        and mask_windows.shape[1] // (2 * src_count) % 16 == 0
        and pixels & (pixels - 1) == 0
        and pixels >= 2 * freqs
        and held <= VMEM_BUDGET // 2
    )


def solution(mesh):
    def run(mask_windows, target_windows, pupil_bands, pupil_phase, source_weight):
        hubs = hubs_serve(mesh, mask_windows, pupil_phase)
        return jax.shard_map(
            hub_shards if hubs else shards,
            mesh=mesh,
            in_specs=(
                P(("parts", "tile"), ("src", "row"), None),
                P(("parts", "tile"), ("src", "row"), None),
                P(("parts", "src"), None, None),
                P(("parts", "src"), None, None),
                P(("parts", "src")),
            ),
            out_specs=(P(("parts", "tile"), ("src", "row"), None), P(("parts", "src"))),
            check_vma=False,
        )(mask_windows, target_windows, pupil_bands, pupil_phase, source_weight)

    return run
```

```python
import functools
import itertools
import math

import jax
import jax.numpy as jnp
from jax import lax
from jax.experimental import pallas as pl
from jax.experimental.pallas import tpu as pltpu
from jax.sharding import PartitionSpec as P

OV = 32
STEEPNESS = 20.0
THRESHOLD = 0.15
LOSS_SCALE = 32.0
PAD = 8
F32 = jnp.float32
BF16 = jnp.bfloat16
VMEM_BUDGET = 24 * 1024 * 1024


def split(a):
    high = a.astype(BF16)
    return high, (a - high.astype(F32)).astype(BF16)


def dot(a, b):
    return jnp.dot(a, b, preferred_element_type=F32)


def dot_nt(a, b):
    return lax.dot_general(a, b, (((1,), (1,)), ((), ())), preferred_element_type=F32)


def mm3(left, right, op=dot):
    (lh, ll), (rh, rl) = left, right
    return op(lh, rh) + (op(lh, rl) + op(ll, rh))


def sincos(phase):
    h = 0.5 * phase
    u = h * h
    s = 1.0 / 6227020800.0
    for coef in (-1.0 / 39916800.0, 1.0 / 362880.0, -1.0 / 5040.0, 1.0 / 120.0, -1.0 / 6.0, 1.0):
        s = s * u + coef
    s = s * h
    c = 1.0 / 479001600.0
    for coef in (-1.0 / 3628800.0, 1.0 / 40320.0, -1.0 / 720.0, 1.0 / 24.0, -0.5, 1.0):
        c = c * u + coef
    two_s = s + s
    return two_s * c, 1.0 - two_s * s


def block_of(src, side, steps, half):
    same = half - 1 - steps
    other = half + steps
    low = src < half
    return jnp.where(low, same if side == 0 else other, other if side == 0 else same)


def fetch_kernel(mask, goal, bands, weight, phase, message, held, bands_in, weight_in, sems):
    rows = mask.shape[1]
    per_device, _, freqs = bands.shape
    message[2 * rows :] = jnp.zeros_like(message[2 * rows :])
    copies = [
        pltpu.make_async_copy(source, target, sems.at[n])
        for n, (source, target) in enumerate(
            (
                (mask.at[0], message.at[pl.ds(0, rows)]),
                (goal.at[0], message.at[pl.ds(rows, rows)]),
                (bands, bands_in),
                (weight, weight_in),
                (phase, held),
            )
        )
    ]
    for copy in copies:
        copy.start()
    for copy in copies:
        copy.wait()
    for i in range(per_device):
        for n in range(2):
            message[2 * rows + i : 2 * rows + i + 1, n * freqs : (n + 1) * freqs] = bands_in[
                i, n : n + 1, :
            ].astype(F32)
    line = 2 * rows + per_device
    message[line : line + 1, :per_device] = weight_in[...]


def tables_kernel(fwd_h, fwd_l, adj_h, adj_l):
    freqs, pixels = fwd_h.shape[0] // 2, fwd_h.shape[1] // 2

    def waves(shape, freq_dim):
        freq = lax.broadcasted_iota(jnp.int32, shape, freq_dim) - freqs // 2
        turn = freq * lax.broadcasted_iota(jnp.int32, shape, 1 - freq_dim)
        turn = ((turn + pixels // 2) & (pixels - 1)) - pixels // 2
        sin, cos = sincos((2.0 * math.pi / pixels) * turn.astype(F32))
        return split(cos), split(sin)

    (cos_h, cos_l), (sin_h, sin_l) = waves((freqs, pixels), 0)
    for table, cos, sin in ((fwd_h, cos_h, sin_h), (fwd_l, cos_l, sin_l)):
        table[:freqs, :pixels] = cos
        table[:freqs, pixels:] = sin
        table[freqs:, :pixels] = -sin
        table[freqs:, pixels:] = cos
    (cos_h, cos_l), (sin_h, sin_l) = waves((pixels, freqs), 1)
    for table, cos, sin in ((adj_h, cos_h, sin_h), (adj_l, cos_l, sin_l)):
        table[:pixels, :freqs] = cos
        table[:pixels, freqs:] = -sin
        table[pixels:, :freqs] = sin
        table[pixels:, freqs:] = cos


def spectrum_kernel(half, order, *refs):
    blocks = [refs[order.index(d)] for d in range(2 * half)]
    fwd_h, fwd_l, adj_h, adj_l, spec, goal, meta, part = refs[2 * half :]
    rows, pixels = goal.shape[1], goal.shape[2]
    freqs = spec.shape[1]
    src, row = lax.axis_index("src"), lax.axis_index("row")
    own = jnp.concatenate([b[:rows] for b in blocks], axis=0)
    waves = mm3(split(own), (adj_h[:pixels], adj_l[:pixels]))
    part[...] = jnp.zeros_like(part)
    for d in range(2 * half):
        block = block_of(src, d // half, d % half, half)
        start = pl.multiple_of((block * 2 + row) * rows, rows)
        mine = waves[d * rows : (d + 1) * rows]
        part[pl.ds(start, rows), :] = mine[:, :freqs]
        part[pl.ds(pl.multiple_of(pixels + start, rows), rows), :] = mine[:, freqs:]
        goal[block] = blocks[d][rows : 2 * rows]
    for j in range(half):
        meta[j] = jnp.where(row == 0, blocks[j][2 * rows :], blocks[half + j][2 * rows :])
    spec[...] = mm3((fwd_h[...], fwd_l[...]), split(part[...]))


def weight_of(meta, source, per_device):
    j, i = divmod(source, per_device)
    return meta[j][per_device : per_device + 1, i : i + 1]


def fields_kernel(per_device, sources, first_row, slots, *refs):
    row = lax.axis_index("row")
    if first_row == 0:
        phase_own, *phases = refs[: slots + 1]
        spec_a, spec_b, meta, goal, fwd_h, fwd_l, adj_h, adj_l = refs[slots + 1 : -7]
        field, intensity, pupil, amp_h, amp_l, half_h, half_l = refs[-7:]
    else:
        meta, goal, amp_h, amp_l, fwd_h, fwd_l, adj_h, adj_l, field, intensity, *half_refs = refs
        half_h, half_l = half_refs
    rows, pixels = field.shape[1], intensity.shape[1]
    count, freqs = field.shape[0], amp_h.shape[1] // field.shape[0]
    if first_row == 0:
        spec = (spec_a[...] + spec_b[...]) * (1.0 / (pixels * freqs))
        spec_r, spec_i = spec[:freqs], spec[freqs:]
        column = lax.broadcasted_iota(jnp.int32, (freqs, freqs), 1).astype(F32)
        bounds = [meta[j].T for j in range(slots)]

    def amplitude(s):
        j, i = divmod(s, per_device)
        inside = (column >= bounds[j][:freqs, i : i + 1]) & (
            column < bounds[j][freqs : 2 * freqs, i : i + 1]
        )
        phase = phases[j][i]
        if j == 0:
            phase = jnp.where(row == 0, phase_own[i], phase)
        sin_p, cos_p = sincos(phase)
        pass_r = jnp.where(inside, cos_p, 0.0)
        pass_i = jnp.where(inside, sin_p, 0.0)
        pupil[s, :freqs] = pass_r
        pupil[s, freqs:] = pass_i
        lanes = slice(s * freqs, (s + 1) * freqs)
        for half, value in enumerate(
            (pass_r * spec_r - pass_i * spec_i, pass_i * spec_r + pass_r * spec_i)
        ):
            high, low = split(value)
            amp_h[half * freqs : (half + 1) * freqs, lanes] = high
            amp_l[half * freqs : (half + 1) * freqs, lanes] = low

    here, there = (slice(n, n + rows) for n in (first_row, pixels + first_row))
    waves = [jnp.concatenate([t[here], t[there]], axis=0) for t in (adj_h, adj_l)]
    for first in range(0, count, 2):
        members = range(first, min(first + 2, count))
        if first_row == 0:
            for s in members:
                amplitude(s)
        lanes = slice(first * freqs, (members[-1] + 1) * freqs)
        half = mm3(waves, (amp_h[:, lanes], amp_l[:, lanes]))
        for n, s in enumerate(members):
            for m in range(2):
                high, low = split(half[m * rows : (m + 1) * rows, n * freqs : (n + 1) * freqs])
                half_h[s * rows : (s + 1) * rows, m * freqs : (m + 1) * freqs] = high
                half_l[s * rows : (s + 1) * rows, m * freqs : (m + 1) * freqs] = low
    out = mm3((half_h[...], half_l[...]), (fwd_h[...], fwd_l[...]))
    total = jnp.zeros((rows, pixels), F32)
    for s in range(count):
        value = out[s * rows : (s + 1) * rows]
        field[s] = value
        out_r, out_i = value[:, :pixels], value[:, pixels:]
        weight = weight_of(meta, s, per_device) * (1.0 / sources)
        total = total + weight * (out_r * out_r + out_i * out_i)
    intensity[:rows] = total
    block = goal.shape[1]
    for n in range(rows // (2 * block)):
        place = rows + n * block
        intensity[place : place + block] = goal[first_row // (2 * block) + n]


def adjoint_kernel(per_device, sources, first_row, block, *refs):
    *before, field, pupil, light_a, light_b, meta = refs[:-8]
    fwd_h, fwd_l, adj_h, adj_l, grad, cot_ref, back_h, back_l = refs[-8:]
    rows, pixels = cot_ref.shape
    count, freqs = field.shape[0], grad.shape[1]
    row = lax.axis_index("row")
    for n in range(rows // block):
        here = slice(n * block, (n + 1) * block)
        place = slice(rows + n // 2 * block, rows + (n // 2 + 1) * block)
        goal = jnp.where(row == n % 2, light_a[place], light_b[place])
        intensity = light_a[here] + light_b[here]
        resist = 1.0 / (1.0 + jnp.exp(-STEEPNESS * (intensity - THRESHOLD)))
        cot_ref[here] = (LOSS_SCALE * STEEPNESS) * (resist - goal) * resist * (1.0 - resist)
    cot = cot_ref[...]
    line = lax.broadcasted_iota(jnp.int32, (PAD, freqs), 0)
    lane = lax.broadcasted_iota(jnp.int32, (PAD, freqs), 1)
    terms = jnp.zeros((PAD, freqs), F32)
    for s in range(count):
        value = field[s]
        back_r, back_i = cot * value[:, :pixels], cot * value[:, pixels:]
        power = back_r * value[:, :pixels] + back_i * value[:, pixels:]
        power = jnp.sum(jnp.sum(power, axis=0, keepdims=True), axis=1, keepdims=True)
        j, i = divmod(s, per_device)
        terms = terms + jnp.where((lane == i) & (line == j), power, 0.0)
        back = jnp.concatenate([back_r, back_i], axis=1)
        half = mm3(split(back), (adj_h[...], adj_l[...]))
        lanes = slice(s * freqs, (s + 1) * freqs)
        for n in range(2):
            high, low = split(half[:, n * freqs : (n + 1) * freqs])
            back_h[n * rows : (n + 1) * rows, lanes] = high
            back_l[n * rows : (n + 1) * rows, lanes] = low
    grad_r = jnp.zeros((freqs, freqs), F32)
    grad_i = jnp.zeros((freqs, freqs), F32)
    here, there = (slice(n, n + rows) for n in (first_row, pixels + first_row))
    waves = [jnp.concatenate([t[:, here], t[:, there]], axis=1) for t in (fwd_h, fwd_l)]
    for first in range(0, count, 2):
        members = range(first, min(first + 2, count))
        lanes = slice(first * freqs, (members[-1] + 1) * freqs)
        out = mm3(waves, (back_h[:, lanes], back_l[:, lanes]))
        for n, s in enumerate(members):
            lanes = slice(n * freqs, (n + 1) * freqs)
            weight = weight_of(meta, s, per_device) * (2.0 / (sources * pixels * freqs))
            pass_r, pass_i = weight * pupil[s, :freqs], weight * pupil[s, freqs:]
            out_r, out_i = out[:freqs, lanes], out[freqs:, lanes]
            grad_r = grad_r + (pass_r * out_r + pass_i * out_i)
            grad_i = grad_i + (pass_r * out_i - pass_i * out_r)
    for place, value in (
        (slice(0, freqs), grad_r),
        (slice(freqs, 2 * freqs), grad_i),
        (slice(2 * freqs, 2 * freqs + PAD), terms),
    ):
        grad[place] = value + before[0][place] if before else value


def window_kernel(half, grad_a, grad_b, fwd_h, fwd_l, adj_h, adj_l, *outs):
    bodies, edges = outs[:half], outs[half:]
    rows, pixels = bodies[0].shape[0] - PAD, bodies[0].shape[1]
    freqs = grad_a.shape[1]
    src, row, tile = lax.axis_index("src"), lax.axis_index("row"), lax.axis_index("tile")
    total = grad_a[: 2 * freqs] + grad_b[: 2 * freqs]
    flat = split(jnp.concatenate([total[:freqs], total[freqs:]], axis=1))
    waves = mm3(flat, (fwd_h[...], fwd_l[...]))
    waves = jnp.concatenate([waves[:, :pixels], waves[:, pixels:]], axis=0)
    tables = []
    for table in (adj_h, adj_l):
        parts = []
        for steps in range(half):
            start = (block_of(src, 0, steps, half) * 2 + row) * rows
            parts.append(table[pl.ds(pl.multiple_of(start, rows), rows), :])
        tables.append(jnp.concatenate(parts, axis=0))
    window = mm3(tables, split(waves))
    terms = jnp.where(row == 0, grad_a[2 * freqs :], grad_b[2 * freqs :])
    for steps in range(half):
        block = window[steps * rows : (steps + 1) * rows]
        term = terms[steps : steps + 1]
        bodies[steps][:rows] = block
        bodies[steps][rows : rows + 1, :freqs] = term
        edge = jnp.where(tile == 0, block[:, pixels - OV :], block[:, :OV])
        edges[steps][:rows, :OV] = edge
        edges[steps][rows : rows + 1, :] = term


def last_order(half):
    far = range(1, half)
    return [("body", n) for n in far] + [("edge", n) for n in far] + [("edge", 0)]


def place_kernel(half, term_scale, *refs):
    own, *moved = refs[: 2 * half]
    moved = dict(zip(last_order(half), moved))
    bodies = [own] + [moved["body", n] for n in range(1, half)]
    edges = [moved["edge", n] for n in range(half)]
    out, source = refs[2 * half :]
    rows, pixels = out.shape[1:]
    per_device = source.shape[1]
    src, tile = lax.axis_index("src"), lax.axis_index("tile")
    steps = jnp.where(src < half, half - 1 - src, src - half)

    def mine(refs, *index):
        value = refs[0][index]
        for n in range(1, half):
            value = jnp.where(steps == n, refs[n][index], value)
        return value

    body = mine(bodies, slice(0, rows), slice(None))
    edge = mine(edges, slice(0, rows), slice(0, OV))
    zero = jnp.zeros_like(edge)
    middle = jnp.zeros((rows, pixels - 2 * OV), F32)
    low, high = jnp.where(tile == 1, edge, zero), jnp.where(tile == 0, edge, zero)
    out[0] = body + jnp.concatenate([low, middle, high], axis=1)
    term = slice(rows, rows + 1), slice(0, per_device)
    source[...] = (mine(bodies, *term) + mine(edges, *term)) * term_scale


def call(kernel, outs, scratch=(), kind=F32, hbm=False):
    kinds = kind if isinstance(kind, list) else [kind] * len(outs)
    held = {"in_specs": [pl.BlockSpec(memory_space=pltpu.HBM)] * 5} if hbm else {}
    return pl.pallas_call(
        kernel,
        out_shape=[jax.ShapeDtypeStruct(o, k) for o, k in zip(outs, kinds)],
        out_specs=[pl.BlockSpec(memory_space=pltpu.VMEM) for _ in outs],
        scratch_shapes=list(scratch),
        compiler_params=pltpu.CompilerParams(vmem_limit_bytes=VMEM_BUDGET),
        **held,
    )


def permute(x, wanted):
    shape = tuple(lax.axis_size(a) for a in ("src", "tile", "row"))
    devices = list(itertools.product(*(range(n) for n in shape)))
    pairs = dict(wanted)
    sources = [d for d in devices if d not in pairs]
    targets = [d for d in devices if d not in pairs.values()]

    def cost(pair):
        source, target = pair
        hops = abs(source[0] - target[0]) + abs(source[1] - target[1])
        return (source == target, hops, source, target)

    for source, target in sorted(itertools.product(sources, targets), key=cost):
        if source not in pairs and target not in pairs.values():
            pairs[source] = target
    flat = {d: n for n, d in enumerate(devices)}
    return lax.ppermute(x, ("src", "tile", "row"), [(flat[a], flat[b]) for a, b in pairs.items()])


def swap_rows(x):
    return lax.ppermute(x, "row", [(0, 1), (1, 0)])


def hub_shards(mask_windows, target_windows, pupil_bands, pupil_phase, source_weight):
    src_count, tile_count = lax.axis_size("src"), lax.axis_size("tile")
    rows, pixels = mask_windows.shape[1:]
    per_device, freqs = pupil_phase.shape[:2]
    sources = per_device * src_count
    half = src_count // 2
    count = half * per_device

    def chip(low, steps):
        return half - 1 - steps if low else half + steps

    cores = list(itertools.product(range(tile_count), range(2)))
    halves = (True, False)

    def to_hub(x, side, steps):
        return permute(
            x,
            {
                (chip(low, steps), t, c): (chip(low != (side == 1), 0), t, c)
                for low in halves
                for t, c in cores
            },
        )

    def phases_to_hub(x, steps):
        pairs = {}
        for low, tile in itertools.product(halves, range(tile_count)):
            if steps:
                pairs[chip(low, steps), tile, 0] = chip(low, 0), tile, 0
            pairs[chip(low, steps), tile, 1 if steps else 0] = chip(not low, 0), tile, 1
        return permute(x, pairs)

    pin = functools.partial(pltpu.with_memory_space_constraint, memory_space=pltpu.HBM)
    message, phase = call(
        fetch_kernel,
        [(2 * rows + PAD, pixels), pupil_phase.shape],
        [
            pltpu.VMEM((per_device, 2, freqs), jnp.int32),
            pltpu.VMEM((1, per_device), F32),
            pltpu.SemaphoreType.DMA((5,)),
        ],
        hbm=True,
    )(
        pin(mask_windows),
        pin(target_windows),
        pin(pupil_bands.transpose(0, 2, 1)),
        pin(source_weight.reshape(1, per_device)),
        pin(pupil_phase),
    )
    order = (0, *(2, 1, 3))
    blocks = [message] + [to_hub(message, d // half, d % half) for d in order[1:]]
    phases = [phases_to_hub(phase, n) for n in reversed(range(half))][::-1]
    tables = call(
        tables_kernel, [(2 * freqs, 2 * pixels)] * 2 + [(2 * pixels, 2 * freqs)] * 2, kind=BF16
    )()

    spec, goal, meta = call(
        functools.partial(spectrum_kernel, half, order),
        [(2 * freqs, freqs), (src_count, rows, pixels), (half, PAD, pixels)],
        [pltpu.VMEM((2 * pixels, freqs), F32)],
    )(*blocks, *tables)
    spec_other = swap_rows(spec)

    shape = (2 * freqs, count * freqs)
    part = pixels // 2
    outs = [(count, part, 2 * pixels), (part + part // 2, pixels)]
    *first, pupil, amp_h, amp_l = call(
        functools.partial(fields_kernel, per_device, sources, 0, half),
        [*outs, (count, 2 * freqs, freqs), shape, shape],
        [pltpu.VMEM((count * part, 2 * freqs), BF16)] * 2,
        kind=[F32, F32, F32, BF16, BF16],
    )(phase, *phases, spec, spec_other, meta, goal, *tables)
    second = call(
        functools.partial(fields_kernel, per_device, sources, part, half),
        outs,
        [pltpu.VMEM((count * part, 2 * freqs), BF16)] * 2,
    )(meta, goal, amp_h, amp_l, *tables)
    fields = [first, second]
    others = [swap_rows(light) for _, light in fields]
    grad = []
    for first_row, (field, light), other in zip((0, part), fields, others):
        grad = call(
            functools.partial(adjoint_kernel, per_device, sources, first_row, rows),
            [(2 * freqs + PAD, freqs)],
            [pltpu.VMEM((part, pixels), F32)]
            + [pltpu.VMEM((2 * part, count * freqs), BF16)] * 2,
        )(*grad, field, pupil, light, other, meta, *tables)
    (grad,) = grad
    grad_other = swap_rows(grad)

    outs = call(
        functools.partial(window_kernel, half),
        [(rows + PAD, pixels)] * half + [(rows + PAD, freqs)] * half,
    )(grad, grad_other, *tables)
    bodies, edges = outs[:half], outs[half:]

    def from_hub(x, steps, flip):
        return permute(
            x,
            {
                (chip(low, 0), t, c): (chip(low, steps), 1 - t if flip else t, c)
                for low in halves
                for t, c in cores
            },
        )

    bodies = [bodies[0]] + [from_hub(bodies[n], n, False) for n in range(1, half)]
    edges = [from_hub(edges[n], n, True) for n in range(half)]
    out, source = call(
        functools.partial(place_kernel, half, 1.0 / (sources * pixels * tile_count)),
        [(1, rows, pixels), (1, per_device)],
    )(bodies[0], *[dict(body=bodies, edge=edges)[k][n] for k, n in last_order(half)])
    return out, source[0]


M = 256
K = 128


def with_halo(block, sides, width):
    for axis, dim in sides:
        count = lax.axis_size(axis)
        forward = [(i, i + 1) for i in range(count - 1)]
        backward = [(target, source) for source, target in forward]
        low = lax.ppermute(
            lax.slice_in_dim(block, block.shape[dim] - width, None, axis=dim), axis, forward
        )
        high = lax.ppermute(lax.slice_in_dim(block, 0, width, axis=dim), axis, backward)
        block = jnp.concatenate([low, block, high], axis=dim)
    return block


def matmul(left_op, right_op):
    return lax.dot_general(
        left_op,
        right_op,
        (((1,), (0,)), ((), ())),
        precision=lax.Precision.HIGHEST,
        preferred_element_type=jnp.float32,
    )


def matmul_tn(left_op, right_op):
    return lax.dot_general(
        left_op,
        right_op,
        (((0,), (0,)), ((), ())),
        precision=lax.Precision.HIGHEST,
        preferred_element_type=jnp.float32,
    )


def matmul_nt(left_op, right_op):
    return lax.dot_general(
        left_op,
        right_op,
        (((1,), (1,)), ((), ())),
        precision=lax.Precision.HIGHEST,
        preferred_element_type=jnp.float32,
    )


def wave_tables(positions):
    freq_index = jnp.arange(K, dtype=jnp.int32) - K // 2
    phase_index = freq_index[:, None] * positions[None, :] % M
    angles = 2.0 * math.pi / M * phase_index.astype(jnp.float32)
    return (jnp.cos(angles), jnp.sin(angles))


def shards(mask_windows, target_windows, pupil_bands, pupil_phase, source_weight):
    src_count = lax.axis_size("src")
    tile_count = lax.axis_size("tile")
    row_count = lax.axis_size("row")
    local_x = mask_windows.shape[1]
    per_device = pupil_phase.shape[0]
    sources = per_device * src_count
    field_scale = 1.0 / (M * K)
    src_id = lax.axis_index("src")
    row_id = lax.axis_index("row")
    x_start = (src_id * row_count + row_id) * local_x
    block_starts = (jnp.arange(src_count, dtype=jnp.int32) * row_count + row_id) * local_x
    row_set = (block_starts[:, None] + jnp.arange(local_x, dtype=jnp.int32)[None, :]).reshape(
        src_count * local_x
    )
    cos_all, sin_all = wave_tables(jnp.arange(M, dtype=jnp.int32))
    cos_set, sin_set = wave_tables(row_set)
    cos_own, sin_own = wave_tables(x_start + jnp.arange(local_x, dtype=jnp.int32))
    window = mask_windows[0]
    goal_block = target_windows[0]
    zero_spec = jnp.zeros((K, K), jnp.float32)
    shard_rows = lax.all_gather(window, ("src", "row"), axis=0, tiled=True)
    part_real = matmul_nt(shard_rows, cos_all)
    part_imag = -matmul_nt(shard_rows, sin_all)
    spec_real = matmul(cos_all, part_real) + matmul(sin_all, part_imag)
    spec_imag = matmul(cos_all, part_imag) - matmul(sin_all, part_real)
    freq_cols = jnp.arange(K, dtype=jnp.int32)
    inside = (freq_cols[None, None, :] >= pupil_bands[:, :, 0:1]) & (
        freq_cols[None, None, :] < pupil_bands[:, :, 1:2]
    )
    passing = inside.astype(jnp.float32)
    pupil_real = passing * jnp.cos(pupil_phase)
    pupil_imag = passing * jnp.sin(pupil_phase)
    amp_real = (pupil_real * spec_real - pupil_imag * spec_imag).reshape(per_device * K, K)
    amp_imag = (pupil_imag * spec_real + pupil_real * spec_imag).reshape(per_device * K, K)
    half_real = (matmul(amp_real, cos_all) - matmul(amp_imag, sin_all)).reshape(per_device, K, M)
    half_imag = (matmul(amp_real, sin_all) + matmul(amp_imag, cos_all)).reshape(per_device, K, M)
    weights = source_weight / sources

    def fields(pair_in):
        one_real, one_imag = pair_in
        field_real = field_scale * (matmul_tn(cos_set, one_real) - matmul_tn(sin_set, one_imag))
        field_imag = field_scale * (matmul_tn(cos_set, one_imag) + matmul_tn(sin_set, one_real))
        return (field_real, field_imag)

    stack_real, stack_imag = lax.map(fields, (half_real, half_imag))
    part_real = stack_real
    part_imag = stack_imag
    intensity = lax.psum_scatter(
        jnp.sum(weights[:, None, None] * (part_real * part_real + part_imag * part_imag), axis=0),
        "src",
        scatter_dimension=0,
        tiled=True,
    )
    resist = jax.nn.sigmoid(STEEPNESS * (intensity - THRESHOLD))
    cotangent = LOSS_SCALE * (resist - goal_block) * STEEPNESS * resist * (1.0 - resist)
    cotangent_all = lax.all_gather(cotangent, "src", axis=0, tiled=True)
    source_ids = jnp.arange(per_device, dtype=jnp.int32)

    def add_back(source_id, totals):
        grad_real, grad_imag, source_terms = totals
        field_real = stack_real[source_id]
        field_imag = stack_imag[source_id]
        back_scale = 2.0 * weights[source_id] * cotangent_all
        back_real = back_scale * field_real
        back_imag = back_scale * field_imag
        adj_real = matmul(cos_set, back_real) + matmul(sin_set, back_imag)
        adj_imag = matmul(cos_set, back_imag) - matmul(sin_set, back_real)
        amp_grad_real = field_scale * (matmul_nt(adj_real, cos_all) + matmul_nt(adj_imag, sin_all))
        amp_grad_imag = field_scale * (matmul_nt(adj_imag, cos_all) - matmul_nt(adj_real, sin_all))
        pass_real = pupil_real[source_id]
        pass_imag = pupil_imag[source_id]
        grad_real = grad_real + pass_real * amp_grad_real + pass_imag * amp_grad_imag
        grad_imag = grad_imag + pass_real * amp_grad_imag - pass_imag * amp_grad_real
        term_value = jnp.sum(cotangent_all * (field_real * field_real + field_imag * field_imag))
        source_terms = source_terms + jnp.where(source_ids == source_id, term_value, 0.0)
        return (grad_real, grad_imag, source_terms)

    grad_real, grad_imag, source_terms = lax.fori_loop(
        0, per_device, add_back, (zero_spec, zero_spec, jnp.zeros((per_device,), jnp.float32))
    )
    grad_real, grad_imag = lax.psum((grad_real, grad_imag), ("src", "row"))
    source_sum = lax.psum(source_terms, ("tile", "row"))
    source_grad = source_sum / (sources * M * tile_count)
    q_one = matmul(grad_real, cos_all) - matmul(grad_imag, sin_all)
    q_two = matmul(grad_real, sin_all) + matmul(grad_imag, cos_all)
    grad_block = matmul_tn(cos_own, q_one) - matmul_tn(sin_own, q_two)
    padded = with_halo(grad_block, (("tile", 1),), OV)
    from_below = padded[:, :OV]
    from_above = padded[:, M + OV :]
    middle = jnp.zeros((local_x, M - 2 * OV), jnp.float32)
    grad_block = grad_block + jnp.concatenate([from_below, middle, from_above], axis=1)
    return (grad_block[None], source_grad)


def hubs_serve(mesh, mask_windows, pupil_phase):
    src_count = mesh.shape["src"]
    pixels = mask_windows.shape[2]
    sources, freqs = pupil_phase.shape[0] // mesh.shape["parts"], pupil_phase.shape[1]
    per_device = sources // src_count
    held = sources // 2 * (2 * pixels * pixels + 4 * freqs * freqs) * 4
    return (
        mesh.shape["row"] == 2
        and mesh.shape["tile"] == 2
        and src_count % 2 == 0
        and src_count // 2 <= PAD
        and per_device < PAD
        and mask_windows.shape[1] // (2 * src_count) % 16 == 0
        and pixels & (pixels - 1) == 0
        and pixels >= 2 * freqs
        and held <= VMEM_BUDGET // 2
    )


def solution(mesh):
    def run(mask_windows, target_windows, pupil_bands, pupil_phase, source_weight):
        hubs = hubs_serve(mesh, mask_windows, pupil_phase)
        return jax.shard_map(
            hub_shards if hubs else shards,
            mesh=mesh,
            in_specs=(
                P(("parts", "tile"), ("src", "row"), None),
                P(("parts", "tile"), ("src", "row"), None),
                P(("parts", "src"), None, None),
                P(("parts", "src"), None, None),
                P(("parts", "src")),
            ),
            out_specs=(P(("parts", "tile"), ("src", "row"), None), P(("parts", "src"))),
            check_vma=False,
        )(mask_windows, target_windows, pupil_bands, pupil_phase, source_weight)

    return run
```

```python
import functools
import itertools
import math

import jax
import jax.numpy as jnp
from jax import lax
from jax.experimental import pallas as pl
from jax.experimental.pallas import tpu as pltpu
from jax.sharding import PartitionSpec as P

OV = 32
STEEPNESS = 20.0
THRESHOLD = 0.15
LOSS_SCALE = 32.0
PAD = 8
F32 = jnp.float32
BF16 = jnp.bfloat16
VMEM_BUDGET = 24 * 1024 * 1024


def split(a):
    high = a.astype(BF16)
    return high, (a - high.astype(F32)).astype(BF16)


def dot(a, b):
    return jnp.dot(a, b, preferred_element_type=F32)


def dot_nt(a, b):
    return lax.dot_general(a, b, (((1,), (1,)), ((), ())), preferred_element_type=F32)


def mm3(left, right, op=dot):
    (lh, ll), (rh, rl) = left, right
    return op(lh, rh) + (op(lh, rl) + op(ll, rh))


def sincos(phase):
    h = 0.5 * phase
    u = h * h
    s = 1.0 / 6227020800.0
    for coef in (-1.0 / 39916800.0, 1.0 / 362880.0, -1.0 / 5040.0, 1.0 / 120.0, -1.0 / 6.0, 1.0):
        s = s * u + coef
    s = s * h
    c = 1.0 / 479001600.0
    for coef in (-1.0 / 3628800.0, 1.0 / 40320.0, -1.0 / 720.0, 1.0 / 24.0, -0.5, 1.0):
        c = c * u + coef
    two_s = s + s
    return two_s * c, 1.0 - two_s * s


def block_of(src, side, steps, half):
    same = half - 1 - steps
    other = half + steps
    low = src < half
    return jnp.where(low, same if side == 0 else other, other if side == 0 else same)


def fetch_kernel(mask, goal, bands, weight, message, bands_in, weight_in, sems):
    rows = mask.shape[1]
    per_device, _, freqs = bands.shape
    message[2 * rows :] = jnp.zeros_like(message[2 * rows :])
    copies = [
        pltpu.make_async_copy(source, target, sems.at[n])
        for n, (source, target) in enumerate(
            (
                (mask.at[0], message.at[pl.ds(0, rows)]),
                (goal.at[0], message.at[pl.ds(rows, rows)]),
                (bands, bands_in),
                (weight, weight_in),
            )
        )
    ]
    for copy in copies:
        copy.start()
    for copy in copies:
        copy.wait()
    for i in range(per_device):
        for n in range(2):
            message[2 * rows + i : 2 * rows + i + 1, n * freqs : (n + 1) * freqs] = bands_in[
                i, n : n + 1, :
            ].astype(F32)
    line = 2 * rows + per_device
    message[line : line + 1, :per_device] = weight_in[...]


def tables_kernel(phase, fwd_h, fwd_l, adj_h, adj_l, held, sem):
    copy = pltpu.make_async_copy(phase, held, sem)
    copy.start()
    freqs, pixels = fwd_h.shape[0] // 2, fwd_h.shape[1] // 2

    def waves(shape, freq_dim):
        freq = lax.broadcasted_iota(jnp.int32, shape, freq_dim) - freqs // 2
        turn = freq * lax.broadcasted_iota(jnp.int32, shape, 1 - freq_dim)
        turn = ((turn + pixels // 2) & (pixels - 1)) - pixels // 2
        sin, cos = sincos((2.0 * math.pi / pixels) * turn.astype(F32))
        return split(cos), split(sin)

    (cos_h, cos_l), (sin_h, sin_l) = waves((freqs, pixels), 0)
    for table, cos, sin in ((fwd_h, cos_h, sin_h), (fwd_l, cos_l, sin_l)):
        table[:freqs, :pixels] = cos
        table[:freqs, pixels:] = sin
        table[freqs:, :pixels] = -sin
        table[freqs:, pixels:] = cos
    (cos_h, cos_l), (sin_h, sin_l) = waves((pixels, freqs), 1)
    for table, cos, sin in ((adj_h, cos_h, sin_h), (adj_l, cos_l, sin_l)):
        table[:pixels, :freqs] = cos
        table[:pixels, freqs:] = -sin
        table[pixels:, :freqs] = sin
        table[pixels:, freqs:] = cos
    copy.wait()


def spectrum_kernel(half, order, *refs):
    blocks = [refs[order.index(d)] for d in range(2 * half)]
    fwd_h, fwd_l, adj_h, adj_l, spec, goal, meta, part = refs[2 * half :]
    rows, pixels = goal.shape[1], goal.shape[2]
    freqs = spec.shape[1]
    src, row = lax.axis_index("src"), lax.axis_index("row")
    own = jnp.concatenate([b[:rows] for b in blocks], axis=0)
    waves = mm3(split(own), (adj_h[:pixels], adj_l[:pixels]))
    part[...] = jnp.zeros_like(part)
    for d in range(2 * half):
        block = block_of(src, d // half, d % half, half)
        start = pl.multiple_of((block * 2 + row) * rows, rows)
        mine = waves[d * rows : (d + 1) * rows]
        part[pl.ds(start, rows), :] = mine[:, :freqs]
        part[pl.ds(pl.multiple_of(pixels + start, rows), rows), :] = mine[:, freqs:]
        goal[block] = blocks[d][rows : 2 * rows]
    for j in range(half):
        meta[j] = jnp.where(row == 0, blocks[j][2 * rows :], blocks[half + j][2 * rows :])
    spec[...] = mm3((fwd_h[...], fwd_l[...]), split(part[...]))


def weight_of(meta, source, per_device):
    j, i = divmod(source, per_device)
    return meta[j][per_device : per_device + 1, i : i + 1]


def fields_kernel(per_device, sources, first_row, slots, *refs):
    row = lax.axis_index("row")
    if first_row == 0:
        phase_own, *phases = refs[: slots + 1]
        spec_a, spec_b, meta, goal, fwd_h, fwd_l, adj_h, adj_l = refs[slots + 1 : -7]
        field, intensity, pupil, amp_h, amp_l, half_h, half_l = refs[-7:]
    else:
        meta, goal, amp_h, amp_l, fwd_h, fwd_l, adj_h, adj_l, field, intensity, *half_refs = refs
        half_h, half_l = half_refs
    rows, pixels = field.shape[1], intensity.shape[1]
    count, freqs = field.shape[0], amp_h.shape[1] // field.shape[0]
    if first_row == 0:
        spec = (spec_a[...] + spec_b[...]) * (1.0 / (pixels * freqs))
        spec_r, spec_i = spec[:freqs], spec[freqs:]
        column = lax.broadcasted_iota(jnp.int32, (freqs, freqs), 1).astype(F32)
        bounds = [meta[j].T for j in range(slots)]

    def amplitude(s):
        j, i = divmod(s, per_device)
        inside = (column >= bounds[j][:freqs, i : i + 1]) & (
            column < bounds[j][freqs : 2 * freqs, i : i + 1]
        )
        phase = phases[j][i]
        if j == 0:
            phase = jnp.where(row == 0, phase_own[i], phase)
        sin_p, cos_p = sincos(phase)
        pass_r = jnp.where(inside, cos_p, 0.0)
        pass_i = jnp.where(inside, sin_p, 0.0)
        pupil[s, :freqs] = pass_r
        pupil[s, freqs:] = pass_i
        lanes = slice(s * freqs, (s + 1) * freqs)
        for half, value in enumerate(
            (pass_r * spec_r - pass_i * spec_i, pass_i * spec_r + pass_r * spec_i)
        ):
            high, low = split(value)
            amp_h[half * freqs : (half + 1) * freqs, lanes] = high
            amp_l[half * freqs : (half + 1) * freqs, lanes] = low

    here, there = (slice(n, n + rows) for n in (first_row, pixels + first_row))
    waves = [jnp.concatenate([t[here], t[there]], axis=0) for t in (adj_h, adj_l)]
    for first in range(0, count, 2):
        members = range(first, min(first + 2, count))
        if first_row == 0:
            for s in members:
                amplitude(s)
        lanes = slice(first * freqs, (members[-1] + 1) * freqs)
        half = mm3(waves, (amp_h[:, lanes], amp_l[:, lanes]))
        for n, s in enumerate(members):
            for m in range(2):
                high, low = split(half[m * rows : (m + 1) * rows, n * freqs : (n + 1) * freqs])
                half_h[s * rows : (s + 1) * rows, m * freqs : (m + 1) * freqs] = high
                half_l[s * rows : (s + 1) * rows, m * freqs : (m + 1) * freqs] = low
    out = mm3((half_h[...], half_l[...]), (fwd_h[...], fwd_l[...]))
    total = jnp.zeros((rows, pixels), F32)
    for s in range(count):
        value = out[s * rows : (s + 1) * rows]
        field[s] = value
        out_r, out_i = value[:, :pixels], value[:, pixels:]
        weight = weight_of(meta, s, per_device) * (1.0 / sources)
        total = total + weight * (out_r * out_r + out_i * out_i)
    intensity[:rows] = total
    block = goal.shape[1]
    for n in range(rows // (2 * block)):
        place = rows + n * block
        intensity[place : place + block] = goal[first_row // (2 * block) + n]


def adjoint_kernel(per_device, sources, first_row, block, *refs):
    *before, field, pupil, light_a, light_b, meta = refs[:-8]
    fwd_h, fwd_l, adj_h, adj_l, grad, cot_ref, back_h, back_l = refs[-8:]
    rows, pixels = cot_ref.shape
    count, freqs = field.shape[0], grad.shape[1]
    row = lax.axis_index("row")
    for n in range(rows // block):
        here = slice(n * block, (n + 1) * block)
        place = slice(rows + n // 2 * block, rows + (n // 2 + 1) * block)
        goal = jnp.where(row == n % 2, light_a[place], light_b[place])
        intensity = light_a[here] + light_b[here]
        resist = 1.0 / (1.0 + jnp.exp(-STEEPNESS * (intensity - THRESHOLD)))
        cot_ref[here] = (LOSS_SCALE * STEEPNESS) * (resist - goal) * resist * (1.0 - resist)
    cot = cot_ref[...]
    line = lax.broadcasted_iota(jnp.int32, (PAD, freqs), 0)
    lane = lax.broadcasted_iota(jnp.int32, (PAD, freqs), 1)
    terms = jnp.zeros((PAD, freqs), F32)
    for s in range(count):
        value = field[s]
        back_r, back_i = cot * value[:, :pixels], cot * value[:, pixels:]
        power = back_r * value[:, :pixels] + back_i * value[:, pixels:]
        power = jnp.sum(jnp.sum(power, axis=0, keepdims=True), axis=1, keepdims=True)
        j, i = divmod(s, per_device)
        terms = terms + jnp.where((lane == i) & (line == j), power, 0.0)
        back = jnp.concatenate([back_r, back_i], axis=1)
        half = mm3(split(back), (adj_h[...], adj_l[...]))
        lanes = slice(s * freqs, (s + 1) * freqs)
        for n in range(2):
            high, low = split(half[:, n * freqs : (n + 1) * freqs])
            back_h[n * rows : (n + 1) * rows, lanes] = high
            back_l[n * rows : (n + 1) * rows, lanes] = low
    grad_r = jnp.zeros((freqs, freqs), F32)
    grad_i = jnp.zeros((freqs, freqs), F32)
    here, there = (slice(n, n + rows) for n in (first_row, pixels + first_row))
    waves = [jnp.concatenate([t[:, here], t[:, there]], axis=1) for t in (fwd_h, fwd_l)]
    for first in range(0, count, 2):
        members = range(first, min(first + 2, count))
        lanes = slice(first * freqs, (members[-1] + 1) * freqs)
        out = mm3(waves, (back_h[:, lanes], back_l[:, lanes]))
        for n, s in enumerate(members):
            lanes = slice(n * freqs, (n + 1) * freqs)
            weight = weight_of(meta, s, per_device) * (2.0 / (sources * pixels * freqs))
            pass_r, pass_i = weight * pupil[s, :freqs], weight * pupil[s, freqs:]
            out_r, out_i = out[:freqs, lanes], out[freqs:, lanes]
            grad_r = grad_r + (pass_r * out_r + pass_i * out_i)
            grad_i = grad_i + (pass_r * out_i - pass_i * out_r)
    for place, value in (
        (slice(0, freqs), grad_r),
        (slice(freqs, 2 * freqs), grad_i),
        (slice(2 * freqs, 2 * freqs + PAD), terms),
    ):
        grad[place] = value + before[0][place] if before else value


def window_kernel(half, grad_a, grad_b, fwd_h, fwd_l, adj_h, adj_l, *outs):
    bodies, edges = outs[:half], outs[half:]
    rows, pixels = bodies[0].shape[0] - PAD, bodies[0].shape[1]
    freqs = grad_a.shape[1]
    src, row, tile = lax.axis_index("src"), lax.axis_index("row"), lax.axis_index("tile")
    total = grad_a[: 2 * freqs] + grad_b[: 2 * freqs]
    flat = split(jnp.concatenate([total[:freqs], total[freqs:]], axis=1))
    waves = mm3(flat, (fwd_h[...], fwd_l[...]))
    waves = jnp.concatenate([waves[:, :pixels], waves[:, pixels:]], axis=0)
    tables = []
    for table in (adj_h, adj_l):
        parts = []
        for steps in range(half):
            core = row if steps == 0 else 1 - row
            start = (block_of(src, 0, steps, half) * 2 + core) * rows
            parts.append(table[pl.ds(pl.multiple_of(start, rows), rows), :])
        tables.append(jnp.concatenate(parts, axis=0))
    window = mm3(tables, split(waves))
    terms = jnp.where(row == 0, grad_a[2 * freqs :], grad_b[2 * freqs :])
    for steps in range(half):
        block = window[steps * rows : (steps + 1) * rows]
        term = terms[steps : steps + 1]
        bodies[steps][:rows] = block
        bodies[steps][rows : rows + 1, :freqs] = term
        edge = jnp.where(tile == 0, block[:, pixels - OV :], block[:, :OV])
        edges[steps][:rows, :OV] = edge
        edges[steps][rows : rows + 1, :] = term


def last_order(half):
    far = range(1, half)
    return [("body", n) for n in far] + [("edge", n) for n in far] + [("edge", 0)]


def place_kernel(half, term_scale, *refs):
    own, *moved = refs[: 2 * half]
    moved = dict(zip(last_order(half), moved))
    bodies = [own] + [moved["body", n] for n in range(1, half)]
    edges = [moved["edge", n] for n in range(half)]
    out, source = refs[2 * half :]
    rows, pixels = out.shape[1:]
    per_device = source.shape[1]
    src, tile = lax.axis_index("src"), lax.axis_index("tile")
    steps = jnp.where(src < half, half - 1 - src, src - half)

    def mine(refs, *index):
        value = refs[0][index]
        for n in range(1, half):
            value = jnp.where(steps == n, refs[n][index], value)
        return value

    body = mine(bodies, slice(0, rows), slice(None))
    edge = mine(edges, slice(0, rows), slice(0, OV))
    zero = jnp.zeros_like(edge)
    middle = jnp.zeros((rows, pixels - 2 * OV), F32)
    low, high = jnp.where(tile == 1, edge, zero), jnp.where(tile == 0, edge, zero)
    out[0] = body + jnp.concatenate([low, middle, high], axis=1)
    term = slice(rows, rows + 1), slice(0, per_device)
    source[...] = (mine(bodies, *term) + mine(edges, *term)) * term_scale


def call(kernel, outs, scratch=(), kind=F32, hbm=0):
    kinds = kind if isinstance(kind, list) else [kind] * len(outs)
    held = {"in_specs": [pl.BlockSpec(memory_space=pltpu.HBM)] * hbm} if hbm else {}
    return pl.pallas_call(
        kernel,
        out_shape=[jax.ShapeDtypeStruct(o, k) for o, k in zip(outs, kinds)],
        out_specs=[pl.BlockSpec(memory_space=pltpu.VMEM) for _ in outs],
        scratch_shapes=list(scratch),
        compiler_params=pltpu.CompilerParams(vmem_limit_bytes=VMEM_BUDGET),
        **held,
    )


def permute(x, wanted):
    shape = tuple(lax.axis_size(a) for a in ("src", "tile", "row"))
    devices = list(itertools.product(*(range(n) for n in shape)))
    pairs = dict(wanted)
    sources = [d for d in devices if d not in pairs]
    targets = [d for d in devices if d not in pairs.values()]

    def cost(pair):
        source, target = pair
        hops = abs(source[0] - target[0]) + abs(source[1] - target[1])
        return (source == target, hops, source, target)

    for source, target in sorted(itertools.product(sources, targets), key=cost):
        if source not in pairs and target not in pairs.values():
            pairs[source] = target
    flat = {d: n for n, d in enumerate(devices)}
    return lax.ppermute(x, ("src", "tile", "row"), [(flat[a], flat[b]) for a, b in pairs.items()])


def swap_rows(x):
    return lax.ppermute(x, "row", [(0, 1), (1, 0)])


def hub_shards(mask_windows, target_windows, pupil_bands, pupil_phase, source_weight):
    src_count, tile_count = lax.axis_size("src"), lax.axis_size("tile")
    rows, pixels = mask_windows.shape[1:]
    per_device, freqs = pupil_phase.shape[:2]
    sources = per_device * src_count
    half = src_count // 2
    count = half * per_device

    def chip(low, steps):
        return half - 1 - steps if low else half + steps

    cores = list(itertools.product(range(tile_count), range(2)))
    halves = (True, False)

    def to_hub(x, side, steps):
        return permute(
            x,
            {
                (chip(low, steps), t, c): (chip(low != (side == 1), 0), t, c)
                for low in halves
                for t, c in cores
            },
        )

    def phases_to_hub(x, steps):
        pairs = {}
        for low, tile in itertools.product(halves, range(tile_count)):
            if steps:
                pairs[chip(low, steps), tile, 0] = chip(low, 0), tile, 0
            pairs[chip(low, steps), tile, 1 if steps else 0] = chip(not low, 0), tile, 1
        return permute(x, pairs)

    pin = functools.partial(pltpu.with_memory_space_constraint, memory_space=pltpu.HBM)
    (message,) = call(
        fetch_kernel,
        [(2 * rows + PAD, pixels)],
        [
            pltpu.VMEM((per_device, 2, freqs), jnp.int32),
            pltpu.VMEM((1, per_device), F32),
            pltpu.SemaphoreType.DMA((4,)),
        ],
        hbm=4,
    )(
        pin(mask_windows),
        pin(target_windows),
        pin(pupil_bands.transpose(0, 2, 1)),
        pin(source_weight.reshape(1, per_device)),
    )
    order = (0, half, *range(1, half), *range(half + 1, 2 * half))
    blocks = [message] + [to_hub(message, d // half, d % half) for d in order[1:]]
    phases = [phases_to_hub(pupil_phase, n) for n in reversed(range(half))][::-1]
    *tables, phase = call(
        tables_kernel,
        [(2 * freqs, 2 * pixels)] * 2 + [(2 * pixels, 2 * freqs)] * 2 + [pupil_phase.shape],
        [pltpu.SemaphoreType.DMA],
        kind=[BF16] * 4 + [F32],
        hbm=1,
    )(pin(pupil_phase))

    spec, goal, meta = call(
        functools.partial(spectrum_kernel, half, order),
        [(2 * freqs, freqs), (src_count, rows, pixels), (half, PAD, pixels)],
        [pltpu.VMEM((2 * pixels, freqs), F32)],
    )(*blocks, *tables)
    spec_other = swap_rows(spec)

    shape = (2 * freqs, count * freqs)
    part = pixels // 2
    outs = [(count, part, 2 * pixels), (part + part // 2, pixels)]
    *first, pupil, amp_h, amp_l = call(
        functools.partial(fields_kernel, per_device, sources, 0, half),
        [*outs, (count, 2 * freqs, freqs), shape, shape],
        [pltpu.VMEM((count * part, 2 * freqs), BF16)] * 2,
        kind=[F32, F32, F32, BF16, BF16],
    )(phase, *phases, spec, spec_other, meta, goal, *tables)
    second = call(
        functools.partial(fields_kernel, per_device, sources, part, half),
        outs,
        [pltpu.VMEM((count * part, 2 * freqs), BF16)] * 2,
    )(meta, goal, amp_h, amp_l, *tables)
    fields = [first, second]
    others = [swap_rows(light) for _, light in fields]
    grad = []
    for first_row, (field, light), other in zip((0, part), fields, others):
        grad = call(
            functools.partial(adjoint_kernel, per_device, sources, first_row, rows),
            [(2 * freqs + PAD, freqs)],
            [pltpu.VMEM((part, pixels), F32)]
            + [pltpu.VMEM((2 * part, count * freqs), BF16)] * 2,
        )(*grad, field, pupil, light, other, meta, *tables)
    (grad,) = grad
    grad_other = swap_rows(grad)

    outs = call(
        functools.partial(window_kernel, half),
        [(rows + PAD, pixels)] * half + [(rows + PAD, freqs)] * half,
    )(grad, grad_other, *tables)
    bodies, edges = outs[:half], outs[half:]

    def from_hub(x, steps, flip):
        return permute(
            x,
            {
                (chip(low, 0), t, c): (
                    chip(low, steps),
                    1 - t if flip else t,
                    1 - c if steps else c,
                )
                for low in halves
                for t, c in cores
            },
        )

    bodies = [bodies[0]] + [from_hub(bodies[n], n, False) for n in range(1, half)]
    edges = [from_hub(edges[n], n, True) for n in range(half)]
    out, source = call(
        functools.partial(place_kernel, half, 1.0 / (sources * pixels * tile_count)),
        [(1, rows, pixels), (1, per_device)],
    )(bodies[0], *[dict(body=bodies, edge=edges)[k][n] for k, n in last_order(half)])
    return out, source[0]


M = 256
K = 128


def with_halo(block, sides, width):
    for axis, dim in sides:
        count = lax.axis_size(axis)
        forward = [(i, i + 1) for i in range(count - 1)]
        backward = [(target, source) for source, target in forward]
        low = lax.ppermute(
            lax.slice_in_dim(block, block.shape[dim] - width, None, axis=dim), axis, forward
        )
        high = lax.ppermute(lax.slice_in_dim(block, 0, width, axis=dim), axis, backward)
        block = jnp.concatenate([low, block, high], axis=dim)
    return block


def matmul(left_op, right_op):
    return lax.dot_general(
        left_op,
        right_op,
        (((1,), (0,)), ((), ())),
        precision=lax.Precision.HIGHEST,
        preferred_element_type=jnp.float32,
    )


def matmul_tn(left_op, right_op):
    return lax.dot_general(
        left_op,
        right_op,
        (((0,), (0,)), ((), ())),
        precision=lax.Precision.HIGHEST,
        preferred_element_type=jnp.float32,
    )


def matmul_nt(left_op, right_op):
    return lax.dot_general(
        left_op,
        right_op,
        (((1,), (1,)), ((), ())),
        precision=lax.Precision.HIGHEST,
        preferred_element_type=jnp.float32,
    )


def wave_tables(positions):
    freq_index = jnp.arange(K, dtype=jnp.int32) - K // 2
    phase_index = freq_index[:, None] * positions[None, :] % M
    angles = 2.0 * math.pi / M * phase_index.astype(jnp.float32)
    return (jnp.cos(angles), jnp.sin(angles))


def shards(mask_windows, target_windows, pupil_bands, pupil_phase, source_weight):
    src_count = lax.axis_size("src")
    tile_count = lax.axis_size("tile")
    row_count = lax.axis_size("row")
    local_x = mask_windows.shape[1]
    per_device = pupil_phase.shape[0]
    sources = per_device * src_count
    field_scale = 1.0 / (M * K)
    src_id = lax.axis_index("src")
    row_id = lax.axis_index("row")
    x_start = (src_id * row_count + row_id) * local_x
    block_starts = (jnp.arange(src_count, dtype=jnp.int32) * row_count + row_id) * local_x
    row_set = (block_starts[:, None] + jnp.arange(local_x, dtype=jnp.int32)[None, :]).reshape(
        src_count * local_x
    )
    cos_all, sin_all = wave_tables(jnp.arange(M, dtype=jnp.int32))
    cos_set, sin_set = wave_tables(row_set)
    cos_own, sin_own = wave_tables(x_start + jnp.arange(local_x, dtype=jnp.int32))
    window = mask_windows[0]
    goal_block = target_windows[0]
    zero_spec = jnp.zeros((K, K), jnp.float32)
    shard_rows = lax.all_gather(window, ("src", "row"), axis=0, tiled=True)
    part_real = matmul_nt(shard_rows, cos_all)
    part_imag = -matmul_nt(shard_rows, sin_all)
    spec_real = matmul(cos_all, part_real) + matmul(sin_all, part_imag)
    spec_imag = matmul(cos_all, part_imag) - matmul(sin_all, part_real)
    freq_cols = jnp.arange(K, dtype=jnp.int32)
    inside = (freq_cols[None, None, :] >= pupil_bands[:, :, 0:1]) & (
        freq_cols[None, None, :] < pupil_bands[:, :, 1:2]
    )
    passing = inside.astype(jnp.float32)
    pupil_real = passing * jnp.cos(pupil_phase)
    pupil_imag = passing * jnp.sin(pupil_phase)
    amp_real = (pupil_real * spec_real - pupil_imag * spec_imag).reshape(per_device * K, K)
    amp_imag = (pupil_imag * spec_real + pupil_real * spec_imag).reshape(per_device * K, K)
    half_real = (matmul(amp_real, cos_all) - matmul(amp_imag, sin_all)).reshape(per_device, K, M)
    half_imag = (matmul(amp_real, sin_all) + matmul(amp_imag, cos_all)).reshape(per_device, K, M)
    weights = source_weight / sources

    def fields(pair_in):
        one_real, one_imag = pair_in
        field_real = field_scale * (matmul_tn(cos_set, one_real) - matmul_tn(sin_set, one_imag))
        field_imag = field_scale * (matmul_tn(cos_set, one_imag) + matmul_tn(sin_set, one_real))
        return (field_real, field_imag)

    stack_real, stack_imag = lax.map(fields, (half_real, half_imag))
    part_real = stack_real
    part_imag = stack_imag
    intensity = lax.psum_scatter(
        jnp.sum(weights[:, None, None] * (part_real * part_real + part_imag * part_imag), axis=0),
        "src",
        scatter_dimension=0,
        tiled=True,
    )
    resist = jax.nn.sigmoid(STEEPNESS * (intensity - THRESHOLD))
    cotangent = LOSS_SCALE * (resist - goal_block) * STEEPNESS * resist * (1.0 - resist)
    cotangent_all = lax.all_gather(cotangent, "src", axis=0, tiled=True)
    source_ids = jnp.arange(per_device, dtype=jnp.int32)

    def add_back(source_id, totals):
        grad_real, grad_imag, source_terms = totals
        field_real = stack_real[source_id]
        field_imag = stack_imag[source_id]
        back_scale = 2.0 * weights[source_id] * cotangent_all
        back_real = back_scale * field_real
        back_imag = back_scale * field_imag
        adj_real = matmul(cos_set, back_real) + matmul(sin_set, back_imag)
        adj_imag = matmul(cos_set, back_imag) - matmul(sin_set, back_real)
        amp_grad_real = field_scale * (matmul_nt(adj_real, cos_all) + matmul_nt(adj_imag, sin_all))
        amp_grad_imag = field_scale * (matmul_nt(adj_imag, cos_all) - matmul_nt(adj_real, sin_all))
        pass_real = pupil_real[source_id]
        pass_imag = pupil_imag[source_id]
        grad_real = grad_real + pass_real * amp_grad_real + pass_imag * amp_grad_imag
        grad_imag = grad_imag + pass_real * amp_grad_imag - pass_imag * amp_grad_real
        term_value = jnp.sum(cotangent_all * (field_real * field_real + field_imag * field_imag))
        source_terms = source_terms + jnp.where(source_ids == source_id, term_value, 0.0)
        return (grad_real, grad_imag, source_terms)

    grad_real, grad_imag, source_terms = lax.fori_loop(
        0, per_device, add_back, (zero_spec, zero_spec, jnp.zeros((per_device,), jnp.float32))
    )
    grad_real, grad_imag = lax.psum((grad_real, grad_imag), ("src", "row"))
    source_sum = lax.psum(source_terms, ("tile", "row"))
    source_grad = source_sum / (sources * M * tile_count)
    q_one = matmul(grad_real, cos_all) - matmul(grad_imag, sin_all)
    q_two = matmul(grad_real, sin_all) + matmul(grad_imag, cos_all)
    grad_block = matmul_tn(cos_own, q_one) - matmul_tn(sin_own, q_two)
    padded = with_halo(grad_block, (("tile", 1),), OV)
    from_below = padded[:, :OV]
    from_above = padded[:, M + OV :]
    middle = jnp.zeros((local_x, M - 2 * OV), jnp.float32)
    grad_block = grad_block + jnp.concatenate([from_below, middle, from_above], axis=1)
    return (grad_block[None], source_grad)


def hubs_serve(mesh, mask_windows, pupil_phase):
    src_count = mesh.shape["src"]
    pixels = mask_windows.shape[2]
    sources, freqs = pupil_phase.shape[0] // mesh.shape["parts"], pupil_phase.shape[1]
    per_device = sources // src_count
    held = sources // 2 * (2 * pixels * pixels + 4 * freqs * freqs) * 4
    return (
        mesh.shape["row"] == 2
        and mesh.shape["tile"] == 2
        and src_count % 2 == 0
        and src_count // 2 <= PAD
        and per_device < PAD
        and mask_windows.shape[1] // (2 * src_count) % 16 == 0
        and pixels & (pixels - 1) == 0
        and pixels >= 2 * freqs
        and held <= VMEM_BUDGET // 2
    )


def solution(mesh):
    def run(mask_windows, target_windows, pupil_bands, pupil_phase, source_weight):
        hubs = hubs_serve(mesh, mask_windows, pupil_phase)
        return jax.shard_map(
            hub_shards if hubs else shards,
            mesh=mesh,
            in_specs=(
                P(("parts", "tile"), ("src", "row"), None),
                P(("parts", "tile"), ("src", "row"), None),
                P(("parts", "src"), None, None),
                P(("parts", "src"), None, None),
                P(("parts", "src")),
            ),
            out_specs=(P(("parts", "tile"), ("src", "row"), None), P(("parts", "src"))),
            check_vma=False,
        )(mask_windows, target_windows, pupil_bands, pupil_phase, source_weight)

    return run
```

```python
import functools
import itertools
import math

import jax
import jax.numpy as jnp
from jax import lax
from jax.experimental import pallas as pl
from jax.experimental.pallas import tpu as pltpu
from jax.sharding import PartitionSpec as P

OV = 32
STEEPNESS = 20.0
THRESHOLD = 0.15
LOSS_SCALE = 32.0
PAD = 8
F32 = jnp.float32
BF16 = jnp.bfloat16
VMEM_BUDGET = 24 * 1024 * 1024


def split(a):
    high = a.astype(BF16)
    return high, (a - high.astype(F32)).astype(BF16)


def dot(a, b):
    return jnp.dot(a, b, preferred_element_type=F32)


def dot_nt(a, b):
    return lax.dot_general(a, b, (((1,), (1,)), ((), ())), preferred_element_type=F32)


def mm3(left, right, op=dot):
    (lh, ll), (rh, rl) = left, right
    return op(lh, rh) + (op(lh, rl) + op(ll, rh))


def sincos(phase):
    h = 0.5 * phase
    u = h * h
    s = 1.0 / 6227020800.0
    for coef in (-1.0 / 39916800.0, 1.0 / 362880.0, -1.0 / 5040.0, 1.0 / 120.0, -1.0 / 6.0, 1.0):
        s = s * u + coef
    s = s * h
    c = 1.0 / 479001600.0
    for coef in (-1.0 / 3628800.0, 1.0 / 40320.0, -1.0 / 720.0, 1.0 / 24.0, -0.5, 1.0):
        c = c * u + coef
    two_s = s + s
    return two_s * c, 1.0 - two_s * s


def block_of(src, side, steps, half):
    same = half - 1 - steps
    other = half + steps
    low = src < half
    return jnp.where(low, same if side == 0 else other, other if side == 0 else same)


def fetch_kernel(mask, goal, bands, weight, message, bands_in, weight_in, sems):
    rows = mask.shape[1]
    per_device, _, freqs = bands.shape
    message[2 * rows :] = jnp.zeros_like(message[2 * rows :])
    copies = [
        pltpu.make_async_copy(source, target, sems.at[n])
        for n, (source, target) in enumerate(
            (
                (mask.at[0], message.at[pl.ds(0, rows)]),
                (goal.at[0], message.at[pl.ds(rows, rows)]),
                (bands, bands_in),
                (weight, weight_in),
            )
        )
    ]
    for copy in copies:
        copy.start()
    for copy in copies:
        copy.wait()
    for i in range(per_device):
        for n in range(2):
            message[2 * rows + i : 2 * rows + i + 1, n * freqs : (n + 1) * freqs] = bands_in[
                i, n : n + 1, :
            ].astype(F32)
    line = 2 * rows + per_device
    message[line : line + 1, :per_device] = weight_in[...]


def tables_kernel(phase, fwd_h, fwd_l, adj_h, adj_l, held, sem):
    copy = pltpu.make_async_copy(phase, held, sem)
    copy.start()
    freqs, pixels = fwd_h.shape[0] // 2, fwd_h.shape[1] // 2

    def waves(shape, freq_dim):
        freq = lax.broadcasted_iota(jnp.int32, shape, freq_dim) - freqs // 2
        turn = freq * lax.broadcasted_iota(jnp.int32, shape, 1 - freq_dim)
        turn = ((turn + pixels // 2) & (pixels - 1)) - pixels // 2
        sin, cos = sincos((2.0 * math.pi / pixels) * turn.astype(F32))
        return split(cos), split(sin)

    (cos_h, cos_l), (sin_h, sin_l) = waves((freqs, pixels), 0)
    for table, cos, sin in ((fwd_h, cos_h, sin_h), (fwd_l, cos_l, sin_l)):
        table[:freqs, :pixels] = cos
        table[:freqs, pixels:] = sin
        table[freqs:, :pixels] = -sin
        table[freqs:, pixels:] = cos
    (cos_h, cos_l), (sin_h, sin_l) = waves((pixels, freqs), 1)
    for table, cos, sin in ((adj_h, cos_h, sin_h), (adj_l, cos_l, sin_l)):
        table[:pixels, :freqs] = cos
        table[:pixels, freqs:] = -sin
        table[pixels:, :freqs] = sin
        table[pixels:, freqs:] = cos
    copy.wait()


def spectrum_kernel(half, order, *refs):
    blocks = [refs[order.index(d)] for d in range(2 * half)]
    fwd_h, fwd_l, adj_h, adj_l, spec, goal, meta, part = refs[2 * half :]
    rows, pixels = goal.shape[1], goal.shape[2]
    freqs = spec.shape[1]
    src, row = lax.axis_index("src"), lax.axis_index("row")
    own = jnp.concatenate([b[:rows] for b in blocks], axis=0)
    waves = mm3(split(own), (adj_h[:pixels], adj_l[:pixels]))
    part[...] = jnp.zeros_like(part)
    for d in range(2 * half):
        block = block_of(src, d // half, d % half, half)
        start = pl.multiple_of((block * 2 + row) * rows, rows)
        mine = waves[d * rows : (d + 1) * rows]
        part[pl.ds(start, rows), :] = mine[:, :freqs]
        part[pl.ds(pl.multiple_of(pixels + start, rows), rows), :] = mine[:, freqs:]
        goal[block] = blocks[d][rows : 2 * rows]
    for j in range(half):
        meta[j] = jnp.where(row == 0, blocks[j][2 * rows :], blocks[half + j][2 * rows :])
    spec[...] = mm3((fwd_h[...], fwd_l[...]), split(part[...]))


def weight_of(meta, source, per_device):
    j, i = divmod(source, per_device)
    return meta[j][per_device : per_device + 1, i : i + 1]


def fields_kernel(per_device, sources, first_row, slots, *refs):
    row = lax.axis_index("row")
    if first_row == 0:
        phase_own, *phases = refs[: slots + 1]
        spec_a, spec_b, meta, goal, fwd_h, fwd_l, adj_h, adj_l = refs[slots + 1 : -7]
        field, intensity, pupil, amp_h, amp_l, half_h, half_l = refs[-7:]
    else:
        meta, goal, amp_h, amp_l, fwd_h, fwd_l, adj_h, adj_l, field, intensity, *half_refs = refs
        half_h, half_l = half_refs
    rows, pixels = field.shape[1], intensity.shape[1]
    count, freqs = field.shape[0], amp_h.shape[1] // field.shape[0]
    if first_row == 0:
        spec = (spec_a[...] + spec_b[...]) * (1.0 / (pixels * freqs))
        spec_r, spec_i = spec[:freqs], spec[freqs:]
        column = lax.broadcasted_iota(jnp.int32, (freqs, freqs), 1).astype(F32)
        bounds = [meta[j].T for j in range(slots)]

    def amplitude(s):
        j, i = divmod(s, per_device)
        inside = (column >= bounds[j][:freqs, i : i + 1]) & (
            column < bounds[j][freqs : 2 * freqs, i : i + 1]
        )
        phase = phases[j][i]
        if j == 0:
            phase = jnp.where(row == 0, phase_own[i], phase)
        sin_p, cos_p = sincos(phase)
        pass_r = jnp.where(inside, cos_p, 0.0)
        pass_i = jnp.where(inside, sin_p, 0.0)
        pupil[s, :freqs] = pass_r
        pupil[s, freqs:] = pass_i
        lanes = slice(s * freqs, (s + 1) * freqs)
        for half, value in enumerate(
            (pass_r * spec_r - pass_i * spec_i, pass_i * spec_r + pass_r * spec_i)
        ):
            high, low = split(value)
            amp_h[half * freqs : (half + 1) * freqs, lanes] = high
            amp_l[half * freqs : (half + 1) * freqs, lanes] = low

    here, there = (slice(n, n + rows) for n in (first_row, pixels + first_row))
    waves = [jnp.concatenate([t[here], t[there]], axis=0) for t in (adj_h, adj_l)]
    for first in range(0, count, 2):
        members = range(first, min(first + 2, count))
        if first_row == 0:
            for s in members:
                amplitude(s)
        lanes = slice(first * freqs, (members[-1] + 1) * freqs)
        half = mm3(waves, (amp_h[:, lanes], amp_l[:, lanes]))
        for n, s in enumerate(members):
            for m in range(2):
                high, low = split(half[m * rows : (m + 1) * rows, n * freqs : (n + 1) * freqs])
                half_h[s * rows : (s + 1) * rows, m * freqs : (m + 1) * freqs] = high
                half_l[s * rows : (s + 1) * rows, m * freqs : (m + 1) * freqs] = low
    out = mm3((half_h[...], half_l[...]), (fwd_h[...], fwd_l[...]))
    total = jnp.zeros((rows, pixels), F32)
    for s in range(count):
        value = out[s * rows : (s + 1) * rows]
        field[s] = value
        out_r, out_i = value[:, :pixels], value[:, pixels:]
        weight = weight_of(meta, s, per_device) * (1.0 / sources)
        total = total + weight * (out_r * out_r + out_i * out_i)
    intensity[:rows] = total
    block = goal.shape[1]
    for n in range(rows // (2 * block)):
        place = rows + n * block
        intensity[place : place + block] = goal[first_row // (2 * block) + n]


def adjoint_kernel(per_device, sources, first_row, block, *refs):
    *before, field, pupil, light_a, light_b, meta = refs[:-8]
    fwd_h, fwd_l, adj_h, adj_l, grad, cot_ref, back_h, back_l = refs[-8:]
    rows, pixels = cot_ref.shape
    count, freqs = field.shape[0], grad.shape[1]
    row = lax.axis_index("row")
    for n in range(rows // block):
        here = slice(n * block, (n + 1) * block)
        place = slice(rows + n // 2 * block, rows + (n // 2 + 1) * block)
        goal = jnp.where(row == n % 2, light_a[place], light_b[place])
        intensity = light_a[here] + light_b[here]
        resist = 1.0 / (1.0 + jnp.exp(-STEEPNESS * (intensity - THRESHOLD)))
        cot_ref[here] = (LOSS_SCALE * STEEPNESS) * (resist - goal) * resist * (1.0 - resist)
    cot = cot_ref[...]
    line = lax.broadcasted_iota(jnp.int32, (PAD, freqs), 0)
    lane = lax.broadcasted_iota(jnp.int32, (PAD, freqs), 1)
    terms = jnp.zeros((PAD, freqs), F32)
    for s in range(count):
        value = field[s]
        back_r, back_i = cot * value[:, :pixels], cot * value[:, pixels:]
        power = back_r * value[:, :pixels] + back_i * value[:, pixels:]
        power = jnp.sum(jnp.sum(power, axis=0, keepdims=True), axis=1, keepdims=True)
        j, i = divmod(s, per_device)
        terms = terms + jnp.where((lane == i) & (line == j), power, 0.0)
        back = jnp.concatenate([back_r, back_i], axis=1)
        half = mm3(split(back), (adj_h[...], adj_l[...]))
        lanes = slice(s * freqs, (s + 1) * freqs)
        for n in range(2):
            high, low = split(half[:, n * freqs : (n + 1) * freqs])
            back_h[n * rows : (n + 1) * rows, lanes] = high
            back_l[n * rows : (n + 1) * rows, lanes] = low
    grad_r = jnp.zeros((freqs, freqs), F32)
    grad_i = jnp.zeros((freqs, freqs), F32)
    here, there = (slice(n, n + rows) for n in (first_row, pixels + first_row))
    waves = [jnp.concatenate([t[:, here], t[:, there]], axis=1) for t in (fwd_h, fwd_l)]
    for first in range(0, count, 2):
        members = range(first, min(first + 2, count))
        lanes = slice(first * freqs, (members[-1] + 1) * freqs)
        out = mm3(waves, (back_h[:, lanes], back_l[:, lanes]))
        for n, s in enumerate(members):
            lanes = slice(n * freqs, (n + 1) * freqs)
            weight = weight_of(meta, s, per_device) * (2.0 / (sources * pixels * freqs))
            pass_r, pass_i = weight * pupil[s, :freqs], weight * pupil[s, freqs:]
            out_r, out_i = out[:freqs, lanes], out[freqs:, lanes]
            grad_r = grad_r + (pass_r * out_r + pass_i * out_i)
            grad_i = grad_i + (pass_r * out_i - pass_i * out_r)
    for place, value in (
        (slice(0, freqs), grad_r),
        (slice(freqs, 2 * freqs), grad_i),
        (slice(2 * freqs, 2 * freqs + PAD), terms),
    ):
        grad[place] = value + before[0][place] if before else value


def window_kernel(half, grad_a, grad_b, fwd_h, fwd_l, adj_h, adj_l, own, pay_a, pay_b, pay_c):
    rows, pixels = own.shape[0] - PAD, own.shape[1]
    freqs = grad_a.shape[1]
    src, row, tile = lax.axis_index("src"), lax.axis_index("row"), lax.axis_index("tile")
    total = grad_a[: 2 * freqs] + grad_b[: 2 * freqs]
    flat = split(jnp.concatenate([total[:freqs], total[freqs:]], axis=1))
    waves = mm3(flat, (fwd_h[...], fwd_l[...]))
    waves = jnp.concatenate([waves[:, :pixels], waves[:, pixels:]], axis=0)
    tables = []
    for table in (adj_h, adj_l):
        parts = []
        for steps, core in ((0, row), (1, 1 - row)):
            start = (block_of(src, 0, steps, half) * 2 + core) * rows
            parts.append(table[pl.ds(pl.multiple_of(start, rows), rows), :])
        tables.append(jnp.concatenate(parts, axis=0))
    window = mm3(tables, split(waves))
    terms = jnp.where(row == 0, grad_a[2 * freqs :], grad_b[2 * freqs :])
    near, far = window[:rows], window[rows:]

    def edge(block):
        return jnp.where(tile == 0, block[:, pixels - OV :], block[:, :OV])

    rest = jnp.zeros((rows, pixels - OV), F32)
    strip_near = jnp.concatenate([edge(near), rest], axis=1)
    strip_far = jnp.concatenate([edge(far), rest], axis=1)
    low = src < half
    for target, rows_low, n_low, rows_high, n_high in (
        (own, near, 0, near, 0),
        (pay_a, far, 1, strip_near, 0),
        (pay_b, strip_far, 1, far, 1),
        (pay_c, strip_near, 0, strip_far, 1),
    ):
        target[:rows] = jnp.where(low, rows_low, rows_high)
        target[rows : rows + 1, :freqs] = jnp.where(
            low, terms[n_low : n_low + 1], terms[n_high : n_high + 1]
        )


def place_kernel(half, term_scale, own, got_a, got_b, got_c, out, source):
    rows, pixels = out.shape[1:]
    per_device = source.shape[1]
    src, tile = lax.axis_index("src"), lax.axis_index("tile")
    low, hub = src < half, (src == half - 1) | (src == half)

    def pick(low_hub, low_end, high_hub, high_end, *index):
        at_hub = jnp.where(low, low_hub[index], high_hub[index])
        at_end = jnp.where(low, low_end[index], high_end[index])
        return jnp.where(hub, at_hub, at_end)

    bodies, strips = (own, got_a, own, got_b), (got_c, got_b, got_a, got_c)
    body = pick(*bodies, slice(0, rows), slice(None))
    strip = pick(*strips, slice(0, rows), slice(0, OV))
    zero = jnp.zeros_like(strip)
    middle = jnp.zeros((rows, pixels - 2 * OV), F32)
    left, right = jnp.where(tile == 1, strip, zero), jnp.where(tile == 0, strip, zero)
    out[0] = body + jnp.concatenate([left, middle, right], axis=1)
    term = slice(rows, rows + 1), slice(0, per_device)
    source[...] = (pick(*bodies, *term) + pick(*strips, *term)) * term_scale


def call(kernel, outs, scratch=(), kind=F32, hbm=0, hub=False):
    def at_hub(*refs):
        src, half = lax.axis_index("src"), lax.axis_size("src") // 2
        pl.when((src == half - 1) | (src == half))(functools.partial(kernel, *refs))

    kinds = kind if isinstance(kind, list) else [kind] * len(outs)
    held = {"in_specs": [pl.BlockSpec(memory_space=pltpu.HBM)] * hbm} if hbm else {}
    return pl.pallas_call(
        at_hub if hub else kernel,
        out_shape=[jax.ShapeDtypeStruct(o, k) for o, k in zip(outs, kinds)],
        out_specs=[pl.BlockSpec(memory_space=pltpu.VMEM) for _ in outs],
        scratch_shapes=list(scratch),
        compiler_params=pltpu.CompilerParams(vmem_limit_bytes=VMEM_BUDGET),
        **held,
    )


def permute(x, wanted):
    shape = tuple(lax.axis_size(a) for a in ("src", "tile", "row"))
    devices = list(itertools.product(*(range(n) for n in shape)))
    pairs = dict(wanted)
    sources = [d for d in devices if d not in pairs]
    targets = [d for d in devices if d not in pairs.values()]

    def cost(pair):
        source, target = pair
        hops = abs(source[0] - target[0]) + abs(source[1] - target[1])
        return (source == target, hops, source, target)

    for source, target in sorted(itertools.product(sources, targets), key=cost):
        if source not in pairs and target not in pairs.values():
            pairs[source] = target
    flat = {d: n for n, d in enumerate(devices)}
    return lax.ppermute(x, ("src", "tile", "row"), [(flat[a], flat[b]) for a, b in pairs.items()])


def swap_rows(x):
    return lax.ppermute(x, "row", [(0, 1), (1, 0)])


def hub_shards(mask_windows, target_windows, pupil_bands, pupil_phase, source_weight):
    src_count, tile_count = lax.axis_size("src"), lax.axis_size("tile")
    rows, pixels = mask_windows.shape[1:]
    per_device, freqs = pupil_phase.shape[:2]
    sources = per_device * src_count
    half = src_count // 2
    count = half * per_device

    def chip(low, steps):
        return half - 1 - steps if low else half + steps

    cores = list(itertools.product(range(tile_count), range(2)))
    halves = (True, False)

    def to_hub(x, side, steps):
        return permute(
            x,
            {
                (chip(low, steps), t, c): (chip(low != (side == 1), 0), t, c)
                for low in halves
                for t, c in cores
            },
        )

    def phases_to_hub(x, steps):
        pairs = {}
        for low, tile in itertools.product(halves, range(tile_count)):
            if steps:
                pairs[chip(low, steps), tile, 0] = chip(low, 0), tile, 0
            pairs[chip(low, steps), tile, 1 if steps else 0] = chip(not low, 0), tile, 1
        return permute(x, pairs)

    pin = functools.partial(pltpu.with_memory_space_constraint, memory_space=pltpu.HBM)
    (message,) = call(
        fetch_kernel,
        [(2 * rows + PAD, pixels)],
        [
            pltpu.VMEM((per_device, 2, freqs), jnp.int32),
            pltpu.VMEM((1, per_device), F32),
            pltpu.SemaphoreType.DMA((4,)),
        ],
        hbm=4,
    )(
        pin(mask_windows),
        pin(target_windows),
        pin(pupil_bands.transpose(0, 2, 1)),
        pin(source_weight.reshape(1, per_device)),
    )
    order = (0, half, *range(1, half), *range(half + 1, 2 * half))
    blocks = [message] + [to_hub(message, d // half, d % half) for d in order[1:]]
    phases = [phases_to_hub(pupil_phase, n) for n in reversed(range(half))][::-1]
    *tables, phase = call(
        tables_kernel,
        [(2 * freqs, 2 * pixels)] * 2 + [(2 * pixels, 2 * freqs)] * 2 + [pupil_phase.shape],
        [pltpu.SemaphoreType.DMA],
        kind=[BF16] * 4 + [F32],
        hbm=1,
    )(pin(pupil_phase))

    spec, goal, meta = call(
        functools.partial(spectrum_kernel, half, order),
        [(2 * freqs, freqs), (src_count, rows, pixels), (half, PAD, pixels)],
        [pltpu.VMEM((2 * pixels, freqs), F32)],
        hub=True,
    )(*blocks, *tables)
    spec_other = swap_rows(spec)

    shape = (2 * freqs, count * freqs)
    part = pixels // 2
    outs = [(count, part, 2 * pixels), (part + part // 2, pixels)]
    *first, pupil, amp_h, amp_l = call(
        functools.partial(fields_kernel, per_device, sources, 0, half),
        [*outs, (count, 2 * freqs, freqs), shape, shape],
        [pltpu.VMEM((count * part, 2 * freqs), BF16)] * 2,
        kind=[F32, F32, F32, BF16, BF16],
        hub=True,
    )(phase, *phases, spec, spec_other, meta, goal, *tables)
    second = call(
        functools.partial(fields_kernel, per_device, sources, part, half),
        outs,
        [pltpu.VMEM((count * part, 2 * freqs), BF16)] * 2,
        hub=True,
    )(meta, goal, amp_h, amp_l, *tables)
    fields = [first, second]
    others = [swap_rows(light) for _, light in fields]
    grad = []
    for first_row, (field, light), other in zip((0, part), fields, others):
        grad = call(
            functools.partial(adjoint_kernel, per_device, sources, first_row, rows),
            [(2 * freqs + PAD, freqs)],
            [pltpu.VMEM((part, pixels), F32)]
            + [pltpu.VMEM((2 * part, count * freqs), BF16)] * 2,
            hub=True,
        )(*grad, field, pupil, light, other, meta, *tables)
    (grad,) = grad
    grad_other = swap_rows(grad)

    own, pay_a, pay_b, pay_c = call(
        functools.partial(window_kernel, half), [(rows + PAD, pixels)] * 4, hub=True
    )(grad, grad_other, *tables)
    low_end, low_hub, high_hub, high_end = chip(True, 1), chip(True, 0), chip(False, 0), chip(False, 1)

    def moves(*chips):
        return {
            (z, t, c): (to, t ^ tile_flip, c ^ core_flip)
            for z, to, tile_flip, core_flip in chips
            for t, c in cores
        }

    got_a = permute(
        pay_a,
        moves(
            (low_hub, low_end, 0, 1),
            (high_hub, high_hub, 1, 0),
            (low_end, high_end, 0, 0),
            (high_end, low_hub, 0, 0),
        ),
    )
    got_b = permute(
        pay_b,
        moves(
            (low_hub, low_end, 1, 1),
            (high_hub, high_end, 0, 1),
            (low_end, low_hub, 0, 1),
            (high_end, high_hub, 0, 1),
        ),
    )
    got_c = permute(
        pay_c,
        moves(
            (low_hub, low_hub, 1, 0),
            (high_hub, high_end, 1, 1),
            (high_end, high_hub, 0, 1),
        ),
    )
    out, source = call(
        functools.partial(place_kernel, half, 1.0 / (sources * pixels * tile_count)),
        [(1, rows, pixels), (1, per_device)],
    )(own, got_a, got_b, got_c)
    return out, source[0]


M = 256
K = 128


def with_halo(block, sides, width):
    for axis, dim in sides:
        count = lax.axis_size(axis)
        forward = [(i, i + 1) for i in range(count - 1)]
        backward = [(target, source) for source, target in forward]
        low = lax.ppermute(
            lax.slice_in_dim(block, block.shape[dim] - width, None, axis=dim), axis, forward
        )
        high = lax.ppermute(lax.slice_in_dim(block, 0, width, axis=dim), axis, backward)
        block = jnp.concatenate([low, block, high], axis=dim)
    return block


def matmul(left_op, right_op):
    return lax.dot_general(
        left_op,
        right_op,
        (((1,), (0,)), ((), ())),
        precision=lax.Precision.HIGHEST,
        preferred_element_type=jnp.float32,
    )


def matmul_tn(left_op, right_op):
    return lax.dot_general(
        left_op,
        right_op,
        (((0,), (0,)), ((), ())),
        precision=lax.Precision.HIGHEST,
        preferred_element_type=jnp.float32,
    )


def matmul_nt(left_op, right_op):
    return lax.dot_general(
        left_op,
        right_op,
        (((1,), (1,)), ((), ())),
        precision=lax.Precision.HIGHEST,
        preferred_element_type=jnp.float32,
    )


def wave_tables(positions):
    freq_index = jnp.arange(K, dtype=jnp.int32) - K // 2
    phase_index = freq_index[:, None] * positions[None, :] % M
    angles = 2.0 * math.pi / M * phase_index.astype(jnp.float32)
    return (jnp.cos(angles), jnp.sin(angles))


def shards(mask_windows, target_windows, pupil_bands, pupil_phase, source_weight):
    src_count = lax.axis_size("src")
    tile_count = lax.axis_size("tile")
    row_count = lax.axis_size("row")
    local_x = mask_windows.shape[1]
    per_device = pupil_phase.shape[0]
    sources = per_device * src_count
    field_scale = 1.0 / (M * K)
    src_id = lax.axis_index("src")
    row_id = lax.axis_index("row")
    x_start = (src_id * row_count + row_id) * local_x
    block_starts = (jnp.arange(src_count, dtype=jnp.int32) * row_count + row_id) * local_x
    row_set = (block_starts[:, None] + jnp.arange(local_x, dtype=jnp.int32)[None, :]).reshape(
        src_count * local_x
    )
    cos_all, sin_all = wave_tables(jnp.arange(M, dtype=jnp.int32))
    cos_set, sin_set = wave_tables(row_set)
    cos_own, sin_own = wave_tables(x_start + jnp.arange(local_x, dtype=jnp.int32))
    window = mask_windows[0]
    goal_block = target_windows[0]
    zero_spec = jnp.zeros((K, K), jnp.float32)
    shard_rows = lax.all_gather(window, ("src", "row"), axis=0, tiled=True)
    part_real = matmul_nt(shard_rows, cos_all)
    part_imag = -matmul_nt(shard_rows, sin_all)
    spec_real = matmul(cos_all, part_real) + matmul(sin_all, part_imag)
    spec_imag = matmul(cos_all, part_imag) - matmul(sin_all, part_real)
    freq_cols = jnp.arange(K, dtype=jnp.int32)
    inside = (freq_cols[None, None, :] >= pupil_bands[:, :, 0:1]) & (
        freq_cols[None, None, :] < pupil_bands[:, :, 1:2]
    )
    passing = inside.astype(jnp.float32)
    pupil_real = passing * jnp.cos(pupil_phase)
    pupil_imag = passing * jnp.sin(pupil_phase)
    amp_real = (pupil_real * spec_real - pupil_imag * spec_imag).reshape(per_device * K, K)
    amp_imag = (pupil_imag * spec_real + pupil_real * spec_imag).reshape(per_device * K, K)
    half_real = (matmul(amp_real, cos_all) - matmul(amp_imag, sin_all)).reshape(per_device, K, M)
    half_imag = (matmul(amp_real, sin_all) + matmul(amp_imag, cos_all)).reshape(per_device, K, M)
    weights = source_weight / sources

    def fields(pair_in):
        one_real, one_imag = pair_in
        field_real = field_scale * (matmul_tn(cos_set, one_real) - matmul_tn(sin_set, one_imag))
        field_imag = field_scale * (matmul_tn(cos_set, one_imag) + matmul_tn(sin_set, one_real))
        return (field_real, field_imag)

    stack_real, stack_imag = lax.map(fields, (half_real, half_imag))
    part_real = stack_real
    part_imag = stack_imag
    intensity = lax.psum_scatter(
        jnp.sum(weights[:, None, None] * (part_real * part_real + part_imag * part_imag), axis=0),
        "src",
        scatter_dimension=0,
        tiled=True,
    )
    resist = jax.nn.sigmoid(STEEPNESS * (intensity - THRESHOLD))
    cotangent = LOSS_SCALE * (resist - goal_block) * STEEPNESS * resist * (1.0 - resist)
    cotangent_all = lax.all_gather(cotangent, "src", axis=0, tiled=True)
    source_ids = jnp.arange(per_device, dtype=jnp.int32)

    def add_back(source_id, totals):
        grad_real, grad_imag, source_terms = totals
        field_real = stack_real[source_id]
        field_imag = stack_imag[source_id]
        back_scale = 2.0 * weights[source_id] * cotangent_all
        back_real = back_scale * field_real
        back_imag = back_scale * field_imag
        adj_real = matmul(cos_set, back_real) + matmul(sin_set, back_imag)
        adj_imag = matmul(cos_set, back_imag) - matmul(sin_set, back_real)
        amp_grad_real = field_scale * (matmul_nt(adj_real, cos_all) + matmul_nt(adj_imag, sin_all))
        amp_grad_imag = field_scale * (matmul_nt(adj_imag, cos_all) - matmul_nt(adj_real, sin_all))
        pass_real = pupil_real[source_id]
        pass_imag = pupil_imag[source_id]
        grad_real = grad_real + pass_real * amp_grad_real + pass_imag * amp_grad_imag
        grad_imag = grad_imag + pass_real * amp_grad_imag - pass_imag * amp_grad_real
        term_value = jnp.sum(cotangent_all * (field_real * field_real + field_imag * field_imag))
        source_terms = source_terms + jnp.where(source_ids == source_id, term_value, 0.0)
        return (grad_real, grad_imag, source_terms)

    grad_real, grad_imag, source_terms = lax.fori_loop(
        0, per_device, add_back, (zero_spec, zero_spec, jnp.zeros((per_device,), jnp.float32))
    )
    grad_real, grad_imag = lax.psum((grad_real, grad_imag), ("src", "row"))
    source_sum = lax.psum(source_terms, ("tile", "row"))
    source_grad = source_sum / (sources * M * tile_count)
    q_one = matmul(grad_real, cos_all) - matmul(grad_imag, sin_all)
    q_two = matmul(grad_real, sin_all) + matmul(grad_imag, cos_all)
    grad_block = matmul_tn(cos_own, q_one) - matmul_tn(sin_own, q_two)
    padded = with_halo(grad_block, (("tile", 1),), OV)
    from_below = padded[:, :OV]
    from_above = padded[:, M + OV :]
    middle = jnp.zeros((local_x, M - 2 * OV), jnp.float32)
    grad_block = grad_block + jnp.concatenate([from_below, middle, from_above], axis=1)
    return (grad_block[None], source_grad)


def hubs_serve(mesh, mask_windows, pupil_phase):
    src_count = mesh.shape["src"]
    pixels = mask_windows.shape[2]
    sources, freqs = pupil_phase.shape[0] // mesh.shape["parts"], pupil_phase.shape[1]
    per_device = sources // src_count
    held = sources // 2 * (2 * pixels * pixels + 4 * freqs * freqs) * 4
    return (
        mesh.shape["row"] == 2
        and mesh.shape["tile"] == 2
        and src_count % 2 == 0
        and src_count // 2 == 2
        and per_device < PAD
        and mask_windows.shape[1] // (2 * src_count) % 16 == 0
        and pixels & (pixels - 1) == 0
        and pixels >= 2 * freqs
        and held <= VMEM_BUDGET // 2
    )


def solution(mesh):
    def run(mask_windows, target_windows, pupil_bands, pupil_phase, source_weight):
        hubs = hubs_serve(mesh, mask_windows, pupil_phase)
        return jax.shard_map(
            hub_shards if hubs else shards,
            mesh=mesh,
            in_specs=(
                P(("parts", "tile"), ("src", "row"), None),
                P(("parts", "tile"), ("src", "row"), None),
                P(("parts", "src"), None, None),
                P(("parts", "src"), None, None),
                P(("parts", "src")),
            ),
            out_specs=(P(("parts", "tile"), ("src", "row"), None), P(("parts", "src"))),
            check_vma=False,
        )(mask_windows, target_windows, pupil_bands, pupil_phase, source_weight)

    return run
```

```python
import functools
import itertools
import math

import jax
import jax.numpy as jnp
from jax import lax
from jax.experimental import pallas as pl
from jax.experimental.pallas import tpu as pltpu
from jax.sharding import PartitionSpec as P

OV = 32
STEEPNESS = 20.0
THRESHOLD = 0.15
LOSS_SCALE = 32.0
PAD = 8
F32 = jnp.float32
BF16 = jnp.bfloat16
VMEM_BUDGET = 24 * 1024 * 1024


def split(a):
    high = a.astype(BF16)
    return high, (a - high.astype(F32)).astype(BF16)


def dot(a, b):
    return jnp.dot(a, b, preferred_element_type=F32)


def dot_nt(a, b):
    return lax.dot_general(a, b, (((1,), (1,)), ((), ())), preferred_element_type=F32)


def mm3(left, right, op=dot):
    (lh, ll), (rh, rl) = left, right
    return op(lh, rh) + (op(lh, rl) + op(ll, rh))


def sincos(phase):
    h = 0.5 * phase
    u = h * h
    s = 1.0 / 6227020800.0
    for coef in (-1.0 / 39916800.0, 1.0 / 362880.0, -1.0 / 5040.0, 1.0 / 120.0, -1.0 / 6.0, 1.0):
        s = s * u + coef
    s = s * h
    c = 1.0 / 479001600.0
    for coef in (-1.0 / 3628800.0, 1.0 / 40320.0, -1.0 / 720.0, 1.0 / 24.0, -0.5, 1.0):
        c = c * u + coef
    two_s = s + s
    return two_s * c, 1.0 - two_s * s


def block_of(src, side, steps, half):
    same = half - 1 - steps
    other = half + steps
    low = src < half
    return jnp.where(low, same if side == 0 else other, other if side == 0 else same)


def fetch_kernel(mask, goal, bands, weight, message, bands_in, weight_in, sems):
    rows = mask.shape[1]
    per_device, _, freqs = bands.shape
    message[2 * rows :] = jnp.zeros_like(message[2 * rows :])
    copies = [
        pltpu.make_async_copy(source, target, sems.at[n])
        for n, (source, target) in enumerate(
            (
                (mask.at[0], message.at[pl.ds(0, rows)]),
                (goal.at[0], message.at[pl.ds(rows, rows)]),
                (bands, bands_in),
                (weight, weight_in),
            )
        )
    ]
    for copy in copies:
        copy.start()
    for copy in copies:
        copy.wait()
    for i in range(per_device):
        for n in range(2):
            message[2 * rows + i : 2 * rows + i + 1, n * freqs : (n + 1) * freqs] = bands_in[
                i, n : n + 1, :
            ].astype(F32)
    line = 2 * rows + per_device
    message[line : line + 1, :per_device] = weight_in[...]


def tables_kernel(phase, fwd_h, fwd_l, adj_h, adj_l, held, sem):
    copy = pltpu.make_async_copy(phase, held, sem)
    copy.start()
    freqs, pixels = fwd_h.shape[0] // 2, fwd_h.shape[1] // 2

    def waves(shape, freq_dim):
        freq = lax.broadcasted_iota(jnp.int32, shape, freq_dim) - freqs // 2
        turn = freq * lax.broadcasted_iota(jnp.int32, shape, 1 - freq_dim)
        turn = ((turn + pixels // 2) & (pixels - 1)) - pixels // 2
        sin, cos = sincos((2.0 * math.pi / pixels) * turn.astype(F32))
        return split(cos), split(sin)

    (cos_h, cos_l), (sin_h, sin_l) = waves((freqs, pixels), 0)
    for table, cos, sin in ((fwd_h, cos_h, sin_h), (fwd_l, cos_l, sin_l)):
        table[:freqs, :pixels] = cos
        table[:freqs, pixels:] = sin
        table[freqs:, :pixels] = -sin
        table[freqs:, pixels:] = cos
    (cos_h, cos_l), (sin_h, sin_l) = waves((pixels, freqs), 1)
    for table, cos, sin in ((adj_h, cos_h, sin_h), (adj_l, cos_l, sin_l)):
        table[:pixels, :freqs] = cos
        table[:pixels, freqs:] = -sin
        table[pixels:, :freqs] = sin
        table[pixels:, freqs:] = cos
    copy.wait()


def spectrum_kernel(half, order, *refs):
    blocks = [refs[order.index(d)] for d in range(2 * half)]
    fwd_h, fwd_l, adj_h, adj_l, spec, goal, meta, part = refs[2 * half :]
    rows, pixels = goal.shape[1], goal.shape[2]
    freqs = spec.shape[1]
    src, row = lax.axis_index("src"), lax.axis_index("row")
    own = jnp.concatenate([b[:rows] for b in blocks], axis=0)
    waves = mm3(split(own), (adj_h[:pixels], adj_l[:pixels]))
    part[...] = jnp.zeros_like(part)
    for d in range(2 * half):
        block = block_of(src, d // half, d % half, half)
        start = pl.multiple_of((block * 2 + row) * rows, rows)
        mine = waves[d * rows : (d + 1) * rows]
        part[pl.ds(start, rows), :] = mine[:, :freqs]
        part[pl.ds(pl.multiple_of(pixels + start, rows), rows), :] = mine[:, freqs:]
        goal[block] = blocks[d][rows : 2 * rows]
    for j in range(half):
        meta[j] = jnp.where(row == 0, blocks[j][2 * rows :], blocks[half + j][2 * rows :])
    spec[...] = mm3((fwd_h[...], fwd_l[...]), split(part[...]))


def weight_of(meta, source, per_device):
    j, i = divmod(source, per_device)
    return meta[j][per_device : per_device + 1, i : i + 1]


def fields_kernel(per_device, sources, first_row, slots, *refs):
    row = lax.axis_index("row")
    if first_row == 0:
        phase_own, *phases = refs[: slots + 1]
        spec_a, spec_b, meta, goal, fwd_h, fwd_l, adj_h, adj_l = refs[slots + 1 : -7]
        field, intensity, pupil, amp_h, amp_l, half_h, half_l = refs[-7:]
    else:
        meta, goal, amp_h, amp_l, fwd_h, fwd_l, adj_h, adj_l, field, intensity, *half_refs = refs
        half_h, half_l = half_refs
    rows, pixels = field.shape[1], intensity.shape[1]
    count, freqs = field.shape[0], amp_h.shape[1] // field.shape[0]
    if first_row == 0:
        spec = (spec_a[...] + spec_b[...]) * (1.0 / (pixels * freqs))
        spec_r, spec_i = spec[:freqs], spec[freqs:]
        column = lax.broadcasted_iota(jnp.int32, (freqs, freqs), 1).astype(F32)
        bounds = [meta[j].T for j in range(slots)]

    def amplitude(s):
        j, i = divmod(s, per_device)
        inside = (column >= bounds[j][:freqs, i : i + 1]) & (
            column < bounds[j][freqs : 2 * freqs, i : i + 1]
        )
        phase = phases[j][i]
        if j == 0:
            phase = jnp.where(row == 0, phase_own[i], phase)
        sin_p, cos_p = sincos(phase)
        pass_r = jnp.where(inside, cos_p, 0.0)
        pass_i = jnp.where(inside, sin_p, 0.0)
        pupil[s, :freqs] = pass_r
        pupil[s, freqs:] = pass_i
        lanes = slice(s * freqs, (s + 1) * freqs)
        for half, value in enumerate(
            (pass_r * spec_r - pass_i * spec_i, pass_i * spec_r + pass_r * spec_i)
        ):
            high, low = split(value)
            amp_h[half * freqs : (half + 1) * freqs, lanes] = high
            amp_l[half * freqs : (half + 1) * freqs, lanes] = low

    here, there = (slice(n, n + rows) for n in (first_row, pixels + first_row))
    waves = [jnp.concatenate([t[here], t[there]], axis=0) for t in (adj_h, adj_l)]
    for first in range(0, count, 2):
        members = range(first, min(first + 2, count))
        if first_row == 0:
            for s in members:
                amplitude(s)
        lanes = slice(first * freqs, (members[-1] + 1) * freqs)
        half = mm3(waves, (amp_h[:, lanes], amp_l[:, lanes]))
        for n, s in enumerate(members):
            for m in range(2):
                high, low = split(half[m * rows : (m + 1) * rows, n * freqs : (n + 1) * freqs])
                half_h[s * rows : (s + 1) * rows, m * freqs : (m + 1) * freqs] = high
                half_l[s * rows : (s + 1) * rows, m * freqs : (m + 1) * freqs] = low
    out = mm3((half_h[...], half_l[...]), (fwd_h[...], fwd_l[...]))
    total = jnp.zeros((rows, pixels), F32)
    for s in range(count):
        value = out[s * rows : (s + 1) * rows]
        field[s] = value
        out_r, out_i = value[:, :pixels], value[:, pixels:]
        weight = weight_of(meta, s, per_device) * (1.0 / sources)
        total = total + weight * (out_r * out_r + out_i * out_i)
    intensity[:rows] = total
    block = goal.shape[1]
    for n in range(rows // (2 * block)):
        place = rows + n * block
        intensity[place : place + block] = goal[first_row // (2 * block) + n]


def adjoint_kernel(per_device, sources, first_row, block, *refs):
    *before, field, pupil, light_a, light_b, meta = refs[:-8]
    fwd_h, fwd_l, adj_h, adj_l, grad, cot_ref, back_h, back_l = refs[-8:]
    rows, pixels = cot_ref.shape
    count, freqs = field.shape[0], grad.shape[1]
    row = lax.axis_index("row")
    for n in range(rows // block):
        here = slice(n * block, (n + 1) * block)
        place = slice(rows + n // 2 * block, rows + (n // 2 + 1) * block)
        goal = jnp.where(row == n % 2, light_a[place], light_b[place])
        intensity = light_a[here] + light_b[here]
        resist = 1.0 / (1.0 + jnp.exp(-STEEPNESS * (intensity - THRESHOLD)))
        cot_ref[here] = (LOSS_SCALE * STEEPNESS) * (resist - goal) * resist * (1.0 - resist)
    cot = cot_ref[...]
    line = lax.broadcasted_iota(jnp.int32, (PAD, freqs), 0)
    lane = lax.broadcasted_iota(jnp.int32, (PAD, freqs), 1)
    terms = jnp.zeros((PAD, freqs), F32)
    for s in range(count):
        value = field[s]
        back_r, back_i = cot * value[:, :pixels], cot * value[:, pixels:]
        power = back_r * value[:, :pixels] + back_i * value[:, pixels:]
        power = jnp.sum(jnp.sum(power, axis=0, keepdims=True), axis=1, keepdims=True)
        j, i = divmod(s, per_device)
        terms = terms + jnp.where((lane == i) & (line == j), power, 0.0)
        back = jnp.concatenate([back_r, back_i], axis=1)
        half = mm3(split(back), (adj_h[...], adj_l[...]))
        lanes = slice(s * freqs, (s + 1) * freqs)
        for n in range(2):
            high, low = split(half[:, n * freqs : (n + 1) * freqs])
            back_h[n * rows : (n + 1) * rows, lanes] = high
            back_l[n * rows : (n + 1) * rows, lanes] = low
    grad_r = jnp.zeros((freqs, freqs), F32)
    grad_i = jnp.zeros((freqs, freqs), F32)
    here, there = (slice(n, n + rows) for n in (first_row, pixels + first_row))
    waves = [jnp.concatenate([t[:, here], t[:, there]], axis=1) for t in (fwd_h, fwd_l)]
    for first in range(0, count, 2):
        members = range(first, min(first + 2, count))
        lanes = slice(first * freqs, (members[-1] + 1) * freqs)
        out = mm3(waves, (back_h[:, lanes], back_l[:, lanes]))
        for n, s in enumerate(members):
            lanes = slice(n * freqs, (n + 1) * freqs)
            weight = weight_of(meta, s, per_device) * (2.0 / (sources * pixels * freqs))
            pass_r, pass_i = weight * pupil[s, :freqs], weight * pupil[s, freqs:]
            out_r, out_i = out[:freqs, lanes], out[freqs:, lanes]
            grad_r = grad_r + (pass_r * out_r + pass_i * out_i)
            grad_i = grad_i + (pass_r * out_i - pass_i * out_r)
    for place, value in (
        (slice(0, freqs), grad_r),
        (slice(freqs, 2 * freqs), grad_i),
        (slice(2 * freqs, 2 * freqs + PAD), terms),
    ):
        grad[place] = value + before[0][place] if before else value


def window_kernel(half, grad_a, grad_b, fwd_h, fwd_l, adj_h, adj_l, own, *pays):
    pay_a, pay_b, pay_c, pay_d = pays
    rows, pixels = own.shape[0] - PAD, own.shape[1]
    freqs = grad_a.shape[1]
    src, row, tile = lax.axis_index("src"), lax.axis_index("row"), lax.axis_index("tile")
    total = grad_a[: 2 * freqs] + grad_b[: 2 * freqs]
    flat = split(jnp.concatenate([total[:freqs], total[freqs:]], axis=1))
    waves = mm3(flat, (fwd_h[...], fwd_l[...]))
    waves = jnp.concatenate([waves[:, :pixels], waves[:, pixels:]], axis=0)
    tables = []
    for table in (adj_h, adj_l):
        parts = []
        for steps, core in ((0, row), (1, 1 - row)):
            start = (block_of(src, 0, steps, half) * 2 + core) * rows
            parts.append(table[pl.ds(pl.multiple_of(start, rows), rows), :])
        tables.append(jnp.concatenate(parts, axis=0))
    window = mm3(tables, split(waves))
    terms = jnp.where(row == 0, grad_a[2 * freqs :], grad_b[2 * freqs :])
    near, far = window[:rows], window[rows:]

    def edge(block):
        return jnp.where(tile == 0, block[:, pixels - OV :], block[:, :OV])

    def put_rows(target, block, n):
        target[:rows] = block
        target[rows : rows + 1, :freqs] = terms[n : n + 1]

    def put_strip(target, block, n):
        block = edge(block)
        lines = range(0, rows, PAD)
        block = jnp.concatenate([block[i : i + PAD] for i in lines], axis=1)
        target[:PAD, : block.shape[1]] = block
        target[PAD : PAD + 1, :freqs] = terms[n : n + 1]

    put_rows(own, near, 0)
    put_rows(pay_b, far, 1)
    put_strip(pay_c, far, 1)

    @pl.when(src < half)
    def _():
        put_rows(pay_a, far, 1)
        put_strip(pay_d, near, 0)

    @pl.when(src >= half)
    def _():
        put_strip(pay_a, near, 0)
        put_strip(pay_d, far, 1)


def place_kernel(half, term_scale, own, got_a, got_b, got_c, got_d, out, source):
    rows, pixels = out.shape[1:]
    per_device = source.shape[1]
    src, tile = lax.axis_index("src"), lax.axis_index("tile")
    low, hub = src < half, (src == half - 1) | (src == half)

    def pick(low_hub, low_end, high_hub, high_end, *index):
        at_hub = jnp.where(low, low_hub[index], high_hub[index])
        at_end = jnp.where(low, low_end[index], high_end[index])
        return jnp.where(hub, at_hub, at_end)

    bodies, strips = (own, got_a, own, got_b), (got_d, got_c, got_a, got_d)
    body = pick(*bodies, slice(0, rows), slice(None))
    strip = pick(*strips, slice(0, PAD), slice(0, rows // PAD * OV))
    places = range(0, rows // PAD * OV, OV)
    strip = jnp.concatenate([strip[:, i : i + OV] for i in places], axis=0)
    zero = jnp.zeros_like(strip)
    middle = jnp.zeros((rows, pixels - 2 * OV), F32)
    left, right = jnp.where(tile == 1, strip, zero), jnp.where(tile == 0, strip, zero)
    out[0] = body + jnp.concatenate([left, middle, right], axis=1)
    own_terms = pick(*bodies, slice(rows, rows + 1), slice(0, per_device))
    other_terms = pick(*strips, slice(PAD, PAD + 1), slice(0, per_device))
    source[...] = (own_terms + other_terms) * term_scale


def call(kernel, outs, scratch=(), kind=F32, hbm=0, hub=False):
    def at_hub(*refs):
        src, half = lax.axis_index("src"), lax.axis_size("src") // 2
        pl.when((src == half - 1) | (src == half))(functools.partial(kernel, *refs))

    kinds = kind if isinstance(kind, list) else [kind] * len(outs)
    held = {"in_specs": [pl.BlockSpec(memory_space=pltpu.HBM)] * hbm} if hbm else {}
    return pl.pallas_call(
        at_hub if hub else kernel,
        out_shape=[jax.ShapeDtypeStruct(o, k) for o, k in zip(outs, kinds)],
        out_specs=[pl.BlockSpec(memory_space=pltpu.VMEM) for _ in outs],
        scratch_shapes=list(scratch),
        compiler_params=pltpu.CompilerParams(vmem_limit_bytes=VMEM_BUDGET),
        **held,
    )


def permute(x, wanted):
    shape = tuple(lax.axis_size(a) for a in ("src", "tile", "row"))
    devices = list(itertools.product(*(range(n) for n in shape)))
    pairs = dict(wanted)
    sources = [d for d in devices if d not in pairs]
    targets = [d for d in devices if d not in pairs.values()]

    def cost(pair):
        source, target = pair
        hops = abs(source[0] - target[0]) + abs(source[1] - target[1])
        return (source == target, hops, source, target)

    for source, target in sorted(itertools.product(sources, targets), key=cost):
        if source not in pairs and target not in pairs.values():
            pairs[source] = target
    flat = {d: n for n, d in enumerate(devices)}
    return lax.ppermute(x, ("src", "tile", "row"), [(flat[a], flat[b]) for a, b in pairs.items()])


def swap_rows(x):
    return lax.ppermute(x, "row", [(0, 1), (1, 0)])


def hub_shards(mask_windows, target_windows, pupil_bands, pupil_phase, source_weight):
    src_count, tile_count = lax.axis_size("src"), lax.axis_size("tile")
    rows, pixels = mask_windows.shape[1:]
    per_device, freqs = pupil_phase.shape[:2]
    sources = per_device * src_count
    half = src_count // 2
    count = half * per_device

    def chip(low, steps):
        return half - 1 - steps if low else half + steps

    cores = list(itertools.product(range(tile_count), range(2)))
    halves = (True, False)

    def to_hub(x, side, steps):
        return permute(
            x,
            {
                (chip(low, steps), t, c): (chip(low != (side == 1), 0), t, c)
                for low in halves
                for t, c in cores
            },
        )

    def phases_to_hub(x, steps):
        pairs = {}
        for low, tile in itertools.product(halves, range(tile_count)):
            if steps:
                pairs[chip(low, steps), tile, 0] = chip(low, 0), tile, 0
            pairs[chip(low, steps), tile, 1 if steps else 0] = chip(not low, 0), tile, 1
        return permute(x, pairs)

    pin = functools.partial(pltpu.with_memory_space_constraint, memory_space=pltpu.HBM)
    (message,) = call(
        fetch_kernel,
        [(2 * rows + PAD, pixels)],
        [
            pltpu.VMEM((per_device, 2, freqs), jnp.int32),
            pltpu.VMEM((1, per_device), F32),
            pltpu.SemaphoreType.DMA((4,)),
        ],
        hbm=4,
    )(
        pin(mask_windows),
        pin(target_windows),
        pin(pupil_bands.transpose(0, 2, 1)),
        pin(source_weight.reshape(1, per_device)),
    )
    order = (0, half, *range(1, half), *range(half + 1, 2 * half))
    blocks = [message] + [to_hub(message, d // half, d % half) for d in order[1:]]
    phases = [phases_to_hub(pupil_phase, n) for n in reversed(range(half))][::-1]
    *tables, phase = call(
        tables_kernel,
        [(2 * freqs, 2 * pixels)] * 2 + [(2 * pixels, 2 * freqs)] * 2 + [pupil_phase.shape],
        [pltpu.SemaphoreType.DMA],
        kind=[BF16] * 4 + [F32],
        hbm=1,
    )(pin(pupil_phase))

    spec, goal, meta = call(
        functools.partial(spectrum_kernel, half, order),
        [(2 * freqs, freqs), (src_count, rows, pixels), (half, PAD, pixels)],
        [pltpu.VMEM((2 * pixels, freqs), F32)],
        hub=True,
    )(*blocks, *tables)
    spec_other = swap_rows(spec)

    shape = (2 * freqs, count * freqs)
    part = pixels // 2
    outs = [(count, part, 2 * pixels), (part + part // 2, pixels)]
    *first, pupil, amp_h, amp_l = call(
        functools.partial(fields_kernel, per_device, sources, 0, half),
        [*outs, (count, 2 * freqs, freqs), shape, shape],
        [pltpu.VMEM((count * part, 2 * freqs), BF16)] * 2,
        kind=[F32, F32, F32, BF16, BF16],
        hub=True,
    )(phase, *phases, spec, spec_other, meta, goal, *tables)
    second = call(
        functools.partial(fields_kernel, per_device, sources, part, half),
        outs,
        [pltpu.VMEM((count * part, 2 * freqs), BF16)] * 2,
        hub=True,
    )(meta, goal, amp_h, amp_l, *tables)
    fields = [first, second]
    others = [swap_rows(light) for _, light in fields]
    grad = []
    for first_row, (field, light), other in zip((0, part), fields, others):
        grad = call(
            functools.partial(adjoint_kernel, per_device, sources, first_row, rows),
            [(2 * freqs + PAD, freqs)],
            [pltpu.VMEM((part, pixels), F32)]
            + [pltpu.VMEM((2 * part, count * freqs), BF16)] * 2,
            hub=True,
        )(*grad, field, pupil, light, other, meta, *tables)
    (grad,) = grad
    grad_other = swap_rows(grad)

    wide, narrow = (rows + PAD, pixels), (2 * PAD, max(freqs, rows // PAD * OV))
    own, pay_a, pay_b, pay_c, pay_d = call(
        functools.partial(window_kernel, half), [wide] * 3 + [narrow] * 2, hub=True
    )(grad, grad_other, *tables)
    low_end, low_hub, high_hub, high_end = chip(True, 1), chip(True, 0), chip(False, 0), chip(False, 1)

    def moves(*chips):
        return {
            (z, t, c): (to, t ^ tile_flip, c ^ core_flip)
            for z, to, tile_flip, core_flip in chips
            for t, c in cores
        }

    got_a = permute(
        pay_a,
        moves(
            (low_hub, low_end, 0, 1),
            (high_hub, high_hub, 1, 0),
            (low_end, high_end, 0, 0),
            (high_end, low_hub, 0, 0),
        ),
    )
    got_b = permute(pay_b, moves((high_hub, high_end, 0, 1), (high_end, high_hub, 0, 1)))
    got_c = permute(pay_c, moves((low_hub, low_end, 1, 1), (low_end, low_hub, 0, 1)))
    got_d = permute(
        pay_d,
        moves((low_hub, low_hub, 1, 0), (high_hub, high_end, 1, 1), (high_end, high_hub, 0, 1)),
    )
    out, source = call(
        functools.partial(place_kernel, half, 1.0 / (sources * pixels * tile_count)),
        [(1, rows, pixels), (1, per_device)],
    )(own, got_a, got_b, got_c, got_d)
    return out, source[0]


M = 256
K = 128


def with_halo(block, sides, width):
    for axis, dim in sides:
        count = lax.axis_size(axis)
        forward = [(i, i + 1) for i in range(count - 1)]
        backward = [(target, source) for source, target in forward]
        low = lax.ppermute(
            lax.slice_in_dim(block, block.shape[dim] - width, None, axis=dim), axis, forward
        )
        high = lax.ppermute(lax.slice_in_dim(block, 0, width, axis=dim), axis, backward)
        block = jnp.concatenate([low, block, high], axis=dim)
    return block


def matmul(left_op, right_op):
    return lax.dot_general(
        left_op,
        right_op,
        (((1,), (0,)), ((), ())),
        precision=lax.Precision.HIGHEST,
        preferred_element_type=jnp.float32,
    )


def matmul_tn(left_op, right_op):
    return lax.dot_general(
        left_op,
        right_op,
        (((0,), (0,)), ((), ())),
        precision=lax.Precision.HIGHEST,
        preferred_element_type=jnp.float32,
    )


def matmul_nt(left_op, right_op):
    return lax.dot_general(
        left_op,
        right_op,
        (((1,), (1,)), ((), ())),
        precision=lax.Precision.HIGHEST,
        preferred_element_type=jnp.float32,
    )


def wave_tables(positions):
    freq_index = jnp.arange(K, dtype=jnp.int32) - K // 2
    phase_index = freq_index[:, None] * positions[None, :] % M
    angles = 2.0 * math.pi / M * phase_index.astype(jnp.float32)
    return (jnp.cos(angles), jnp.sin(angles))


def shards(mask_windows, target_windows, pupil_bands, pupil_phase, source_weight):
    src_count = lax.axis_size("src")
    tile_count = lax.axis_size("tile")
    row_count = lax.axis_size("row")
    local_x = mask_windows.shape[1]
    per_device = pupil_phase.shape[0]
    sources = per_device * src_count
    field_scale = 1.0 / (M * K)
    src_id = lax.axis_index("src")
    row_id = lax.axis_index("row")
    x_start = (src_id * row_count + row_id) * local_x
    block_starts = (jnp.arange(src_count, dtype=jnp.int32) * row_count + row_id) * local_x
    row_set = (block_starts[:, None] + jnp.arange(local_x, dtype=jnp.int32)[None, :]).reshape(
        src_count * local_x
    )
    cos_all, sin_all = wave_tables(jnp.arange(M, dtype=jnp.int32))
    cos_set, sin_set = wave_tables(row_set)
    cos_own, sin_own = wave_tables(x_start + jnp.arange(local_x, dtype=jnp.int32))
    window = mask_windows[0]
    goal_block = target_windows[0]
    zero_spec = jnp.zeros((K, K), jnp.float32)
    shard_rows = lax.all_gather(window, ("src", "row"), axis=0, tiled=True)
    part_real = matmul_nt(shard_rows, cos_all)
    part_imag = -matmul_nt(shard_rows, sin_all)
    spec_real = matmul(cos_all, part_real) + matmul(sin_all, part_imag)
    spec_imag = matmul(cos_all, part_imag) - matmul(sin_all, part_real)
    freq_cols = jnp.arange(K, dtype=jnp.int32)
    inside = (freq_cols[None, None, :] >= pupil_bands[:, :, 0:1]) & (
        freq_cols[None, None, :] < pupil_bands[:, :, 1:2]
    )
    passing = inside.astype(jnp.float32)
    pupil_real = passing * jnp.cos(pupil_phase)
    pupil_imag = passing * jnp.sin(pupil_phase)
    amp_real = (pupil_real * spec_real - pupil_imag * spec_imag).reshape(per_device * K, K)
    amp_imag = (pupil_imag * spec_real + pupil_real * spec_imag).reshape(per_device * K, K)
    half_real = (matmul(amp_real, cos_all) - matmul(amp_imag, sin_all)).reshape(per_device, K, M)
    half_imag = (matmul(amp_real, sin_all) + matmul(amp_imag, cos_all)).reshape(per_device, K, M)
    weights = source_weight / sources

    def fields(pair_in):
        one_real, one_imag = pair_in
        field_real = field_scale * (matmul_tn(cos_set, one_real) - matmul_tn(sin_set, one_imag))
        field_imag = field_scale * (matmul_tn(cos_set, one_imag) + matmul_tn(sin_set, one_real))
        return (field_real, field_imag)

    stack_real, stack_imag = lax.map(fields, (half_real, half_imag))
    part_real = stack_real
    part_imag = stack_imag
    intensity = lax.psum_scatter(
        jnp.sum(weights[:, None, None] * (part_real * part_real + part_imag * part_imag), axis=0),
        "src",
        scatter_dimension=0,
        tiled=True,
    )
    resist = jax.nn.sigmoid(STEEPNESS * (intensity - THRESHOLD))
    cotangent = LOSS_SCALE * (resist - goal_block) * STEEPNESS * resist * (1.0 - resist)
    cotangent_all = lax.all_gather(cotangent, "src", axis=0, tiled=True)
    source_ids = jnp.arange(per_device, dtype=jnp.int32)

    def add_back(source_id, totals):
        grad_real, grad_imag, source_terms = totals
        field_real = stack_real[source_id]
        field_imag = stack_imag[source_id]
        back_scale = 2.0 * weights[source_id] * cotangent_all
        back_real = back_scale * field_real
        back_imag = back_scale * field_imag
        adj_real = matmul(cos_set, back_real) + matmul(sin_set, back_imag)
        adj_imag = matmul(cos_set, back_imag) - matmul(sin_set, back_real)
        amp_grad_real = field_scale * (matmul_nt(adj_real, cos_all) + matmul_nt(adj_imag, sin_all))
        amp_grad_imag = field_scale * (matmul_nt(adj_imag, cos_all) - matmul_nt(adj_real, sin_all))
        pass_real = pupil_real[source_id]
        pass_imag = pupil_imag[source_id]
        grad_real = grad_real + pass_real * amp_grad_real + pass_imag * amp_grad_imag
        grad_imag = grad_imag + pass_real * amp_grad_imag - pass_imag * amp_grad_real
        term_value = jnp.sum(cotangent_all * (field_real * field_real + field_imag * field_imag))
        source_terms = source_terms + jnp.where(source_ids == source_id, term_value, 0.0)
        return (grad_real, grad_imag, source_terms)

    grad_real, grad_imag, source_terms = lax.fori_loop(
        0, per_device, add_back, (zero_spec, zero_spec, jnp.zeros((per_device,), jnp.float32))
    )
    grad_real, grad_imag = lax.psum((grad_real, grad_imag), ("src", "row"))
    source_sum = lax.psum(source_terms, ("tile", "row"))
    source_grad = source_sum / (sources * M * tile_count)
    q_one = matmul(grad_real, cos_all) - matmul(grad_imag, sin_all)
    q_two = matmul(grad_real, sin_all) + matmul(grad_imag, cos_all)
    grad_block = matmul_tn(cos_own, q_one) - matmul_tn(sin_own, q_two)
    padded = with_halo(grad_block, (("tile", 1),), OV)
    from_below = padded[:, :OV]
    from_above = padded[:, M + OV :]
    middle = jnp.zeros((local_x, M - 2 * OV), jnp.float32)
    grad_block = grad_block + jnp.concatenate([from_below, middle, from_above], axis=1)
    return (grad_block[None], source_grad)


def hubs_serve(mesh, mask_windows, pupil_phase):
    src_count = mesh.shape["src"]
    pixels = mask_windows.shape[2]
    sources, freqs = pupil_phase.shape[0] // mesh.shape["parts"], pupil_phase.shape[1]
    per_device = sources // src_count
    held = sources // 2 * (2 * pixels * pixels + 4 * freqs * freqs) * 4
    return (
        mesh.shape["row"] == 2
        and mesh.shape["tile"] == 2
        and src_count % 2 == 0
        and src_count // 2 == 2
        and per_device < PAD
        and mask_windows.shape[1] // (2 * src_count) % 16 == 0
        and pixels & (pixels - 1) == 0
        and pixels >= 2 * freqs
        and held <= VMEM_BUDGET // 2
    )


def solution(mesh):
    def run(mask_windows, target_windows, pupil_bands, pupil_phase, source_weight):
        hubs = hubs_serve(mesh, mask_windows, pupil_phase)
        return jax.shard_map(
            hub_shards if hubs else shards,
            mesh=mesh,
            in_specs=(
                P(("parts", "tile"), ("src", "row"), None),
                P(("parts", "tile"), ("src", "row"), None),
                P(("parts", "src"), None, None),
                P(("parts", "src"), None, None),
                P(("parts", "src")),
            ),
            out_specs=(P(("parts", "tile"), ("src", "row"), None), P(("parts", "src"))),
            check_vma=False,
        )(mask_windows, target_windows, pupil_bands, pupil_phase, source_weight)

    return run
```

```python
import functools
import itertools
import math

import jax
import jax.numpy as jnp
from jax import lax
from jax.experimental import pallas as pl
from jax.experimental.pallas import tpu as pltpu
from jax.sharding import PartitionSpec as P

OV = 32
STEEPNESS = 20.0
THRESHOLD = 0.15
LOSS_SCALE = 32.0
PAD = 8
F32 = jnp.float32
BF16 = jnp.bfloat16
VMEM_BUDGET = 24 * 1024 * 1024


def split(a):
    high = a.astype(BF16)
    return high, (a - high.astype(F32)).astype(BF16)


def dot(a, b):
    return jnp.dot(a, b, preferred_element_type=F32)


def dot_nt(a, b):
    return lax.dot_general(a, b, (((1,), (1,)), ((), ())), preferred_element_type=F32)


def dot_tn(a, b):
    return lax.dot_general(a, b, (((0,), (0,)), ((), ())), preferred_element_type=F32)


def mm3(left, right, op=dot):
    (lh, ll), (rh, rl) = left, right
    return op(lh, rh) + (op(lh, rl) + op(ll, rh))


def sincos(phase):
    h = 0.5 * phase
    u = h * h
    s = 2.59043003e-06
    for coef in (-1.98008653e-04, 8.33289922e-03, -1.66666476e-01, 9.99999977e-01):
        s = s * u + coef
    s = s * h
    c = -2.60510764e-07
    for coef in (2.47601355e-05, -1.38883608e-03, 4.16666362e-02, -4.99999994e-01, 1.0):
        c = c * u + coef
    two_s = s + s
    return two_s * c, 1.0 - two_s * s


def block_of(src, side, steps, half):
    same = half - 1 - steps
    other = half + steps
    low = src < half
    return jnp.where(low, same if side == 0 else other, other if side == 0 else same)


def fetch_kernel(mask, goal, bands, weight, message, bands_in, weight_in, sems):
    rows = mask.shape[1]
    per_device, _, freqs = bands.shape
    message[2 * rows :] = jnp.zeros_like(message[2 * rows :])
    copies = [
        pltpu.make_async_copy(source, target, sems.at[n])
        for n, (source, target) in enumerate(
            (
                (mask.at[0], message.at[pl.ds(0, rows)]),
                (goal.at[0], message.at[pl.ds(rows, rows)]),
                (bands, bands_in),
                (weight, weight_in),
            )
        )
    ]
    for copy in copies:
        copy.start()
    for copy in copies:
        copy.wait()
    for i in range(per_device):
        for n in range(2):
            message[2 * rows + i : 2 * rows + i + 1, n * freqs : (n + 1) * freqs] = bands_in[
                i, n : n + 1, :
            ].astype(F32)
    line = 2 * rows + per_device
    message[line : line + 1, :per_device] = weight_in[...]


def tables_kernel(phase, fwd_h, fwd_l, adj_h, adj_l, held, sem):
    copy = pltpu.make_async_copy(phase, held, sem)
    copy.start()
    freqs, pixels = fwd_h.shape[0] // 2, fwd_h.shape[1] // 2

    def waves(shape, freq_dim):
        freq = lax.broadcasted_iota(jnp.int32, shape, freq_dim) - freqs // 2
        turn = freq * lax.broadcasted_iota(jnp.int32, shape, 1 - freq_dim)
        turn = ((turn + pixels // 2) & (pixels - 1)) - pixels // 2
        sin, cos = sincos((2.0 * math.pi / pixels) * turn.astype(F32))
        return split(cos), split(sin)

    (cos_h, cos_l), (sin_h, sin_l) = waves((freqs, pixels), 0)
    for table, cos, sin in ((fwd_h, cos_h, sin_h), (fwd_l, cos_l, sin_l)):
        table[:freqs, :pixels] = cos
        table[:freqs, pixels:] = sin
        table[freqs:, :pixels] = -sin
        table[freqs:, pixels:] = cos
    (cos_h, cos_l), (sin_h, sin_l) = waves((pixels, freqs), 1)
    for table, cos, sin in ((adj_h, cos_h, sin_h), (adj_l, cos_l, sin_l)):
        table[:pixels, :freqs] = cos
        table[:pixels, freqs:] = -sin
        table[pixels:, :freqs] = sin
        table[pixels:, freqs:] = cos
    copy.wait()


def spectrum_kernel(half, order, *refs):
    blocks = [refs[order.index(d)] for d in range(2 * half)]
    _, _, adj_h, adj_l, spec, goal, meta = refs[2 * half :]
    rows, pixels = goal.shape[1], goal.shape[2]
    freqs = spec.shape[1]
    src, row = lax.axis_index("src"), lax.axis_index("row")
    own = jnp.concatenate([b[:rows] for b in blocks], axis=0)
    waves = mm3(split(own), (adj_h[:pixels], adj_l[:pixels]))
    tables = []
    starts = []
    for d in range(2 * half):
        block = block_of(src, d // half, d % half, half)
        starts.append(pl.multiple_of((block * 2 + row) * rows, rows))
        goal[block] = blocks[d][rows : 2 * rows]
    for table in (adj_h, adj_l):
        tables.append(jnp.concatenate([table[pl.ds(n, rows), :] for n in starts], axis=0))
    for j in range(half):
        meta[j] = jnp.where(row == 0, blocks[j][2 * rows :], blocks[half + j][2 * rows :])
    both = mm3(tables, split(waves), dot_tn)
    spec[:freqs] = both[:freqs, :freqs] - both[freqs:, freqs:]
    spec[freqs:] = both[:freqs, freqs:] + both[freqs:, :freqs]


def weight_of(meta, source, per_device):
    j, i = divmod(source, per_device)
    return meta[j][per_device : per_device + 1, i : i + 1]


def fields_kernel(per_device, sources, first_row, slots, *refs):
    row = lax.axis_index("row")
    if first_row == 0:
        phase_own, *phases = refs[: slots + 1]
        spec_a, spec_b, meta, goal, fwd_h, fwd_l, adj_h, adj_l = refs[slots + 1 : -7]
        field, intensity, pupil, amp_h, amp_l, half_h, half_l = refs[-7:]
    else:
        meta, goal, amp_h, amp_l, fwd_h, fwd_l, adj_h, adj_l, field, intensity, *half_refs = refs
        half_h, half_l = half_refs
    rows, pixels = field.shape[1], intensity.shape[1]
    count, freqs = field.shape[0], amp_h.shape[1] // field.shape[0]
    if first_row == 0:
        spec = (spec_a[...] + spec_b[...]) * (1.0 / (pixels * freqs))
        spec_r, spec_i = spec[:freqs], spec[freqs:]
        column = lax.broadcasted_iota(jnp.int32, (freqs, freqs), 1).astype(F32)
        bounds = [meta[j].T for j in range(slots)]

    def amplitude(s):
        j, i = divmod(s, per_device)
        inside = (column >= bounds[j][:freqs, i : i + 1]) & (
            column < bounds[j][freqs : 2 * freqs, i : i + 1]
        )
        phase = phases[j][i]
        if j == 0:
            phase = jnp.where(row == 0, phase_own[i], phase)
        sin_p, cos_p = sincos(phase)
        pass_r = jnp.where(inside, cos_p, 0.0)
        pass_i = jnp.where(inside, sin_p, 0.0)
        pupil[s, :freqs] = pass_r
        pupil[s, freqs:] = pass_i
        lanes = slice(s * freqs, (s + 1) * freqs)
        for half, value in enumerate(
            (pass_r * spec_r - pass_i * spec_i, pass_i * spec_r + pass_r * spec_i)
        ):
            high, low = split(value)
            amp_h[half * freqs : (half + 1) * freqs, lanes] = high
            amp_l[half * freqs : (half + 1) * freqs, lanes] = low

    here, there = (slice(n, n + rows) for n in (first_row, pixels + first_row))
    waves = [jnp.concatenate([t[here], t[there]], axis=0) for t in (adj_h, adj_l)]
    for first in range(0, count, 2):
        members = range(first, min(first + 2, count))
        if first_row == 0:
            for s in members:
                amplitude(s)
        lanes = slice(first * freqs, (members[-1] + 1) * freqs)
        half = mm3(waves, (amp_h[:, lanes], amp_l[:, lanes]))
        for n, s in enumerate(members):
            for m in range(2):
                high, low = split(half[m * rows : (m + 1) * rows, n * freqs : (n + 1) * freqs])
                half_h[s * rows : (s + 1) * rows, m * freqs : (m + 1) * freqs] = high
                half_l[s * rows : (s + 1) * rows, m * freqs : (m + 1) * freqs] = low
    out = mm3((half_h[...], half_l[...]), (fwd_h[...], fwd_l[...]))
    total = jnp.zeros((rows, pixels), F32)
    for s in range(count):
        value = out[s * rows : (s + 1) * rows]
        field[s] = value
        out_r, out_i = value[:, :pixels], value[:, pixels:]
        weight = weight_of(meta, s, per_device) * (1.0 / sources)
        total = total + weight * (out_r * out_r + out_i * out_i)
    intensity[:rows] = total
    block = goal.shape[1]
    for n in range(rows // (2 * block)):
        place = rows + n * block
        intensity[place : place + block] = goal[first_row // (2 * block) + n]


def adjoint_kernel(per_device, sources, first_row, block, *refs):
    *before, field, pupil, light_a, light_b, meta = refs[:-8]
    fwd_h, fwd_l, adj_h, adj_l, grad, cot_ref, back_h, back_l = refs[-8:]
    rows, pixels = cot_ref.shape
    count, freqs = field.shape[0], grad.shape[1]
    row = lax.axis_index("row")
    for n in range(rows // block):
        here = slice(n * block, (n + 1) * block)
        place = slice(rows + n // 2 * block, rows + (n // 2 + 1) * block)
        goal = jnp.where(row == n % 2, light_a[place], light_b[place])
        intensity = light_a[here] + light_b[here]
        resist = 1.0 / (1.0 + jnp.exp(-STEEPNESS * (intensity - THRESHOLD)))
        cot_ref[here] = (LOSS_SCALE * STEEPNESS) * (resist - goal) * resist * (1.0 - resist)
    cot = cot_ref[...]
    line = lax.broadcasted_iota(jnp.int32, (PAD, freqs), 0)
    lane = lax.broadcasted_iota(jnp.int32, (PAD, freqs), 1)
    terms = jnp.zeros((PAD, freqs), F32)
    for s in range(count):
        value = field[s]
        back_r, back_i = cot * value[:, :pixels], cot * value[:, pixels:]
        power = back_r * value[:, :pixels] + back_i * value[:, pixels:]
        power = jnp.sum(jnp.sum(power, axis=0, keepdims=True), axis=1, keepdims=True)
        j, i = divmod(s, per_device)
        terms = terms + jnp.where((lane == i) & (line == j), power, 0.0)
        back = jnp.concatenate([back_r, back_i], axis=1)
        half = mm3(split(back), (adj_h[...], adj_l[...]))
        lanes = slice(s * freqs, (s + 1) * freqs)
        for n in range(2):
            high, low = split(half[:, n * freqs : (n + 1) * freqs])
            back_h[n * rows : (n + 1) * rows, lanes] = high
            back_l[n * rows : (n + 1) * rows, lanes] = low
    grad_r = jnp.zeros((freqs, freqs), F32)
    grad_i = jnp.zeros((freqs, freqs), F32)
    here, there = (slice(n, n + rows) for n in (first_row, pixels + first_row))
    waves = [jnp.concatenate([t[:, here], t[:, there]], axis=1) for t in (fwd_h, fwd_l)]
    for first in range(0, count, 2):
        members = range(first, min(first + 2, count))
        lanes = slice(first * freqs, (members[-1] + 1) * freqs)
        out = mm3(waves, (back_h[:, lanes], back_l[:, lanes]))
        for n, s in enumerate(members):
            lanes = slice(n * freqs, (n + 1) * freqs)
            weight = weight_of(meta, s, per_device) * (2.0 / (sources * pixels * freqs))
            pass_r, pass_i = weight * pupil[s, :freqs], weight * pupil[s, freqs:]
            out_r, out_i = out[:freqs, lanes], out[freqs:, lanes]
            grad_r = grad_r + (pass_r * out_r + pass_i * out_i)
            grad_i = grad_i + (pass_r * out_i - pass_i * out_r)
    for place, value in (
        (slice(0, freqs), grad_r),
        (slice(freqs, 2 * freqs), grad_i),
        (slice(2 * freqs, 2 * freqs + PAD), terms),
    ):
        grad[place] = value + before[0][place] if before else value


def window_kernel(half, grad_a, grad_b, fwd_h, fwd_l, adj_h, adj_l, own, *pays):
    pay_a, pay_b, pay_c, pay_d = pays
    rows, pixels = own.shape[0] - PAD, own.shape[1]
    freqs = grad_a.shape[1]
    src, row, tile = lax.axis_index("src"), lax.axis_index("row"), lax.axis_index("tile")
    total = grad_a[: 2 * freqs] + grad_b[: 2 * freqs]
    flat = split(jnp.concatenate([total[:freqs], total[freqs:]], axis=1))
    waves = mm3(flat, (fwd_h[...], fwd_l[...]))
    waves = jnp.concatenate([waves[:, :pixels], waves[:, pixels:]], axis=0)
    tables = []
    for table in (adj_h, adj_l):
        parts = []
        for steps, core in ((0, row), (1, 1 - row)):
            start = (block_of(src, 0, steps, half) * 2 + core) * rows
            parts.append(table[pl.ds(pl.multiple_of(start, rows), rows), :])
        tables.append(jnp.concatenate(parts, axis=0))
    window = mm3(tables, split(waves))
    terms = jnp.where(row == 0, grad_a[2 * freqs :], grad_b[2 * freqs :])
    near, far = window[:rows], window[rows:]

    def edge(block):
        return jnp.where(tile == 0, block[:, pixels - OV :], block[:, :OV])

    def put_rows(target, block, n):
        target[:rows] = block
        target[rows : rows + 1, :freqs] = terms[n : n + 1]

    def put_strip(target, block, n):
        block = edge(block)
        lines = range(0, rows, PAD)
        block = jnp.concatenate([block[i : i + PAD] for i in lines], axis=1)
        target[:PAD, : block.shape[1]] = block
        target[PAD : PAD + 1, :freqs] = terms[n : n + 1]

    put_rows(own, near, 0)
    put_rows(pay_b, far, 1)
    put_strip(pay_c, far, 1)

    @pl.when(src < half)
    def _():
        put_rows(pay_a, far, 1)
        put_strip(pay_d, near, 0)

    @pl.when(src >= half)
    def _():
        put_strip(pay_a, near, 0)
        put_strip(pay_d, far, 1)


def place_kernel(half, term_scale, own, got_a, got_b, got_c, got_d, out, source):
    rows, pixels = out.shape[1:]
    per_device = source.shape[1]
    src, tile = lax.axis_index("src"), lax.axis_index("tile")
    low, hub = src < half, (src == half - 1) | (src == half)

    def pick(low_hub, low_end, high_hub, high_end, *index):
        at_hub = jnp.where(low, low_hub[index], high_hub[index])
        at_end = jnp.where(low, low_end[index], high_end[index])
        return jnp.where(hub, at_hub, at_end)

    bodies, strips = (own, got_a, own, got_b), (got_d, got_c, got_a, got_d)
    body = pick(*bodies, slice(0, rows), slice(None))
    strip = pick(*strips, slice(0, PAD), slice(0, rows // PAD * OV))
    places = range(0, rows // PAD * OV, OV)
    strip = jnp.concatenate([strip[:, i : i + OV] for i in places], axis=0)
    zero = jnp.zeros_like(strip)
    middle = jnp.zeros((rows, pixels - 2 * OV), F32)
    left, right = jnp.where(tile == 1, strip, zero), jnp.where(tile == 0, strip, zero)
    out[0] = body + jnp.concatenate([left, middle, right], axis=1)
    own_terms = pick(*bodies, slice(rows, rows + 1), slice(0, per_device))
    other_terms = pick(*strips, slice(PAD, PAD + 1), slice(0, per_device))
    source[...] = (own_terms + other_terms) * term_scale


def call(kernel, outs, scratch=(), kind=F32, hbm=0, hub=False):
    def at_hub(*refs):
        src, half = lax.axis_index("src"), lax.axis_size("src") // 2
        pl.when((src == half - 1) | (src == half))(functools.partial(kernel, *refs))

    kinds = kind if isinstance(kind, list) else [kind] * len(outs)
    held = {"in_specs": [pl.BlockSpec(memory_space=pltpu.HBM)] * hbm} if hbm else {}
    return pl.pallas_call(
        at_hub if hub else kernel,
        out_shape=[jax.ShapeDtypeStruct(o, k) for o, k in zip(outs, kinds)],
        out_specs=[pl.BlockSpec(memory_space=pltpu.VMEM) for _ in outs],
        scratch_shapes=list(scratch),
        compiler_params=pltpu.CompilerParams(vmem_limit_bytes=VMEM_BUDGET),
        **held,
    )


def permute(x, wanted):
    shape = tuple(lax.axis_size(a) for a in ("src", "tile", "row"))
    devices = list(itertools.product(*(range(n) for n in shape)))
    pairs = dict(wanted)
    sources = [d for d in devices if d not in pairs]
    targets = [d for d in devices if d not in pairs.values()]

    def cost(pair):
        source, target = pair
        hops = abs(source[0] - target[0]) + abs(source[1] - target[1])
        return (source == target, hops, source, target)

    for source, target in sorted(itertools.product(sources, targets), key=cost):
        if source not in pairs and target not in pairs.values():
            pairs[source] = target
    flat = {d: n for n, d in enumerate(devices)}
    return lax.ppermute(x, ("src", "tile", "row"), [(flat[a], flat[b]) for a, b in pairs.items()])


def swap_rows(x):
    return lax.ppermute(x, "row", [(0, 1), (1, 0)])


def hub_shards(mask_windows, target_windows, pupil_bands, pupil_phase, source_weight):
    src_count, tile_count = lax.axis_size("src"), lax.axis_size("tile")
    rows, pixels = mask_windows.shape[1:]
    per_device, freqs = pupil_phase.shape[:2]
    sources = per_device * src_count
    half = src_count // 2
    count = half * per_device

    def chip(low, steps):
        return half - 1 - steps if low else half + steps

    cores = list(itertools.product(range(tile_count), range(2)))
    halves = (True, False)

    def to_hub(x, side, steps):
        return permute(
            x,
            {
                (chip(low, steps), t, c): (chip(low != (side == 1), 0), t, c)
                for low in halves
                for t, c in cores
            },
        )

    def phases_to_hub(x, steps):
        pairs = {}
        for low, tile in itertools.product(halves, range(tile_count)):
            if steps:
                pairs[chip(low, steps), tile, 0] = chip(low, 0), tile, 0
            pairs[chip(low, steps), tile, 1 if steps else 0] = chip(not low, 0), tile, 1
        return permute(x, pairs)

    pin = functools.partial(pltpu.with_memory_space_constraint, memory_space=pltpu.HBM)
    (message,) = call(
        fetch_kernel,
        [(2 * rows + PAD, pixels)],
        [
            pltpu.VMEM((per_device, 2, freqs), jnp.int32),
            pltpu.VMEM((1, per_device), F32),
            pltpu.SemaphoreType.DMA((4,)),
        ],
        hbm=4,
    )(
        pin(mask_windows),
        pin(target_windows),
        pin(pupil_bands.transpose(0, 2, 1)),
        pin(source_weight.reshape(1, per_device)),
    )
    order = (0, half, *range(1, half), *range(half + 1, 2 * half))
    blocks = [message] + [to_hub(message, d // half, d % half) for d in order[1:]]
    phases = [phases_to_hub(pupil_phase, n) for n in reversed(range(half))][::-1]
    *tables, phase = call(
        tables_kernel,
        [(2 * freqs, 2 * pixels)] * 2 + [(2 * pixels, 2 * freqs)] * 2 + [pupil_phase.shape],
        [pltpu.SemaphoreType.DMA],
        kind=[BF16] * 4 + [F32],
        hbm=1,
    )(pin(pupil_phase))

    spec, goal, meta = call(
        functools.partial(spectrum_kernel, half, order),
        [(2 * freqs, freqs), (src_count, rows, pixels), (half, PAD, pixels)],
        hub=True,
    )(*blocks, *tables)
    spec_other = swap_rows(spec)

    shape = (2 * freqs, count * freqs)
    part = pixels // 2
    outs = [(count, part, 2 * pixels), (part + part // 2, pixels)]
    *first, pupil, amp_h, amp_l = call(
        functools.partial(fields_kernel, per_device, sources, 0, half),
        [*outs, (count, 2 * freqs, freqs), shape, shape],
        [pltpu.VMEM((count * part, 2 * freqs), BF16)] * 2,
        kind=[F32, F32, F32, BF16, BF16],
        hub=True,
    )(phase, *phases, spec, spec_other, meta, goal, *tables)
    second = call(
        functools.partial(fields_kernel, per_device, sources, part, half),
        outs,
        [pltpu.VMEM((count * part, 2 * freqs), BF16)] * 2,
        hub=True,
    )(meta, goal, amp_h, amp_l, *tables)
    fields = [first, second]
    others = [swap_rows(light) for _, light in fields]
    grad = []
    for first_row, (field, light), other in zip((0, part), fields, others):
        grad = call(
            functools.partial(adjoint_kernel, per_device, sources, first_row, rows),
            [(2 * freqs + PAD, freqs)],
            [pltpu.VMEM((part, pixels), F32)]
            + [pltpu.VMEM((2 * part, count * freqs), BF16)] * 2,
            hub=True,
        )(*grad, field, pupil, light, other, meta, *tables)
    (grad,) = grad
    grad_other = swap_rows(grad)

    wide, narrow = (rows + PAD, pixels), (2 * PAD, max(freqs, rows // PAD * OV))
    own, pay_a, pay_b, pay_c, pay_d = call(
        functools.partial(window_kernel, half), [wide] * 3 + [narrow] * 2, hub=True
    )(grad, grad_other, *tables)
    low_end, low_hub, high_hub, high_end = chip(True, 1), chip(True, 0), chip(False, 0), chip(False, 1)

    def moves(*chips):
        return {
            (z, t, c): (to, t ^ tile_flip, c ^ core_flip)
            for z, to, tile_flip, core_flip in chips
            for t, c in cores
        }

    got_a = permute(
        pay_a,
        moves(
            (low_hub, low_end, 0, 1),
            (high_hub, high_hub, 1, 0),
            (low_end, high_end, 0, 0),
            (high_end, low_hub, 0, 0),
        ),
    )
    got_b = permute(pay_b, moves((high_hub, high_end, 0, 1), (high_end, high_hub, 0, 1)))
    got_c = permute(pay_c, moves((low_hub, low_end, 1, 1), (low_end, low_hub, 0, 1)))
    got_d = permute(
        pay_d,
        moves((low_hub, low_hub, 1, 0), (high_hub, high_end, 1, 1), (high_end, high_hub, 0, 1)),
    )
    out, source = call(
        functools.partial(place_kernel, half, 1.0 / (sources * pixels * tile_count)),
        [(1, rows, pixels), (1, per_device)],
    )(own, got_a, got_b, got_c, got_d)
    return out, source[0]


M = 256
K = 128


def with_halo(block, sides, width):
    for axis, dim in sides:
        count = lax.axis_size(axis)
        forward = [(i, i + 1) for i in range(count - 1)]
        backward = [(target, source) for source, target in forward]
        low = lax.ppermute(
            lax.slice_in_dim(block, block.shape[dim] - width, None, axis=dim), axis, forward
        )
        high = lax.ppermute(lax.slice_in_dim(block, 0, width, axis=dim), axis, backward)
        block = jnp.concatenate([low, block, high], axis=dim)
    return block


def matmul(left_op, right_op):
    return lax.dot_general(
        left_op,
        right_op,
        (((1,), (0,)), ((), ())),
        precision=lax.Precision.HIGHEST,
        preferred_element_type=jnp.float32,
    )


def matmul_tn(left_op, right_op):
    return lax.dot_general(
        left_op,
        right_op,
        (((0,), (0,)), ((), ())),
        precision=lax.Precision.HIGHEST,
        preferred_element_type=jnp.float32,
    )


def matmul_nt(left_op, right_op):
    return lax.dot_general(
        left_op,
        right_op,
        (((1,), (1,)), ((), ())),
        precision=lax.Precision.HIGHEST,
        preferred_element_type=jnp.float32,
    )


def wave_tables(positions):
    freq_index = jnp.arange(K, dtype=jnp.int32) - K // 2
    phase_index = freq_index[:, None] * positions[None, :] % M
    angles = 2.0 * math.pi / M * phase_index.astype(jnp.float32)
    return (jnp.cos(angles), jnp.sin(angles))


def shards(mask_windows, target_windows, pupil_bands, pupil_phase, source_weight):
    src_count = lax.axis_size("src")
    tile_count = lax.axis_size("tile")
    row_count = lax.axis_size("row")
    local_x = mask_windows.shape[1]
    per_device = pupil_phase.shape[0]
    sources = per_device * src_count
    field_scale = 1.0 / (M * K)
    src_id = lax.axis_index("src")
    row_id = lax.axis_index("row")
    x_start = (src_id * row_count + row_id) * local_x
    block_starts = (jnp.arange(src_count, dtype=jnp.int32) * row_count + row_id) * local_x
    row_set = (block_starts[:, None] + jnp.arange(local_x, dtype=jnp.int32)[None, :]).reshape(
        src_count * local_x
    )
    cos_all, sin_all = wave_tables(jnp.arange(M, dtype=jnp.int32))
    cos_set, sin_set = wave_tables(row_set)
    cos_own, sin_own = wave_tables(x_start + jnp.arange(local_x, dtype=jnp.int32))
    window = mask_windows[0]
    goal_block = target_windows[0]
    zero_spec = jnp.zeros((K, K), jnp.float32)
    shard_rows = lax.all_gather(window, ("src", "row"), axis=0, tiled=True)
    part_real = matmul_nt(shard_rows, cos_all)
    part_imag = -matmul_nt(shard_rows, sin_all)
    spec_real = matmul(cos_all, part_real) + matmul(sin_all, part_imag)
    spec_imag = matmul(cos_all, part_imag) - matmul(sin_all, part_real)
    freq_cols = jnp.arange(K, dtype=jnp.int32)
    inside = (freq_cols[None, None, :] >= pupil_bands[:, :, 0:1]) & (
        freq_cols[None, None, :] < pupil_bands[:, :, 1:2]
    )
    passing = inside.astype(jnp.float32)
    pupil_real = passing * jnp.cos(pupil_phase)
    pupil_imag = passing * jnp.sin(pupil_phase)
    amp_real = (pupil_real * spec_real - pupil_imag * spec_imag).reshape(per_device * K, K)
    amp_imag = (pupil_imag * spec_real + pupil_real * spec_imag).reshape(per_device * K, K)
    half_real = (matmul(amp_real, cos_all) - matmul(amp_imag, sin_all)).reshape(per_device, K, M)
    half_imag = (matmul(amp_real, sin_all) + matmul(amp_imag, cos_all)).reshape(per_device, K, M)
    weights = source_weight / sources

    def fields(pair_in):
        one_real, one_imag = pair_in
        field_real = field_scale * (matmul_tn(cos_set, one_real) - matmul_tn(sin_set, one_imag))
        field_imag = field_scale * (matmul_tn(cos_set, one_imag) + matmul_tn(sin_set, one_real))
        return (field_real, field_imag)

    stack_real, stack_imag = lax.map(fields, (half_real, half_imag))
    part_real = stack_real
    part_imag = stack_imag
    intensity = lax.psum_scatter(
        jnp.sum(weights[:, None, None] * (part_real * part_real + part_imag * part_imag), axis=0),
        "src",
        scatter_dimension=0,
        tiled=True,
    )
    resist = jax.nn.sigmoid(STEEPNESS * (intensity - THRESHOLD))
    cotangent = LOSS_SCALE * (resist - goal_block) * STEEPNESS * resist * (1.0 - resist)
    cotangent_all = lax.all_gather(cotangent, "src", axis=0, tiled=True)
    source_ids = jnp.arange(per_device, dtype=jnp.int32)

    def add_back(source_id, totals):
        grad_real, grad_imag, source_terms = totals
        field_real = stack_real[source_id]
        field_imag = stack_imag[source_id]
        back_scale = 2.0 * weights[source_id] * cotangent_all
        back_real = back_scale * field_real
        back_imag = back_scale * field_imag
        adj_real = matmul(cos_set, back_real) + matmul(sin_set, back_imag)
        adj_imag = matmul(cos_set, back_imag) - matmul(sin_set, back_real)
        amp_grad_real = field_scale * (matmul_nt(adj_real, cos_all) + matmul_nt(adj_imag, sin_all))
        amp_grad_imag = field_scale * (matmul_nt(adj_imag, cos_all) - matmul_nt(adj_real, sin_all))
        pass_real = pupil_real[source_id]
        pass_imag = pupil_imag[source_id]
        grad_real = grad_real + pass_real * amp_grad_real + pass_imag * amp_grad_imag
        grad_imag = grad_imag + pass_real * amp_grad_imag - pass_imag * amp_grad_real
        term_value = jnp.sum(cotangent_all * (field_real * field_real + field_imag * field_imag))
        source_terms = source_terms + jnp.where(source_ids == source_id, term_value, 0.0)
        return (grad_real, grad_imag, source_terms)

    grad_real, grad_imag, source_terms = lax.fori_loop(
        0, per_device, add_back, (zero_spec, zero_spec, jnp.zeros((per_device,), jnp.float32))
    )
    grad_real, grad_imag = lax.psum((grad_real, grad_imag), ("src", "row"))
    source_sum = lax.psum(source_terms, ("tile", "row"))
    source_grad = source_sum / (sources * M * tile_count)
    q_one = matmul(grad_real, cos_all) - matmul(grad_imag, sin_all)
    q_two = matmul(grad_real, sin_all) + matmul(grad_imag, cos_all)
    grad_block = matmul_tn(cos_own, q_one) - matmul_tn(sin_own, q_two)
    padded = with_halo(grad_block, (("tile", 1),), OV)
    from_below = padded[:, :OV]
    from_above = padded[:, M + OV :]
    middle = jnp.zeros((local_x, M - 2 * OV), jnp.float32)
    grad_block = grad_block + jnp.concatenate([from_below, middle, from_above], axis=1)
    return (grad_block[None], source_grad)


def hubs_serve(mesh, mask_windows, pupil_phase):
    src_count = mesh.shape["src"]
    pixels = mask_windows.shape[2]
    sources, freqs = pupil_phase.shape[0] // mesh.shape["parts"], pupil_phase.shape[1]
    per_device = sources // src_count
    held = sources // 2 * (2 * pixels * pixels + 4 * freqs * freqs) * 4
    return (
        mesh.shape["row"] == 2
        and mesh.shape["tile"] == 2
        and src_count % 2 == 0
        and src_count // 2 == 2
        and per_device < PAD
        and mask_windows.shape[1] // (2 * src_count) % 16 == 0
        and pixels & (pixels - 1) == 0
        and pixels >= 2 * freqs
        and held <= VMEM_BUDGET // 2
    )


def solution(mesh):
    def run(mask_windows, target_windows, pupil_bands, pupil_phase, source_weight):
        hubs = hubs_serve(mesh, mask_windows, pupil_phase)
        return jax.shard_map(
            hub_shards if hubs else shards,
            mesh=mesh,
            in_specs=(
                P(("parts", "tile"), ("src", "row"), None),
                P(("parts", "tile"), ("src", "row"), None),
                P(("parts", "src"), None, None),
                P(("parts", "src"), None, None),
                P(("parts", "src")),
            ),
            out_specs=(P(("parts", "tile"), ("src", "row"), None), P(("parts", "src"))),
            check_vma=False,
        )(mask_windows, target_windows, pupil_bands, pupil_phase, source_weight)

    return run
```

```python
import functools
import itertools
import math

import jax
import jax.numpy as jnp
from jax import lax
from jax.experimental import pallas as pl
from jax.experimental.pallas import tpu as pltpu
from jax.sharding import PartitionSpec as P

OV = 32
STEEPNESS = 20.0
THRESHOLD = 0.15
LOSS_SCALE = 32.0
PAD = 8
F32 = jnp.float32
BF16 = jnp.bfloat16
VMEM_BUDGET = 24 * 1024 * 1024


def split(a):
    high = a.astype(BF16)
    return high, (a - high.astype(F32)).astype(BF16)


def dot(a, b):
    return jnp.dot(a, b, preferred_element_type=F32)


def dot_nt(a, b):
    return lax.dot_general(a, b, (((1,), (1,)), ((), ())), preferred_element_type=F32)


def dot_tn(a, b):
    return lax.dot_general(a, b, (((0,), (0,)), ((), ())), preferred_element_type=F32)


def mm3(left, right, op=dot):
    (lh, ll), (rh, rl) = left, right
    return op(lh, rh) + (op(lh, rl) + op(ll, rh))


def sincos(phase):
    h = 0.5 * phase
    u = h * h
    s = 2.59043003e-06
    for coef in (-1.98008653e-04, 8.33289922e-03, -1.66666476e-01, 9.99999977e-01):
        s = s * u + coef
    s = s * h
    c = -2.60510764e-07
    for coef in (2.47601355e-05, -1.38883608e-03, 4.16666362e-02, -4.99999994e-01, 1.0):
        c = c * u + coef
    two_s = s + s
    return two_s * c, 1.0 - two_s * s


def block_of(src, side, steps, half):
    same = half - 1 - steps
    other = half + steps
    low = src < half
    return jnp.where(low, same if side == 0 else other, other if side == 0 else same)


def fetch_kernel(mask, goal, bands, weight, message, bands_in, weight_in, sems):
    rows = mask.shape[1]
    per_device, _, freqs = bands.shape
    message[2 * rows :] = jnp.zeros_like(message[2 * rows :])
    copies = [
        pltpu.make_async_copy(source, target, sems.at[n])
        for n, (source, target) in enumerate(
            (
                (mask.at[0], message.at[pl.ds(0, rows)]),
                (goal.at[0], message.at[pl.ds(rows, rows)]),
                (bands, bands_in),
                (weight, weight_in),
            )
        )
    ]
    for copy in copies:
        copy.start()
    for copy in copies:
        copy.wait()
    for i in range(per_device):
        for n in range(2):
            message[2 * rows + i : 2 * rows + i + 1, n * freqs : (n + 1) * freqs] = bands_in[
                i, n : n + 1, :
            ].astype(F32)
    line = 2 * rows + per_device
    message[line : line + 1, :per_device] = weight_in[...]


def tables_kernel(phase, fwd_h, fwd_l, adj_h, adj_l, held, sem):
    copy = pltpu.make_async_copy(phase, held, sem)
    copy.start()
    freqs, pixels = fwd_h.shape[0] // 2, fwd_h.shape[1] // 2

    def waves(shape, freq_dim):
        freq = lax.broadcasted_iota(jnp.int32, shape, freq_dim) - freqs // 2
        turn = freq * lax.broadcasted_iota(jnp.int32, shape, 1 - freq_dim)
        turn = ((turn + pixels // 2) & (pixels - 1)) - pixels // 2
        sin, cos = sincos((2.0 * math.pi / pixels) * turn.astype(F32))
        return split(cos), split(sin)

    (cos_h, cos_l), (sin_h, sin_l) = waves((freqs, pixels), 0)
    for table, cos, sin in ((fwd_h, cos_h, sin_h), (fwd_l, cos_l, sin_l)):
        table[:freqs, :pixels] = cos
        table[:freqs, pixels:] = sin
        table[freqs:, :pixels] = -sin
        table[freqs:, pixels:] = cos
    (cos_h, cos_l), (sin_h, sin_l) = waves((pixels, freqs), 1)
    for table, cos, sin in ((adj_h, cos_h, sin_h), (adj_l, cos_l, sin_l)):
        table[:pixels, :freqs] = cos
        table[:pixels, freqs:] = -sin
        table[pixels:, :freqs] = sin
        table[pixels:, freqs:] = cos
    copy.wait()


def spectrum_kernel(half, order, *refs):
    blocks = [refs[order.index(d)] for d in range(2 * half)]
    _, _, adj_h, adj_l, spec, goal, meta = refs[2 * half :]
    rows, pixels = goal.shape[1], goal.shape[2]
    freqs = spec.shape[1]
    src, row = lax.axis_index("src"), lax.axis_index("row")
    own = jnp.concatenate([b[:rows] for b in blocks], axis=0)
    waves = mm3(split(own), (adj_h[:pixels], adj_l[:pixels]))
    tables = []
    starts = []
    for d in range(2 * half):
        block = block_of(src, d // half, d % half, half)
        starts.append(pl.multiple_of((block * 2 + row) * rows, rows))
        goal[block] = blocks[d][rows : 2 * rows]
    for table in (adj_h, adj_l):
        tables.append(jnp.concatenate([table[pl.ds(n, rows), :] for n in starts], axis=0))
    for j in range(half):
        meta[j] = jnp.where(row == 0, blocks[j][2 * rows :], blocks[half + j][2 * rows :])
    both = mm3(tables, split(waves), dot_tn)
    spec[:freqs] = both[:freqs, :freqs] - both[freqs:, freqs:]
    spec[freqs:] = both[:freqs, freqs:] + both[freqs:, :freqs]


def weight_of(meta, source, per_device):
    j, i = divmod(source, per_device)
    return meta[j][per_device : per_device + 1, i : i + 1]


def fields_kernel(per_device, sources, first_row, slots, *refs):
    row = lax.axis_index("row")
    if first_row == 0:
        phase_own, *phases = refs[: slots + 1]
        spec_a, spec_b, meta, goal, fwd_h, fwd_l, adj_h, adj_l = refs[slots + 1 : -7]
        field, intensity, pupil, amp_h, amp_l, half_h, half_l = refs[-7:]
    else:
        meta, goal, amp_h, amp_l, fwd_h, fwd_l, adj_h, adj_l, field, intensity, *half_refs = refs
        half_h, half_l = half_refs
    rows, pixels = field.shape[1], intensity.shape[1]
    count, freqs = field.shape[0], amp_h.shape[1] // field.shape[0]
    if first_row == 0:
        spec = (spec_a[...] + spec_b[...]) * (1.0 / (pixels * freqs))
        spec_r, spec_i = spec[:freqs], spec[freqs:]
        column = lax.broadcasted_iota(jnp.int32, (freqs, freqs), 1).astype(F32)
        bounds = [meta[j].T for j in range(slots)]

    def amplitude(s):
        j, i = divmod(s, per_device)
        inside = (column >= bounds[j][:freqs, i : i + 1]) & (
            column < bounds[j][freqs : 2 * freqs, i : i + 1]
        )
        phase = phases[j][i]
        if j == 0:
            phase = jnp.where(row == 0, phase_own[i], phase)
        sin_p, cos_p = sincos(phase)
        pass_r = jnp.where(inside, cos_p, 0.0)
        pass_i = jnp.where(inside, sin_p, 0.0)
        pupil[s, :freqs] = pass_r
        pupil[s, freqs:] = pass_i
        lanes = slice(s * freqs, (s + 1) * freqs)
        for half, value in enumerate(
            (pass_r * spec_r - pass_i * spec_i, pass_i * spec_r + pass_r * spec_i)
        ):
            high, low = split(value)
            amp_h[half * freqs : (half + 1) * freqs, lanes] = high
            amp_l[half * freqs : (half + 1) * freqs, lanes] = low

    here, there = (slice(n, n + rows) for n in (first_row, pixels + first_row))
    waves = [jnp.concatenate([t[here], t[there]], axis=0) for t in (adj_h, adj_l)]
    for first in range(0, count, 2):
        members = range(first, min(first + 2, count))
        if first_row == 0:
            for s in members:
                amplitude(s)
        lanes = slice(first * freqs, (members[-1] + 1) * freqs)
        half = mm3(waves, (amp_h[:, lanes], amp_l[:, lanes]))
        for n, s in enumerate(members):
            for m in range(2):
                high, low = split(half[m * rows : (m + 1) * rows, n * freqs : (n + 1) * freqs])
                half_h[s * rows : (s + 1) * rows, m * freqs : (m + 1) * freqs] = high
                half_l[s * rows : (s + 1) * rows, m * freqs : (m + 1) * freqs] = low
    out = mm3((half_h[...], half_l[...]), (fwd_h[...], fwd_l[...]))
    total = jnp.zeros((rows, pixels), F32)
    for s in range(count):
        value = out[s * rows : (s + 1) * rows]
        field[s] = value
        out_r, out_i = value[:, :pixels], value[:, pixels:]
        weight = weight_of(meta, s, per_device) * (1.0 / sources)
        total = total + weight * (out_r * out_r + out_i * out_i)
    intensity[:rows] = total
    block = goal.shape[1]
    for n in range(rows // (2 * block)):
        place = rows + n * block
        intensity[place : place + block] = goal[first_row // (2 * block) + n]


def adjoint_kernel(per_device, sources, first_row, block, *refs):
    *before, field, pupil, light_a, light_b, meta = refs[:-8]
    fwd_h, fwd_l, adj_h, adj_l, grad, cot_ref, back_h, back_l = refs[-8:]
    rows, pixels = cot_ref.shape
    count, freqs = field.shape[0], grad.shape[1]
    row = lax.axis_index("row")
    for n in range(rows // block):
        here = slice(n * block, (n + 1) * block)
        place = slice(rows + n // 2 * block, rows + (n // 2 + 1) * block)
        goal = jnp.where(row == n % 2, light_a[place], light_b[place])
        intensity = light_a[here] + light_b[here]
        resist = 1.0 / (1.0 + jnp.exp(-STEEPNESS * (intensity - THRESHOLD)))
        cot_ref[here] = (LOSS_SCALE * STEEPNESS) * (resist - goal) * resist * (1.0 - resist)
    cot = cot_ref[...]
    line = lax.broadcasted_iota(jnp.int32, (PAD, freqs), 0)
    lane = lax.broadcasted_iota(jnp.int32, (PAD, freqs), 1)
    terms = jnp.zeros((PAD, freqs), F32)
    powers = []
    for s in range(count):
        value = field[s]
        back_r, back_i = cot * value[:, :pixels], cot * value[:, pixels:]
        power = back_r * value[:, :pixels] + back_i * value[:, pixels:]
        powers.append(jnp.sum(power, axis=0, keepdims=True))
        back = jnp.concatenate([back_r, back_i], axis=1)
        half = mm3(split(back), (adj_h[...], adj_l[...]))
        lanes = slice(s * freqs, (s + 1) * freqs)
        for n in range(2):
            high, low = split(half[:, n * freqs : (n + 1) * freqs])
            back_h[n * rows : (n + 1) * rows, lanes] = high
            back_l[n * rows : (n + 1) * rows, lanes] = low
    powers = jnp.sum(jnp.concatenate(powers, axis=0), axis=1, keepdims=True)
    for s in range(count):
        j, i = divmod(s, per_device)
        terms = terms + jnp.where((lane == i) & (line == j), powers[s : s + 1], 0.0)
    grad_r = jnp.zeros((freqs, freqs), F32)
    grad_i = jnp.zeros((freqs, freqs), F32)
    here, there = (slice(n, n + rows) for n in (first_row, pixels + first_row))
    waves = [jnp.concatenate([t[:, here], t[:, there]], axis=1) for t in (fwd_h, fwd_l)]
    for first in range(0, count, 2):
        members = range(first, min(first + 2, count))
        lanes = slice(first * freqs, (members[-1] + 1) * freqs)
        out = mm3(waves, (back_h[:, lanes], back_l[:, lanes]))
        for n, s in enumerate(members):
            lanes = slice(n * freqs, (n + 1) * freqs)
            weight = weight_of(meta, s, per_device) * (2.0 / (sources * pixels * freqs))
            pass_r, pass_i = weight * pupil[s, :freqs], weight * pupil[s, freqs:]
            out_r, out_i = out[:freqs, lanes], out[freqs:, lanes]
            grad_r = grad_r + (pass_r * out_r + pass_i * out_i)
            grad_i = grad_i + (pass_r * out_i - pass_i * out_r)
    for place, value in (
        (slice(0, freqs), grad_r),
        (slice(freqs, 2 * freqs), grad_i),
        (slice(2 * freqs, 2 * freqs + PAD), terms),
    ):
        grad[place] = value + before[0][place] if before else value


def window_kernel(half, grad_a, grad_b, fwd_h, fwd_l, adj_h, adj_l, own, *pays):
    pay_a, pay_b, pay_c, pay_d = pays
    rows, pixels = own.shape[0] - PAD, own.shape[1]
    freqs = grad_a.shape[1]
    src, row, tile = lax.axis_index("src"), lax.axis_index("row"), lax.axis_index("tile")
    total = grad_a[: 2 * freqs] + grad_b[: 2 * freqs]
    flat = split(jnp.concatenate([total[:freqs], total[freqs:]], axis=1))
    waves = mm3(flat, (fwd_h[...], fwd_l[...]))
    waves = jnp.concatenate([waves[:, :pixels], waves[:, pixels:]], axis=0)
    tables = []
    for table in (adj_h, adj_l):
        parts = []
        for steps, core in ((0, row), (1, 1 - row)):
            start = (block_of(src, 0, steps, half) * 2 + core) * rows
            parts.append(table[pl.ds(pl.multiple_of(start, rows), rows), :])
        tables.append(jnp.concatenate(parts, axis=0))
    window = mm3(tables, split(waves))
    terms = jnp.where(row == 0, grad_a[2 * freqs :], grad_b[2 * freqs :])
    near, far = window[:rows], window[rows:]

    def edge(block):
        return jnp.where(tile == 0, block[:, pixels - OV :], block[:, :OV])

    def put_rows(target, block, n):
        target[:rows] = block
        target[rows : rows + 1, :freqs] = terms[n : n + 1]

    def put_strip(target, block, n):
        block = edge(block)
        lines = range(0, rows, PAD)
        block = jnp.concatenate([block[i : i + PAD] for i in lines], axis=1)
        target[:PAD, : block.shape[1]] = block
        target[PAD : PAD + 1, :freqs] = terms[n : n + 1]

    put_rows(own, near, 0)
    put_rows(pay_b, far, 1)
    put_strip(pay_c, far, 1)

    @pl.when(src < half)
    def _():
        put_rows(pay_a, far, 1)
        put_strip(pay_d, near, 0)

    @pl.when(src >= half)
    def _():
        put_strip(pay_a, near, 0)
        put_strip(pay_d, far, 1)


def place_kernel(half, term_scale, own, got_a, got_b, got_c, got_d, out, source):
    rows, pixels = out.shape[1:]
    per_device = source.shape[1]
    src, tile = lax.axis_index("src"), lax.axis_index("tile")
    low, hub = src < half, (src == half - 1) | (src == half)

    def place(at, rows_from, strips_from):
        @pl.when(at)
        def _():
            strip = strips_from[:PAD, : rows // PAD * OV]
            places = range(0, rows // PAD * OV, OV)
            strip = jnp.concatenate([strip[:, i : i + OV] for i in places], axis=0)
            zero = jnp.zeros_like(strip)
            middle = jnp.zeros((rows, pixels - 2 * OV), F32)
            left, right = jnp.where(tile == 1, strip, zero), jnp.where(tile == 0, strip, zero)
            out[0] = rows_from[:rows] + jnp.concatenate([left, middle, right], axis=1)
            own_terms = rows_from[rows : rows + 1, :per_device]
            source[...] = (own_terms + strips_from[PAD : PAD + 1, :per_device]) * term_scale

    place(low & hub, own, got_d)
    place(low & ~hub, got_a, got_c)
    place(~low & hub, own, got_a)
    place(~(low | hub), got_b, got_d)


def call(kernel, outs, scratch=(), kind=F32, hbm=0, hub=False):
    def at_hub(*refs):
        src, half = lax.axis_index("src"), lax.axis_size("src") // 2
        pl.when((src == half - 1) | (src == half))(functools.partial(kernel, *refs))

    kinds = kind if isinstance(kind, list) else [kind] * len(outs)
    held = {"in_specs": [pl.BlockSpec(memory_space=pltpu.HBM)] * hbm} if hbm else {}
    return pl.pallas_call(
        at_hub if hub else kernel,
        out_shape=[jax.ShapeDtypeStruct(o, k) for o, k in zip(outs, kinds)],
        out_specs=[pl.BlockSpec(memory_space=pltpu.VMEM) for _ in outs],
        scratch_shapes=list(scratch),
        compiler_params=pltpu.CompilerParams(vmem_limit_bytes=VMEM_BUDGET),
        **held,
    )


def permute(x, wanted):
    shape = tuple(lax.axis_size(a) for a in ("src", "tile", "row"))
    devices = list(itertools.product(*(range(n) for n in shape)))
    pairs = dict(wanted)
    sources = [d for d in devices if d not in pairs]
    targets = [d for d in devices if d not in pairs.values()]

    def cost(pair):
        source, target = pair
        hops = abs(source[0] - target[0]) + abs(source[1] - target[1])
        return (source == target, hops, source, target)

    for source, target in sorted(itertools.product(sources, targets), key=cost):
        if source not in pairs and target not in pairs.values():
            pairs[source] = target
    flat = {d: n for n, d in enumerate(devices)}
    return lax.ppermute(x, ("src", "tile", "row"), [(flat[a], flat[b]) for a, b in pairs.items()])


def swap_rows(x):
    return lax.ppermute(x, "row", [(0, 1), (1, 0)])


def hub_shards(mask_windows, target_windows, pupil_bands, pupil_phase, source_weight):
    src_count, tile_count = lax.axis_size("src"), lax.axis_size("tile")
    rows, pixels = mask_windows.shape[1:]
    per_device, freqs = pupil_phase.shape[:2]
    sources = per_device * src_count
    half = src_count // 2
    count = half * per_device

    def chip(low, steps):
        return half - 1 - steps if low else half + steps

    cores = list(itertools.product(range(tile_count), range(2)))
    halves = (True, False)

    def to_hub(x, side, steps):
        return permute(
            x,
            {
                (chip(low, steps), t, c): (chip(low != (side == 1), 0), t, c)
                for low in halves
                for t, c in cores
            },
        )

    def phases_to_hub(x, steps):
        pairs = {}
        for low, tile in itertools.product(halves, range(tile_count)):
            if steps:
                pairs[chip(low, steps), tile, 0] = chip(low, 0), tile, 0
            pairs[chip(low, steps), tile, 1 if steps else 0] = chip(not low, 0), tile, 1
        return permute(x, pairs)

    pin = functools.partial(pltpu.with_memory_space_constraint, memory_space=pltpu.HBM)
    (message,) = call(
        fetch_kernel,
        [(2 * rows + PAD, pixels)],
        [
            pltpu.VMEM((per_device, 2, freqs), jnp.int32),
            pltpu.VMEM((1, per_device), F32),
            pltpu.SemaphoreType.DMA((4,)),
        ],
        hbm=4,
    )(
        pin(mask_windows),
        pin(target_windows),
        pin(pupil_bands.transpose(0, 2, 1)),
        pin(source_weight.reshape(1, per_device)),
    )
    order = (0, half, *range(1, half), *range(half + 1, 2 * half))
    blocks = [message] + [to_hub(message, d // half, d % half) for d in order[1:]]
    phases = [phases_to_hub(pupil_phase, n) for n in reversed(range(half))][::-1]
    *tables, phase = call(
        tables_kernel,
        [(2 * freqs, 2 * pixels)] * 2 + [(2 * pixels, 2 * freqs)] * 2 + [pupil_phase.shape],
        [pltpu.SemaphoreType.DMA],
        kind=[BF16] * 4 + [F32],
        hbm=1,
    )(pin(pupil_phase))

    spec, goal, meta = call(
        functools.partial(spectrum_kernel, half, order),
        [(2 * freqs, freqs), (src_count, rows, pixels), (half, PAD, pixels)],
        hub=True,
    )(*blocks, *tables)
    spec_other = swap_rows(spec)

    shape = (2 * freqs, count * freqs)
    part = pixels // 2
    outs = [(count, part, 2 * pixels), (part + part // 2, pixels)]
    *first, pupil, amp_h, amp_l = call(
        functools.partial(fields_kernel, per_device, sources, 0, half),
        [*outs, (count, 2 * freqs, freqs), shape, shape],
        [pltpu.VMEM((count * part, 2 * freqs), BF16)] * 2,
        kind=[F32, F32, F32, BF16, BF16],
        hub=True,
    )(phase, *phases, spec, spec_other, meta, goal, *tables)
    second = call(
        functools.partial(fields_kernel, per_device, sources, part, half),
        outs,
        [pltpu.VMEM((count * part, 2 * freqs), BF16)] * 2,
        hub=True,
    )(meta, goal, amp_h, amp_l, *tables)
    fields = [first, second]
    others = [swap_rows(light) for _, light in fields]
    grad = []
    for first_row, (field, light), other in zip((0, part), fields, others):
        grad = call(
            functools.partial(adjoint_kernel, per_device, sources, first_row, rows),
            [(2 * freqs + PAD, freqs)],
            [pltpu.VMEM((part, pixels), F32)]
            + [pltpu.VMEM((2 * part, count * freqs), BF16)] * 2,
            hub=True,
        )(*grad, field, pupil, light, other, meta, *tables)
    (grad,) = grad
    grad_other = swap_rows(grad)

    wide, narrow = (rows + PAD, pixels), (2 * PAD, max(freqs, rows // PAD * OV))
    own, pay_a, pay_b, pay_c, pay_d = call(
        functools.partial(window_kernel, half), [wide] * 3 + [narrow] * 2, hub=True
    )(grad, grad_other, *tables)
    low_end, low_hub, high_hub, high_end = chip(True, 1), chip(True, 0), chip(False, 0), chip(False, 1)

    def moves(*chips):
        return {
            (z, t, c): (to, t ^ tile_flip, c ^ core_flip)
            for z, to, tile_flip, core_flip in chips
            for t, c in cores
        }

    got_a = permute(
        pay_a,
        moves(
            (low_hub, low_end, 0, 1),
            (high_hub, high_hub, 1, 0),
            (low_end, high_end, 0, 0),
            (high_end, low_hub, 0, 0),
        ),
    )
    got_b = permute(pay_b, moves((high_hub, high_end, 0, 1), (high_end, high_hub, 0, 1)))
    got_c = permute(pay_c, moves((low_hub, low_end, 1, 1), (low_end, low_hub, 0, 1)))
    got_d = permute(
        pay_d,
        moves((low_hub, low_hub, 1, 0), (high_hub, high_end, 1, 1), (high_end, high_hub, 0, 1)),
    )
    out, source = call(
        functools.partial(place_kernel, half, 1.0 / (sources * pixels * tile_count)),
        [(1, rows, pixels), (1, per_device)],
    )(own, got_a, got_b, got_c, got_d)
    return out, source[0]


M = 256
K = 128


def with_halo(block, sides, width):
    for axis, dim in sides:
        count = lax.axis_size(axis)
        forward = [(i, i + 1) for i in range(count - 1)]
        backward = [(target, source) for source, target in forward]
        low = lax.ppermute(
            lax.slice_in_dim(block, block.shape[dim] - width, None, axis=dim), axis, forward
        )
        high = lax.ppermute(lax.slice_in_dim(block, 0, width, axis=dim), axis, backward)
        block = jnp.concatenate([low, block, high], axis=dim)
    return block


def matmul(left_op, right_op):
    return lax.dot_general(
        left_op,
        right_op,
        (((1,), (0,)), ((), ())),
        precision=lax.Precision.HIGHEST,
        preferred_element_type=jnp.float32,
    )


def matmul_tn(left_op, right_op):
    return lax.dot_general(
        left_op,
        right_op,
        (((0,), (0,)), ((), ())),
        precision=lax.Precision.HIGHEST,
        preferred_element_type=jnp.float32,
    )


def matmul_nt(left_op, right_op):
    return lax.dot_general(
        left_op,
        right_op,
        (((1,), (1,)), ((), ())),
        precision=lax.Precision.HIGHEST,
        preferred_element_type=jnp.float32,
    )


def wave_tables(positions):
    freq_index = jnp.arange(K, dtype=jnp.int32) - K // 2
    phase_index = freq_index[:, None] * positions[None, :] % M
    angles = 2.0 * math.pi / M * phase_index.astype(jnp.float32)
    return (jnp.cos(angles), jnp.sin(angles))


def shards(mask_windows, target_windows, pupil_bands, pupil_phase, source_weight):
    src_count = lax.axis_size("src")
    tile_count = lax.axis_size("tile")
    row_count = lax.axis_size("row")
    local_x = mask_windows.shape[1]
    per_device = pupil_phase.shape[0]
    sources = per_device * src_count
    field_scale = 1.0 / (M * K)
    src_id = lax.axis_index("src")
    row_id = lax.axis_index("row")
    x_start = (src_id * row_count + row_id) * local_x
    block_starts = (jnp.arange(src_count, dtype=jnp.int32) * row_count + row_id) * local_x
    row_set = (block_starts[:, None] + jnp.arange(local_x, dtype=jnp.int32)[None, :]).reshape(
        src_count * local_x
    )
    cos_all, sin_all = wave_tables(jnp.arange(M, dtype=jnp.int32))
    cos_set, sin_set = wave_tables(row_set)
    cos_own, sin_own = wave_tables(x_start + jnp.arange(local_x, dtype=jnp.int32))
    window = mask_windows[0]
    goal_block = target_windows[0]
    zero_spec = jnp.zeros((K, K), jnp.float32)
    shard_rows = lax.all_gather(window, ("src", "row"), axis=0, tiled=True)
    part_real = matmul_nt(shard_rows, cos_all)
    part_imag = -matmul_nt(shard_rows, sin_all)
    spec_real = matmul(cos_all, part_real) + matmul(sin_all, part_imag)
    spec_imag = matmul(cos_all, part_imag) - matmul(sin_all, part_real)
    freq_cols = jnp.arange(K, dtype=jnp.int32)
    inside = (freq_cols[None, None, :] >= pupil_bands[:, :, 0:1]) & (
        freq_cols[None, None, :] < pupil_bands[:, :, 1:2]
    )
    passing = inside.astype(jnp.float32)
    pupil_real = passing * jnp.cos(pupil_phase)
    pupil_imag = passing * jnp.sin(pupil_phase)
    amp_real = (pupil_real * spec_real - pupil_imag * spec_imag).reshape(per_device * K, K)
    amp_imag = (pupil_imag * spec_real + pupil_real * spec_imag).reshape(per_device * K, K)
    half_real = (matmul(amp_real, cos_all) - matmul(amp_imag, sin_all)).reshape(per_device, K, M)
    half_imag = (matmul(amp_real, sin_all) + matmul(amp_imag, cos_all)).reshape(per_device, K, M)
    weights = source_weight / sources

    def fields(pair_in):
        one_real, one_imag = pair_in
        field_real = field_scale * (matmul_tn(cos_set, one_real) - matmul_tn(sin_set, one_imag))
        field_imag = field_scale * (matmul_tn(cos_set, one_imag) + matmul_tn(sin_set, one_real))
        return (field_real, field_imag)

    stack_real, stack_imag = lax.map(fields, (half_real, half_imag))
    part_real = stack_real
    part_imag = stack_imag
    intensity = lax.psum_scatter(
        jnp.sum(weights[:, None, None] * (part_real * part_real + part_imag * part_imag), axis=0),
        "src",
        scatter_dimension=0,
        tiled=True,
    )
    resist = jax.nn.sigmoid(STEEPNESS * (intensity - THRESHOLD))
    cotangent = LOSS_SCALE * (resist - goal_block) * STEEPNESS * resist * (1.0 - resist)
    cotangent_all = lax.all_gather(cotangent, "src", axis=0, tiled=True)
    source_ids = jnp.arange(per_device, dtype=jnp.int32)

    def add_back(source_id, totals):
        grad_real, grad_imag, source_terms = totals
        field_real = stack_real[source_id]
        field_imag = stack_imag[source_id]
        back_scale = 2.0 * weights[source_id] * cotangent_all
        back_real = back_scale * field_real
        back_imag = back_scale * field_imag
        adj_real = matmul(cos_set, back_real) + matmul(sin_set, back_imag)
        adj_imag = matmul(cos_set, back_imag) - matmul(sin_set, back_real)
        amp_grad_real = field_scale * (matmul_nt(adj_real, cos_all) + matmul_nt(adj_imag, sin_all))
        amp_grad_imag = field_scale * (matmul_nt(adj_imag, cos_all) - matmul_nt(adj_real, sin_all))
        pass_real = pupil_real[source_id]
        pass_imag = pupil_imag[source_id]
        grad_real = grad_real + pass_real * amp_grad_real + pass_imag * amp_grad_imag
        grad_imag = grad_imag + pass_real * amp_grad_imag - pass_imag * amp_grad_real
        term_value = jnp.sum(cotangent_all * (field_real * field_real + field_imag * field_imag))
        source_terms = source_terms + jnp.where(source_ids == source_id, term_value, 0.0)
        return (grad_real, grad_imag, source_terms)

    grad_real, grad_imag, source_terms = lax.fori_loop(
        0, per_device, add_back, (zero_spec, zero_spec, jnp.zeros((per_device,), jnp.float32))
    )
    grad_real, grad_imag = lax.psum((grad_real, grad_imag), ("src", "row"))
    source_sum = lax.psum(source_terms, ("tile", "row"))
    source_grad = source_sum / (sources * M * tile_count)
    q_one = matmul(grad_real, cos_all) - matmul(grad_imag, sin_all)
    q_two = matmul(grad_real, sin_all) + matmul(grad_imag, cos_all)
    grad_block = matmul_tn(cos_own, q_one) - matmul_tn(sin_own, q_two)
    padded = with_halo(grad_block, (("tile", 1),), OV)
    from_below = padded[:, :OV]
    from_above = padded[:, M + OV :]
    middle = jnp.zeros((local_x, M - 2 * OV), jnp.float32)
    grad_block = grad_block + jnp.concatenate([from_below, middle, from_above], axis=1)
    return (grad_block[None], source_grad)


def hubs_serve(mesh, mask_windows, pupil_phase):
    src_count = mesh.shape["src"]
    pixels = mask_windows.shape[2]
    sources, freqs = pupil_phase.shape[0] // mesh.shape["parts"], pupil_phase.shape[1]
    per_device = sources // src_count
    held = sources // 2 * (2 * pixels * pixels + 4 * freqs * freqs) * 4
    return (
        mesh.shape["row"] == 2
        and mesh.shape["tile"] == 2
        and src_count % 2 == 0
        and src_count // 2 == 2
        and per_device < PAD
        and mask_windows.shape[1] // (2 * src_count) % 16 == 0
        and pixels & (pixels - 1) == 0
        and pixels >= 2 * freqs
        and held <= VMEM_BUDGET // 2
    )


def solution(mesh):
    def run(mask_windows, target_windows, pupil_bands, pupil_phase, source_weight):
        hubs = hubs_serve(mesh, mask_windows, pupil_phase)
        return jax.shard_map(
            hub_shards if hubs else shards,
            mesh=mesh,
            in_specs=(
                P(("parts", "tile"), ("src", "row"), None),
                P(("parts", "tile"), ("src", "row"), None),
                P(("parts", "src"), None, None),
                P(("parts", "src"), None, None),
                P(("parts", "src")),
            ),
            out_specs=(P(("parts", "tile"), ("src", "row"), None), P(("parts", "src"))),
            check_vma=False,
        )(mask_windows, target_windows, pupil_bands, pupil_phase, source_weight)

    return run
```

```python
import functools
import itertools
import math

import jax
import jax.numpy as jnp
from jax import lax
from jax.experimental import pallas as pl
from jax.experimental.pallas import tpu as pltpu
from jax.sharding import PartitionSpec as P

OV = 32
STEEPNESS = 20.0
THRESHOLD = 0.15
LOSS_SCALE = 32.0
PAD = 8
F32 = jnp.float32
BF16 = jnp.bfloat16
VMEM_BUDGET = 24 * 1024 * 1024


def split(a):
    high = a.astype(BF16)
    return high, (a - high.astype(F32)).astype(BF16)


def dot(a, b):
    return jnp.dot(a, b, preferred_element_type=F32)


def dot_nt(a, b):
    return lax.dot_general(a, b, (((1,), (1,)), ((), ())), preferred_element_type=F32)


def dot_tn(a, b):
    return lax.dot_general(a, b, (((0,), (0,)), ((), ())), preferred_element_type=F32)


def mm3(left, right, op=dot):
    (lh, ll), (rh, rl) = left, right
    return op(lh, rh) + (op(lh, rl) + op(ll, rh))


def sincos(phase):
    h = 0.5 * phase
    u = h * h
    s = 2.59043003e-06
    for coef in (-1.98008653e-04, 8.33289922e-03, -1.66666476e-01, 9.99999977e-01):
        s = s * u + coef
    s = s * h
    c = -2.60510764e-07
    for coef in (2.47601355e-05, -1.38883608e-03, 4.16666362e-02, -4.99999994e-01, 1.0):
        c = c * u + coef
    two_s = s + s
    return two_s * c, 1.0 - two_s * s


def block_of(src, side, steps, half):
    same = half - 1 - steps
    other = half + steps
    low = src < half
    return jnp.where(low, same if side == 0 else other, other if side == 0 else same)


def fetch_kernel(mask, goal, bands, weight, message, bands_in, weight_in, sems):
    rows = mask.shape[1]
    per_device, _, freqs = bands.shape
    message[2 * rows :] = jnp.zeros_like(message[2 * rows :])
    copies = [
        pltpu.make_async_copy(source, target, sems.at[n])
        for n, (source, target) in enumerate(
            (
                (mask.at[0], message.at[pl.ds(0, rows)]),
                (goal.at[0], message.at[pl.ds(rows, rows)]),
                (bands, bands_in),
                (weight, weight_in),
            )
        )
    ]
    for copy in copies:
        copy.start()
    for copy in copies:
        copy.wait()
    for i in range(per_device):
        for n in range(2):
            message[2 * rows + i : 2 * rows + i + 1, n * freqs : (n + 1) * freqs] = bands_in[
                i, n : n + 1, :
            ].astype(F32)
    line = 2 * rows + per_device
    message[line : line + 1, :per_device] = weight_in[...]


def tables_kernel(phase, fwd_h, fwd_l, adj_h, adj_l, held, sem):
    copy = pltpu.make_async_copy(phase, held, sem)
    copy.start()
    freqs, pixels = fwd_h.shape[0] // 2, fwd_h.shape[1] // 2

    def waves(shape, freq_dim):
        freq = lax.broadcasted_iota(jnp.int32, shape, freq_dim) - freqs // 2
        turn = freq * lax.broadcasted_iota(jnp.int32, shape, 1 - freq_dim)
        turn = ((turn + pixels // 2) & (pixels - 1)) - pixels // 2
        sin, cos = sincos((2.0 * math.pi / pixels) * turn.astype(F32))
        return split(cos), split(sin)

    (cos_h, cos_l), (sin_h, sin_l) = waves((freqs, pixels), 0)
    for table, cos, sin in ((fwd_h, cos_h, sin_h), (fwd_l, cos_l, sin_l)):
        table[:freqs, :pixels] = cos
        table[:freqs, pixels:] = sin
        table[freqs:, :pixels] = -sin
        table[freqs:, pixels:] = cos
    (cos_h, cos_l), (sin_h, sin_l) = waves((pixels, freqs), 1)
    for table, cos, sin in ((adj_h, cos_h, sin_h), (adj_l, cos_l, sin_l)):
        table[:pixels, :freqs] = cos
        table[:pixels, freqs:] = -sin
        table[pixels:, :freqs] = sin
        table[pixels:, freqs:] = cos
    copy.wait()


def spectrum_kernel(half, order, *refs):
    blocks = [refs[order.index(d)] for d in range(2 * half)]
    _, _, adj_h, adj_l, spec, goal, meta = refs[2 * half :]
    rows, pixels = goal.shape[1], goal.shape[2]
    freqs = spec.shape[1]
    src, row = lax.axis_index("src"), lax.axis_index("row")
    own = jnp.concatenate([b[:rows] for b in blocks], axis=0)
    waves = mm3(split(own), (adj_h[:pixels], adj_l[:pixels]))
    tables = []
    starts = []
    for d in range(2 * half):
        block = block_of(src, d // half, d % half, half)
        starts.append(pl.multiple_of((block * 2 + row) * rows, rows))
        goal[block] = blocks[d][rows : 2 * rows]
    for table in (adj_h, adj_l):
        tables.append(jnp.concatenate([table[pl.ds(n, rows), :] for n in starts], axis=0))
    for j in range(half):
        meta[j] = jnp.where(row == 0, blocks[j][2 * rows :], blocks[half + j][2 * rows :])
    both = mm3(tables, split(waves), dot_tn)
    spec[:freqs] = both[:freqs, :freqs] - both[freqs:, freqs:]
    spec[freqs:] = both[:freqs, freqs:] + both[freqs:, :freqs]


def weight_of(meta, source, per_device):
    j, i = divmod(source, per_device)
    return meta[j][per_device : per_device + 1, i : i + 1]


def fields_kernel(per_device, sources, first_row, slots, *refs):
    row = lax.axis_index("row")
    if first_row == 0:
        phase_own, *phases = refs[: slots + 1]
        spec_a, spec_b, meta, goal, fwd_h, fwd_l, adj_h, adj_l = refs[slots + 1 : -7]
        field, intensity, pupil, amp_h, amp_l, half_h, half_l = refs[-7:]
    else:
        meta, goal, amp_h, amp_l, fwd_h, fwd_l, adj_h, adj_l, field, intensity, *half_refs = refs
        half_h, half_l = half_refs
    rows, pixels = field.shape[1], intensity.shape[1]
    count, freqs = field.shape[0], amp_h.shape[1] // field.shape[0]
    if first_row == 0:
        spec = (spec_a[...] + spec_b[...]) * (1.0 / (pixels * freqs))
        spec_r, spec_i = spec[:freqs], spec[freqs:]
        column = lax.broadcasted_iota(jnp.int32, (freqs, freqs), 1).astype(F32)
        bounds = [meta[j].T for j in range(slots)]

    def amplitude(s):
        j, i = divmod(s, per_device)
        inside = (column >= bounds[j][:freqs, i : i + 1]) & (
            column < bounds[j][freqs : 2 * freqs, i : i + 1]
        )
        phase = phases[j][i]
        if j == 0:
            phase = jnp.where(row == 0, phase_own[i], phase)
        sin_p, cos_p = sincos(phase)
        pass_r = jnp.where(inside, cos_p, 0.0)
        pass_i = jnp.where(inside, sin_p, 0.0)
        pupil[s, :freqs] = pass_r
        pupil[s, freqs:] = pass_i
        lanes = slice(s * freqs, (s + 1) * freqs)
        for half, value in enumerate(
            (pass_r * spec_r - pass_i * spec_i, pass_i * spec_r + pass_r * spec_i)
        ):
            high, low = split(value)
            amp_h[half * freqs : (half + 1) * freqs, lanes] = high
            amp_l[half * freqs : (half + 1) * freqs, lanes] = low

    here, there = (slice(n, n + rows) for n in (first_row, pixels + first_row))
    waves = [jnp.concatenate([t[here], t[there]], axis=0) for t in (adj_h, adj_l)]
    for first in range(0, count, 2):
        members = range(first, min(first + 2, count))
        if first_row == 0:
            for s in members:
                amplitude(s)
        lanes = slice(first * freqs, (members[-1] + 1) * freqs)
        half = mm3(waves, (amp_h[:, lanes], amp_l[:, lanes]))
        for n, s in enumerate(members):
            for m in range(2):
                high, low = split(half[m * rows : (m + 1) * rows, n * freqs : (n + 1) * freqs])
                half_h[s * rows : (s + 1) * rows, m * freqs : (m + 1) * freqs] = high
                half_l[s * rows : (s + 1) * rows, m * freqs : (m + 1) * freqs] = low
    out = mm3((half_h[...], half_l[...]), (fwd_h[...], fwd_l[...]))
    total = jnp.zeros((rows, pixels), F32)
    for s in range(count):
        value = out[s * rows : (s + 1) * rows]
        field[s] = value
        out_r, out_i = value[:, :pixels], value[:, pixels:]
        weight = weight_of(meta, s, per_device) * (1.0 / sources)
        total = total + weight * (out_r * out_r + out_i * out_i)
    intensity[:rows] = total
    block = goal.shape[1]
    for n in range(rows // (2 * block)):
        place = rows + n * block
        intensity[place : place + block] = goal[first_row // (2 * block) + n]


def adjoint_kernel(per_device, sources, first_row, block, *refs):
    *before, field, pupil, light_a, light_b, meta = refs[:-8]
    fwd_h, fwd_l, adj_h, adj_l, grad, cot_ref, back_h, back_l = refs[-8:]
    rows, pixels = cot_ref.shape
    count, freqs = field.shape[0], grad.shape[1]
    row = lax.axis_index("row")
    for n in range(rows // block):
        here = slice(n * block, (n + 1) * block)
        place = slice(rows + n // 2 * block, rows + (n // 2 + 1) * block)
        goal = jnp.where(row == n % 2, light_a[place], light_b[place])
        intensity = light_a[here] + light_b[here]
        resist = 1.0 / (1.0 + jnp.exp(-STEEPNESS * (intensity - THRESHOLD)))
        cot_ref[here] = (LOSS_SCALE * STEEPNESS) * (resist - goal) * resist * (1.0 - resist)
    cot = cot_ref[...]
    line = lax.broadcasted_iota(jnp.int32, (PAD, freqs), 0)
    lane = lax.broadcasted_iota(jnp.int32, (PAD, freqs), 1)
    terms = jnp.zeros((PAD, freqs), F32)
    for s in range(count):
        value = field[s]
        back_r, back_i = cot * value[:, :pixels], cot * value[:, pixels:]
        power = back_r * value[:, :pixels] + back_i * value[:, pixels:]
        power = jnp.sum(jnp.sum(power, axis=0, keepdims=True), axis=1, keepdims=True)
        j, i = divmod(s, per_device)
        terms = terms + jnp.where((lane == i) & (line == j), power, 0.0)
        back = jnp.concatenate([back_r, back_i], axis=1)
        half = mm3(split(back), (adj_h[...], adj_l[...]))
        lanes = slice(s * freqs, (s + 1) * freqs)
        for n in range(2):
            high, low = split(half[:, n * freqs : (n + 1) * freqs])
            back_h[n * rows : (n + 1) * rows, lanes] = high
            back_l[n * rows : (n + 1) * rows, lanes] = low
    grad_r = jnp.zeros((freqs, freqs), F32)
    grad_i = jnp.zeros((freqs, freqs), F32)
    here, there = (slice(n, n + rows) for n in (first_row, pixels + first_row))
    waves = [jnp.concatenate([t[:, here], t[:, there]], axis=1) for t in (fwd_h, fwd_l)]
    for first in range(0, count, 2):
        members = range(first, min(first + 2, count))
        lanes = slice(first * freqs, (members[-1] + 1) * freqs)
        out = mm3(waves, (back_h[:, lanes], back_l[:, lanes]))
        for n, s in enumerate(members):
            lanes = slice(n * freqs, (n + 1) * freqs)
            weight = weight_of(meta, s, per_device) * (2.0 / (sources * pixels * freqs))
            pass_r, pass_i = weight * pupil[s, :freqs], weight * pupil[s, freqs:]
            out_r, out_i = out[:freqs, lanes], out[freqs:, lanes]
            grad_r = grad_r + (pass_r * out_r + pass_i * out_i)
            grad_i = grad_i + (pass_r * out_i - pass_i * out_r)
    for place, value in (
        (slice(0, freqs), grad_r),
        (slice(freqs, 2 * freqs), grad_i),
        (slice(2 * freqs, 2 * freqs + PAD), terms),
    ):
        grad[place] = value + before[0][place] if before else value


def window_kernel(half, grad_a, grad_b, fwd_h, fwd_l, adj_h, adj_l, own, *pays):
    pay_a, pay_b, pay_c, pay_d = pays
    rows, pixels = own.shape[0] - PAD, own.shape[1]
    freqs = grad_a.shape[1]
    src, row, tile = lax.axis_index("src"), lax.axis_index("row"), lax.axis_index("tile")
    total = grad_a[: 2 * freqs] + grad_b[: 2 * freqs]
    flat = split(jnp.concatenate([total[:freqs], total[freqs:]], axis=1))
    waves = mm3(flat, (fwd_h[...], fwd_l[...]))
    waves = jnp.concatenate([waves[:, :pixels], waves[:, pixels:]], axis=0)
    tables = []
    for table in (adj_h, adj_l):
        parts = []
        for steps, core in ((0, row), (1, 1 - row)):
            start = (block_of(src, 0, steps, half) * 2 + core) * rows
            parts.append(table[pl.ds(pl.multiple_of(start, rows), rows), :])
        tables.append(jnp.concatenate(parts, axis=0))
    window = mm3(tables, split(waves))
    terms = jnp.where(row == 0, grad_a[2 * freqs :], grad_b[2 * freqs :])
    near, far = window[:rows], window[rows:]

    def edge(block):
        return jnp.where(tile == 0, block[:, pixels - OV :], block[:, :OV])

    def put_rows(target, block, n):
        target[:rows] = block
        target[rows : rows + 1, :freqs] = terms[n : n + 1]

    def put_strip(target, block, n):
        block = edge(block)
        lines = range(0, rows, PAD)
        block = jnp.concatenate([block[i : i + PAD] for i in lines], axis=1)
        target[:PAD, : block.shape[1]] = block
        target[PAD : PAD + 1, :freqs] = terms[n : n + 1]

    put_rows(own, near, 0)
    put_rows(pay_b, far, 1)
    put_strip(pay_c, far, 1)

    @pl.when(src < half)
    def _():
        put_rows(pay_a, far, 1)
        put_strip(pay_d, near, 0)

    @pl.when(src >= half)
    def _():
        put_strip(pay_a, near, 0)
        put_strip(pay_d, far, 1)


def place_kernel(half, term_scale, own, got_a, got_b, got_c, got_d, out, source):
    rows, pixels = out.shape[1:]
    per_device = source.shape[1]
    src, tile = lax.axis_index("src"), lax.axis_index("tile")
    low, hub = src < half, (src == half - 1) | (src == half)

    def pick(low_hub, low_end, high_hub, high_end, *index):
        at_hub = jnp.where(low, low_hub[index], high_hub[index])
        at_end = jnp.where(low, low_end[index], high_end[index])
        return jnp.where(hub, at_hub, at_end)

    bodies, strips = (own, got_a, own, got_b), (got_d, got_c, got_a, got_d)
    body = pick(*bodies, slice(0, rows), slice(None))
    strip = pick(*strips, slice(0, PAD), slice(0, rows // PAD * OV))
    places = range(0, rows // PAD * OV, OV)
    strip = jnp.concatenate([strip[:, i : i + OV] for i in places], axis=0)
    zero = jnp.zeros_like(strip)
    middle = jnp.zeros((rows, pixels - 2 * OV), F32)
    left, right = jnp.where(tile == 1, strip, zero), jnp.where(tile == 0, strip, zero)
    out[0] = body + jnp.concatenate([left, middle, right], axis=1)
    own_terms = pick(*bodies, slice(rows, rows + 1), slice(0, per_device))
    other_terms = pick(*strips, slice(PAD, PAD + 1), slice(0, per_device))
    source[...] = (own_terms + other_terms) * term_scale


def call(kernel, outs, scratch=(), kind=F32, hbm=0, hub=False):
    def at_hub(*refs):
        src, half = lax.axis_index("src"), lax.axis_size("src") // 2
        pl.when((src == half - 1) | (src == half))(functools.partial(kernel, *refs))

    kinds = kind if isinstance(kind, list) else [kind] * len(outs)
    held = {"in_specs": [pl.BlockSpec(memory_space=pltpu.HBM)] * hbm} if hbm else {}
    return pl.pallas_call(
        at_hub if hub else kernel,
        out_shape=[jax.ShapeDtypeStruct(o, k) for o, k in zip(outs, kinds)],
        out_specs=[pl.BlockSpec(memory_space=pltpu.VMEM) for _ in outs],
        scratch_shapes=list(scratch),
        compiler_params=pltpu.CompilerParams(vmem_limit_bytes=VMEM_BUDGET),
        **held,
    )


def permute(x, wanted):
    shape = tuple(lax.axis_size(a) for a in ("src", "tile", "row"))
    devices = list(itertools.product(*(range(n) for n in shape)))
    pairs = dict(wanted)
    sources = [d for d in devices if d not in pairs]
    targets = [d for d in devices if d not in pairs.values()]

    def cost(pair):
        source, target = pair
        hops = abs(source[0] - target[0]) + abs(source[1] - target[1])
        return (source == target, hops, source, target)

    for source, target in sorted(itertools.product(sources, targets), key=cost):
        if source not in pairs and target not in pairs.values():
            pairs[source] = target
    flat = {d: n for n, d in enumerate(devices)}
    return lax.ppermute(x, ("src", "tile", "row"), [(flat[a], flat[b]) for a, b in pairs.items()])


def swap_rows(x):
    return lax.ppermute(x, "row", [(0, 1), (1, 0)])


def hub_shards(mask_windows, target_windows, pupil_bands, pupil_phase, source_weight):
    src_count, tile_count = lax.axis_size("src"), lax.axis_size("tile")
    rows, pixels = mask_windows.shape[1:]
    per_device, freqs = pupil_phase.shape[:2]
    sources = per_device * src_count
    half = src_count // 2
    count = half * per_device

    def chip(low, steps):
        return half - 1 - steps if low else half + steps

    cores = list(itertools.product(range(tile_count), range(2)))
    halves = (True, False)

    def to_hub(x, side, steps):
        return permute(
            x,
            {
                (chip(low, steps), t, c): (chip(low != (side == 1), 0), t, c)
                for low in halves
                for t, c in cores
            },
        )

    def phases_to_hub(x, steps):
        pairs = {}
        for low, tile in itertools.product(halves, range(tile_count)):
            if steps:
                pairs[chip(low, steps), tile, 0] = chip(low, 0), tile, 0
            pairs[chip(low, steps), tile, 1 if steps else 0] = chip(not low, 0), tile, 1
        return permute(x, pairs)

    pin = functools.partial(pltpu.with_memory_space_constraint, memory_space=pltpu.HBM)
    (message,) = call(
        fetch_kernel,
        [(2 * rows + PAD, pixels)],
        [
            pltpu.VMEM((per_device, 2, freqs), jnp.int32),
            pltpu.VMEM((1, per_device), F32),
            pltpu.SemaphoreType.DMA((4,)),
        ],
        hbm=4,
    )(
        pin(mask_windows),
        pin(target_windows),
        pin(pupil_bands.transpose(0, 2, 1)),
        pin(source_weight.reshape(1, per_device)),
    )
    order = (0, *range(1, half), half, *range(half + 1, 2 * half))
    blocks = [message] + [to_hub(message, d // half, d % half) for d in order[1:]]
    phases = [phases_to_hub(pupil_phase, n) for n in reversed(range(half))][::-1]
    *tables, phase = call(
        tables_kernel,
        [(2 * freqs, 2 * pixels)] * 2 + [(2 * pixels, 2 * freqs)] * 2 + [pupil_phase.shape],
        [pltpu.SemaphoreType.DMA],
        kind=[BF16] * 4 + [F32],
        hbm=1,
    )(pin(pupil_phase))

    spec, goal, meta = call(
        functools.partial(spectrum_kernel, half, order),
        [(2 * freqs, freqs), (src_count, rows, pixels), (half, PAD, pixels)],
        hub=True,
    )(*blocks, *tables)
    spec_other = swap_rows(spec)

    shape = (2 * freqs, count * freqs)
    part = pixels // 2
    outs = [(count, part, 2 * pixels), (part + part // 2, pixels)]
    *first, pupil, amp_h, amp_l = call(
        functools.partial(fields_kernel, per_device, sources, 0, half),
        [*outs, (count, 2 * freqs, freqs), shape, shape],
        [pltpu.VMEM((count * part, 2 * freqs), BF16)] * 2,
        kind=[F32, F32, F32, BF16, BF16],
        hub=True,
    )(phase, *phases, spec, spec_other, meta, goal, *tables)
    second = call(
        functools.partial(fields_kernel, per_device, sources, part, half),
        outs,
        [pltpu.VMEM((count * part, 2 * freqs), BF16)] * 2,
        hub=True,
    )(meta, goal, amp_h, amp_l, *tables)
    fields = [first, second]
    others = [swap_rows(light) for _, light in fields]
    grad = []
    for first_row, (field, light), other in zip((0, part), fields, others):
        grad = call(
            functools.partial(adjoint_kernel, per_device, sources, first_row, rows),
            [(2 * freqs + PAD, freqs)],
            [pltpu.VMEM((part, pixels), F32)]
            + [pltpu.VMEM((2 * part, count * freqs), BF16)] * 2,
            hub=True,
        )(*grad, field, pupil, light, other, meta, *tables)
    (grad,) = grad
    grad_other = swap_rows(grad)

    wide, narrow = (rows + PAD, pixels), (2 * PAD, max(freqs, rows // PAD * OV))
    own, pay_a, pay_b, pay_c, pay_d = call(
        functools.partial(window_kernel, half), [wide] * 3 + [narrow] * 2, hub=True
    )(grad, grad_other, *tables)
    low_end, low_hub, high_hub, high_end = chip(True, 1), chip(True, 0), chip(False, 0), chip(False, 1)

    def moves(*chips):
        return {
            (z, t, c): (to, t ^ tile_flip, c ^ core_flip)
            for z, to, tile_flip, core_flip in chips
            for t, c in cores
        }

    got_a = permute(
        pay_a,
        moves(
            (low_hub, low_end, 0, 1),
            (high_hub, high_hub, 1, 0),
            (low_end, high_end, 0, 0),
            (high_end, low_hub, 0, 0),
        ),
    )
    got_b = permute(pay_b, moves((high_hub, high_end, 0, 1), (high_end, high_hub, 0, 1)))
    got_c = permute(pay_c, moves((low_hub, low_end, 1, 1), (low_end, low_hub, 0, 1)))
    got_d = permute(
        pay_d,
        moves((low_hub, low_hub, 1, 0), (high_hub, high_end, 1, 1), (high_end, high_hub, 0, 1)),
    )
    out, source = call(
        functools.partial(place_kernel, half, 1.0 / (sources * pixels * tile_count)),
        [(1, rows, pixels), (1, per_device)],
    )(own, got_a, got_b, got_c, got_d)
    return out, source[0]


M = 256
K = 128


def with_halo(block, sides, width):
    for axis, dim in sides:
        count = lax.axis_size(axis)
        forward = [(i, i + 1) for i in range(count - 1)]
        backward = [(target, source) for source, target in forward]
        low = lax.ppermute(
            lax.slice_in_dim(block, block.shape[dim] - width, None, axis=dim), axis, forward
        )
        high = lax.ppermute(lax.slice_in_dim(block, 0, width, axis=dim), axis, backward)
        block = jnp.concatenate([low, block, high], axis=dim)
    return block


def matmul(left_op, right_op):
    return lax.dot_general(
        left_op,
        right_op,
        (((1,), (0,)), ((), ())),
        precision=lax.Precision.HIGHEST,
        preferred_element_type=jnp.float32,
    )


def matmul_tn(left_op, right_op):
    return lax.dot_general(
        left_op,
        right_op,
        (((0,), (0,)), ((), ())),
        precision=lax.Precision.HIGHEST,
        preferred_element_type=jnp.float32,
    )


def matmul_nt(left_op, right_op):
    return lax.dot_general(
        left_op,
        right_op,
        (((1,), (1,)), ((), ())),
        precision=lax.Precision.HIGHEST,
        preferred_element_type=jnp.float32,
    )


def wave_tables(positions):
    freq_index = jnp.arange(K, dtype=jnp.int32) - K // 2
    phase_index = freq_index[:, None] * positions[None, :] % M
    angles = 2.0 * math.pi / M * phase_index.astype(jnp.float32)
    return (jnp.cos(angles), jnp.sin(angles))


def shards(mask_windows, target_windows, pupil_bands, pupil_phase, source_weight):
    src_count = lax.axis_size("src")
    tile_count = lax.axis_size("tile")
    row_count = lax.axis_size("row")
    local_x = mask_windows.shape[1]
    per_device = pupil_phase.shape[0]
    sources = per_device * src_count
    field_scale = 1.0 / (M * K)
    src_id = lax.axis_index("src")
    row_id = lax.axis_index("row")
    x_start = (src_id * row_count + row_id) * local_x
    block_starts = (jnp.arange(src_count, dtype=jnp.int32) * row_count + row_id) * local_x
    row_set = (block_starts[:, None] + jnp.arange(local_x, dtype=jnp.int32)[None, :]).reshape(
        src_count * local_x
    )
    cos_all, sin_all = wave_tables(jnp.arange(M, dtype=jnp.int32))
    cos_set, sin_set = wave_tables(row_set)
    cos_own, sin_own = wave_tables(x_start + jnp.arange(local_x, dtype=jnp.int32))
    window = mask_windows[0]
    goal_block = target_windows[0]
    zero_spec = jnp.zeros((K, K), jnp.float32)
    shard_rows = lax.all_gather(window, ("src", "row"), axis=0, tiled=True)
    part_real = matmul_nt(shard_rows, cos_all)
    part_imag = -matmul_nt(shard_rows, sin_all)
    spec_real = matmul(cos_all, part_real) + matmul(sin_all, part_imag)
    spec_imag = matmul(cos_all, part_imag) - matmul(sin_all, part_real)
    freq_cols = jnp.arange(K, dtype=jnp.int32)
    inside = (freq_cols[None, None, :] >= pupil_bands[:, :, 0:1]) & (
        freq_cols[None, None, :] < pupil_bands[:, :, 1:2]
    )
    passing = inside.astype(jnp.float32)
    pupil_real = passing * jnp.cos(pupil_phase)
    pupil_imag = passing * jnp.sin(pupil_phase)
    amp_real = (pupil_real * spec_real - pupil_imag * spec_imag).reshape(per_device * K, K)
    amp_imag = (pupil_imag * spec_real + pupil_real * spec_imag).reshape(per_device * K, K)
    half_real = (matmul(amp_real, cos_all) - matmul(amp_imag, sin_all)).reshape(per_device, K, M)
    half_imag = (matmul(amp_real, sin_all) + matmul(amp_imag, cos_all)).reshape(per_device, K, M)
    weights = source_weight / sources

    def fields(pair_in):
        one_real, one_imag = pair_in
        field_real = field_scale * (matmul_tn(cos_set, one_real) - matmul_tn(sin_set, one_imag))
        field_imag = field_scale * (matmul_tn(cos_set, one_imag) + matmul_tn(sin_set, one_real))
        return (field_real, field_imag)

    stack_real, stack_imag = lax.map(fields, (half_real, half_imag))
    part_real = stack_real
    part_imag = stack_imag
    intensity = lax.psum_scatter(
        jnp.sum(weights[:, None, None] * (part_real * part_real + part_imag * part_imag), axis=0),
        "src",
        scatter_dimension=0,
        tiled=True,
    )
    resist = jax.nn.sigmoid(STEEPNESS * (intensity - THRESHOLD))
    cotangent = LOSS_SCALE * (resist - goal_block) * STEEPNESS * resist * (1.0 - resist)
    cotangent_all = lax.all_gather(cotangent, "src", axis=0, tiled=True)
    source_ids = jnp.arange(per_device, dtype=jnp.int32)

    def add_back(source_id, totals):
        grad_real, grad_imag, source_terms = totals
        field_real = stack_real[source_id]
        field_imag = stack_imag[source_id]
        back_scale = 2.0 * weights[source_id] * cotangent_all
        back_real = back_scale * field_real
        back_imag = back_scale * field_imag
        adj_real = matmul(cos_set, back_real) + matmul(sin_set, back_imag)
        adj_imag = matmul(cos_set, back_imag) - matmul(sin_set, back_real)
        amp_grad_real = field_scale * (matmul_nt(adj_real, cos_all) + matmul_nt(adj_imag, sin_all))
        amp_grad_imag = field_scale * (matmul_nt(adj_imag, cos_all) - matmul_nt(adj_real, sin_all))
        pass_real = pupil_real[source_id]
        pass_imag = pupil_imag[source_id]
        grad_real = grad_real + pass_real * amp_grad_real + pass_imag * amp_grad_imag
        grad_imag = grad_imag + pass_real * amp_grad_imag - pass_imag * amp_grad_real
        term_value = jnp.sum(cotangent_all * (field_real * field_real + field_imag * field_imag))
        source_terms = source_terms + jnp.where(source_ids == source_id, term_value, 0.0)
        return (grad_real, grad_imag, source_terms)

    grad_real, grad_imag, source_terms = lax.fori_loop(
        0, per_device, add_back, (zero_spec, zero_spec, jnp.zeros((per_device,), jnp.float32))
    )
    grad_real, grad_imag = lax.psum((grad_real, grad_imag), ("src", "row"))
    source_sum = lax.psum(source_terms, ("tile", "row"))
    source_grad = source_sum / (sources * M * tile_count)
    q_one = matmul(grad_real, cos_all) - matmul(grad_imag, sin_all)
    q_two = matmul(grad_real, sin_all) + matmul(grad_imag, cos_all)
    grad_block = matmul_tn(cos_own, q_one) - matmul_tn(sin_own, q_two)
    padded = with_halo(grad_block, (("tile", 1),), OV)
    from_below = padded[:, :OV]
    from_above = padded[:, M + OV :]
    middle = jnp.zeros((local_x, M - 2 * OV), jnp.float32)
    grad_block = grad_block + jnp.concatenate([from_below, middle, from_above], axis=1)
    return (grad_block[None], source_grad)


def hubs_serve(mesh, mask_windows, pupil_phase):
    src_count = mesh.shape["src"]
    pixels = mask_windows.shape[2]
    sources, freqs = pupil_phase.shape[0] // mesh.shape["parts"], pupil_phase.shape[1]
    per_device = sources // src_count
    held = sources // 2 * (2 * pixels * pixels + 4 * freqs * freqs) * 4
    return (
        mesh.shape["row"] == 2
        and mesh.shape["tile"] == 2
        and src_count % 2 == 0
        and src_count // 2 == 2
        and per_device < PAD
        and mask_windows.shape[1] // (2 * src_count) % 16 == 0
        and pixels & (pixels - 1) == 0
        and pixels >= 2 * freqs
        and held <= VMEM_BUDGET // 2
    )


def solution(mesh):
    def run(mask_windows, target_windows, pupil_bands, pupil_phase, source_weight):
        hubs = hubs_serve(mesh, mask_windows, pupil_phase)
        return jax.shard_map(
            hub_shards if hubs else shards,
            mesh=mesh,
            in_specs=(
                P(("parts", "tile"), ("src", "row"), None),
                P(("parts", "tile"), ("src", "row"), None),
                P(("parts", "src"), None, None),
                P(("parts", "src"), None, None),
                P(("parts", "src")),
            ),
            out_specs=(P(("parts", "tile"), ("src", "row"), None), P(("parts", "src"))),
            check_vma=False,
        )(mask_windows, target_windows, pupil_bands, pupil_phase, source_weight)

    return run
```
